32 devices in a mesh: dp: 4 (over y, x), ctx: 8 (over z, core).
Axes of the slice: x: 2, y: 2, z: 4, core: 2. Of those that a mesh axis runs over, the one named last changes fastest.
Arguments:
- tokens: bfloat16 [4, 32768, 768], P('dp', 'ctx'), may hold values from -6 to 6
- cotangent: bfloat16 [4, 32768, 768], P('dp', 'ctx'), may hold values from -6 to 6
- first_factor: bfloat16 [256, 256], replicated, may hold values from -0.375 to 0.375
- second_factor: bfloat16 [128, 128], replicated, may hold values from -0.5 to 0.5
- twiddle: float32 [256, 128], P('ctx'), may hold values from -4 to 4
- gate_gain: float32 [768], replicated, may hold values from 0.5 to 2
- gate_bias: float32 [768], replicated, may hold values from -1 to 1
- skip_gain: float32 [768], replicated, may hold values from -4 to 4
Outputs:
- grad_tokens: bfloat16 [4, 32768, 768], P('dp', 'ctx')
- grad_first: float32 [256, 256], replicated
- grad_second: float32 [128, 128], replicated
- grad_twiddle: float32 [256, 128], P('ctx')
- grad_gain: float32 [768], replicated
- grad_bias: float32 [768], replicated
- grad_skip: float32 [768], replicated
The draws below stay inside these ranges and needn't reach their ends.
All inputs are finite; a program needn't handle non-finite values.
Results may differ from the reference program's by a relative error of at most 0.0059.
Values may be sent and summed in bfloat16 or wider, within the bound.
No kernel may reach another device: no remote copies, remote signals or barrier semaphores. Data moves between devices by JAX's collectives and lax.ppermute only.
A program may use at most 192 MiB of HBM per device.

```python
import math
import jax
import jax.numpy as jnp
from jax import lax

D = 768
A = 256
B = 128
SEQS = 4
L = 32768


def shard_levels(own_key, extent, shards, smallest, largest):
    loudness = 1.0
    for axis_at, shards_of in shards:
        heights = jax.random.uniform(jax.random.fold_in(jax.random.fold_in(own_key, 6), axis_at), (shards_of,), jnp.float32, smallest / len(shards), largest / len(shards))
        loudness = loudness * jnp.repeat(jnp.exp(heights), extent[axis_at] // shards_of).reshape((-1,) + (1,) * (len(extent) - 1 - axis_at))
    return loudness


def bell_draw(rng, dims, scale, limit, pieces=(), dtype=jnp.bfloat16):
    factor_of = shard_levels(rng, dims, pieces, -0.22, 0.18) if pieces else 1.0
    array = jax.random.normal(rng, dims, jnp.float32) * scale * factor_of
    return jnp.minimum(jnp.maximum(array, -limit), limit).astype(dtype)


def setup_inputs(seed: int = 0) -> dict:
    arg_keys = jax.random.split(jax.random.key(seed), 9)
    return {
        "tokens": bell_draw(arg_keys[0], (SEQS, L, D), 1.0, 6.0, ((0, 4), (1, 8))),
        "cotangent": bell_draw(arg_keys[1], (SEQS, L, D), 1.0, 6.0, ((0, 4), (1, 8))),
        "first_factor": bell_draw(arg_keys[2], (A, A), A ** -0.5, 0.375),
        "second_factor": bell_draw(arg_keys[3], (B, B), B ** -0.5, 0.5),
        "twiddle": bell_draw(arg_keys[4], (A, B), 1.0, 4.0, ((0, 8),), jnp.float32),
        "gate_gain": jnp.clip(jnp.exp(jax.random.uniform(arg_keys[5], (D,), jnp.float32, math.log(0.5), math.log(2.0))), 0.5, 2.0),
        "gate_bias": jnp.clip(jax.random.uniform(arg_keys[6], (D,), jnp.float32, -1.0, 1.0), -1.0, 1.0),
        "skip_gain": bell_draw(arg_keys[7], (D,), 1.0, 4.0, (), jnp.float32),
    }


def mixdot(form, left, right):
    return jnp.einsum(form, left, right, precision=lax.Precision.HIGHEST)

def reference(tokens, cotangent, first_factor, second_factor, twiddle, gate_gain, gate_bias, skip_gain):
    first_wide = first_factor.astype(jnp.float32)
    second_wide = second_factor.astype(jnp.float32)

    def per_sequence(carry, pair):
        tok_seq, cot_seq = pair
        inputs = tok_seq.reshape(A, B, D).astype(jnp.float32)
        upstream = cot_seq.reshape(A, B, D).astype(jnp.float32)
        gate_vals = jax.nn.sigmoid(gate_gain * inputs + gate_bias)
        inner = mixdot('pb,abc->apc', second_wide, inputs)
        scaled = lax.optimization_barrier((inner * twiddle[:, :, None]).astype(jnp.bfloat16)).astype(jnp.float32)
        outer = mixdot('qa,apc->qpc', first_wide, scaled)
        outer_back = lax.optimization_barrier(outer.astype(jnp.bfloat16)).astype(jnp.float32)
        hidden = outer_back + skip_gain * inputs
        grad_hidden = upstream * gate_vals
        grad_outer = lax.optimization_barrier(grad_hidden.astype(jnp.bfloat16)).astype(jnp.float32)
        grad_pre = upstream * hidden * gate_vals * (1.0 - gate_vals)
        first_term = mixdot('qpc,apc->qa', grad_outer, scaled)
        grad_scaled = lax.optimization_barrier(mixdot('qa,qpc->apc', first_wide, grad_outer).astype(jnp.bfloat16)).astype(jnp.float32)
        twiddle_term = lax.optimization_barrier(jnp.sum(grad_scaled * inner, axis=2))
        grad_inner = lax.optimization_barrier((grad_scaled * twiddle[:, :, None]).astype(jnp.bfloat16)).astype(jnp.float32)
        second_term = mixdot('apc,abc->pb', grad_inner, inputs)
        grad_in = mixdot('pb,apc->abc', second_wide, grad_inner) + grad_hidden * skip_gain + grad_pre * gate_gain
        gain_term = lax.optimization_barrier(jnp.sum(grad_pre * inputs, axis=(0, 1)))
        bias_term = lax.optimization_barrier(jnp.sum(grad_pre, axis=(0, 1)))
        skip_term = lax.optimization_barrier(jnp.sum(grad_hidden * inputs, axis=(0, 1)))
        updated = (carry[0] + first_term, carry[1] + second_term, carry[2] + twiddle_term, carry[3] + gain_term, carry[4] + bias_term, carry[5] + skip_term)
        return (updated, grad_in.astype(jnp.bfloat16).reshape(A * B, D))
    start = (jnp.zeros((A, A), jnp.float32), jnp.zeros((B, B), jnp.float32), jnp.zeros((A, B), jnp.float32), jnp.zeros((D,), jnp.float32), jnp.zeros((D,), jnp.float32), jnp.zeros((D,), jnp.float32))
    totals, grad_tokens = lax.scan(per_sequence, start, (tokens, cotangent))
    first_norm = math.sqrt(SEQS * B * D)
    second_norm = math.sqrt(SEQS * A * D)
    twiddle_norm = math.sqrt(SEQS * D)
    channel_norm = math.sqrt(SEQS * A * B)
    return (grad_tokens, totals[0] / first_norm, totals[1] / second_norm, totals[2] / twiddle_norm, totals[3] / channel_norm, totals[4] / channel_norm, totals[5] / channel_norm)
```

```python
import functools
import math

import jax
import jax.numpy as jnp
from jax import lax
from jax.experimental import pallas as pl
from jax.experimental.pallas import tpu as pltpu
from jax.sharding import PartitionSpec as P

A = 256
B = 128
LANES = 128
VMEM_BYTES = 48 * 1024 * 1024


def dot(left, right, left_dim, right_dim):
    return lax.dot_general(
        left, right, (((left_dim,), (right_dim,)), ((), ())), preferred_element_type=jnp.float32
    )


def split_kernel(tok_ref, cot_ref, out_ref, swap_ref):
    rows = tok_ref.shape[0]
    share = out_ref.shape[2]
    for which, ref in enumerate((tok_ref, cot_ref)):
        for row in range(rows):
            swap_ref[row * LANES : (row + 1) * LANES, :] = ref[row].astype(jnp.float32).T
        for channel in range(LANES):
            out_ref[channel // share, which, channel % share] = swap_ref[
                pl.ds(channel, rows, stride=LANES), :
            ].astype(jnp.bfloat16)


def split_channels(tokens, cotangent, tile, ctx_size):
    rows = tokens.shape[0]
    step = min(16, rows)
    share = LANES // ctx_size
    block = pl.BlockSpec((step, B, LANES), lambda i: (i, 0, tile))
    return pl.pallas_call(
        split_kernel,
        grid=(rows // step,),
        in_specs=[block, block],
        out_specs=pl.BlockSpec((ctx_size, 2, share, step, B), lambda i: (0, 0, 0, i, 0)),
        out_shape=jax.ShapeDtypeStruct((ctx_size, 2, share, rows, B), jnp.bfloat16),
        scratch_shapes=[pltpu.VMEM((step * LANES, B), jnp.float32)],
        compiler_params=pltpu.CompilerParams(vmem_limit_bytes=VMEM_BYTES),
        cost_estimate=pl.CostEstimate(
            flops=0, bytes_accessed=8 * rows * B * LANES * 4, transcendentals=0
        ),
    )(tokens, cotangent)


def merge_kernel(part_ref, *rest):
    out_ref, swap_ref = rest[-2:]
    devices, share, rows, _ = part_ref.shape
    for device in range(devices):
        for channel in range(share):
            at = (device * share + channel) * rows
            swap_ref[at : at + rows, :] = part_ref[device, channel].astype(jnp.float32)
    for row in range(rows):
        out_ref[row] = swap_ref[pl.ds(row, LANES, stride=rows), :].T.astype(jnp.bfloat16)


def merge_channels(parts, held, tile, width):
    devices, share, rows, _ = parts.shape
    step = min(16, rows)
    given = [parts] if held is None else [parts, held]
    specs = [pl.BlockSpec((devices, share, step, B), lambda i: (0, 0, i, 0))]
    if held is not None:
        specs.append(pl.BlockSpec(memory_space=pl.ANY))
    return pl.pallas_call(
        merge_kernel,
        grid=(rows // step,),
        in_specs=specs,
        out_specs=pl.BlockSpec((step, B, LANES), lambda i: (i, 0, tile)),
        out_shape=jax.ShapeDtypeStruct((rows, B, width), jnp.bfloat16),
        scratch_shapes=[pltpu.VMEM((step * LANES, B), jnp.float32)],
        input_output_aliases={} if held is None else {1: 0},
        compiler_params=pltpu.CompilerParams(vmem_limit_bytes=VMEM_BYTES),
        cost_estimate=pl.CostEstimate(
            flops=0, bytes_accessed=4 * rows * B * LANES * 4, transcendentals=0
        ),
    )(*given)


def mix_kernel(
    base_ref, gain_ref, bias_ref, skip_ref, part_ref, first_ref, first_t_ref, second_ref,
    second_t_ref, twiddle_ref, first_in, second_in, twiddle_in,
    out_ref, first_out, second_out, twiddle_out, sums_out,
):
    step = pl.program_id(0)

    @pl.when(step == 0)
    def _():
        first_out[...] = first_in[...]
        second_out[...] = second_in[...]
        twiddle_out[...] = twiddle_in[...]

    devices, _, pair, rows, _ = part_ref.shape
    at = base_ref[0] + step * pair

    def together(which):
        return jnp.concatenate(
            [part_ref[:, which, c].reshape(A, B) for c in range(pair)], axis=1
        )

    def spread(ref):
        lane = lax.broadcasted_iota(jnp.int32, (1, pair * B), 1)
        row = jnp.full((1, pair * B), ref[at], jnp.float32)
        for c in range(1, pair):
            row = jnp.where(lane >= c * B, ref[at + c], row)
        return row

    gain, bias, skip = spread(gain_ref), spread(bias_ref), spread(skip_ref)
    tok = together(0)
    inputs = tok.astype(jnp.float32)
    upstream = together(1).astype(jnp.float32)
    twiddle = jnp.concatenate([twiddle_ref[...]] * pair, axis=1)
    inner = dot(tok, second_t_ref[...], 1, 0)
    scaled = (inner * twiddle).astype(jnp.bfloat16)
    gate = jax.nn.sigmoid(gain * inputs + bias)
    grad_hidden = upstream * gate
    grad_outer = grad_hidden.astype(jnp.bfloat16)
    outer = dot(first_ref[...], scaled, 1, 0).astype(jnp.bfloat16).astype(jnp.float32)
    grad_scaled = dot(first_t_ref[...], grad_outer, 1, 0).astype(jnp.bfloat16).astype(jnp.float32)
    first_out[...] += dot(grad_outer, scaled, 1, 1)
    hidden = outer + skip * inputs
    grad_pre = upstream * hidden * gate * (1.0 - gate)
    product = grad_scaled * inner
    twiddle_out[...] += sum(product[:, c * B : (c + 1) * B] for c in range(pair))
    grad_inner = (grad_scaled * twiddle).astype(jnp.bfloat16)
    second_out[...] += dot(grad_inner, tok, 0, 0)
    grad_in = dot(grad_inner, second_ref[...], 1, 0)
    grad_in = (grad_in + grad_hidden * skip + grad_pre * gain).astype(jnp.bfloat16)
    for c in range(pair):
        out_ref[:, c] = grad_in[:, c * B : (c + 1) * B].reshape(devices, rows, B)
    rows_of = (grad_pre * inputs, grad_pre, grad_hidden * inputs)
    for which, value in enumerate(rows_of):
        total = jnp.sum(value, axis=0, keepdims=True)
        for c in range(pair):
            sums_out[c, which : which + 1] = total[:, c * B : (c + 1) * B]


def mix(parts, base, gain, bias, skip, first, first_t, second, second_t, twiddle, totals):
    devices, _, share, rows, _ = parts.shape
    pair = second.shape[0] // B
    whole = lambda shape: pl.BlockSpec(shape, lambda i: (0,) * len(shape))
    smem = pl.BlockSpec(memory_space=pltpu.SMEM)
    total_specs = [whole(t.shape) for t in totals]
    return pl.pallas_call(
        mix_kernel,
        grid=(share // pair,),
        in_specs=[smem] * 4
        + [pl.BlockSpec((devices, 2, pair, rows, B), lambda i: (0, 0, i, 0, 0))]
        + [whole(t.shape) for t in (first, first_t, second, second_t, twiddle)]
        + total_specs,
        out_specs=[pl.BlockSpec((devices, pair, rows, B), lambda i: (0, i, 0, 0))]
        + total_specs
        + [pl.BlockSpec((pair, 8, B), lambda i: (i, 0, 0))],
        out_shape=[jax.ShapeDtypeStruct((devices, share, rows, B), jnp.bfloat16)]
        + [jax.ShapeDtypeStruct(t.shape, t.dtype) for t in totals]
        + [jax.ShapeDtypeStruct((share, 8, B), jnp.float32)],
        compiler_params=pltpu.CompilerParams(vmem_limit_bytes=VMEM_BYTES),
        cost_estimate=pl.CostEstimate(
            flops=share * A * B * 2 * 2304,
            bytes_accessed=share * A * B * 6,
            transcendentals=share * A * B * 2,
        ),
    )(base, gain, bias, skip, parts, first, first_t, second, second_t, twiddle, *totals)


def block_diagonal(square, count):
    zero = jnp.zeros_like(square)
    return jnp.concatenate(
        [
            jnp.concatenate([square if i == j else zero for j in range(count)], axis=1)
            for i in range(count)
        ],
        axis=0,
    )


def body(tokens, cotangent, first_factor, second_factor, twiddle, gate_gain, gate_bias, skip_gain):
    seq_count, tok_rows, width = tokens.shape
    ctx_size = lax.axis_size("ctx")
    me = lax.axis_index("ctx")
    share = LANES // ctx_size
    local_rows = tok_rows // B
    pair = 2
    tiles = width // LANES

    first_t = first_factor.T
    second = block_diagonal(second_factor, pair)
    second_t = block_diagonal(second_factor.T, pair)
    twiddle_all = lax.all_gather(twiddle, "ctx", axis=0, tiled=True)
    totals = [
        jnp.zeros((A, A), jnp.float32),
        jnp.zeros((pair * B, pair * B), jnp.float32),
        jnp.zeros((A, B), jnp.float32),
    ]
    grads = []
    channel_sums = [[] for _ in range(tiles)]
    for seq in range(seq_count):
        tok_blocks = tokens[seq].reshape(local_rows, B, width)
        cot_blocks = cotangent[seq].reshape(local_rows, B, width)
        arrived = []
        for tile in range(tiles):
            parts = split_channels(tok_blocks, cot_blocks, tile, ctx_size)
            arrived.append(
                lax.all_to_all(parts, "ctx", split_axis=0, concat_axis=0, tiled=True)
            )
        held = None
        for tile in range(tiles):
            base = (tile * LANES + me * share).astype(jnp.int32).reshape(1)
            grad_parts, *totals, sums = mix(
                arrived[tile], base, gate_gain, gate_bias, skip_gain, first_factor, first_t,
                second, second_t, twiddle_all, totals,
            )
            channel_sums[tile].append(jnp.sum(sums, axis=2))
            back = lax.all_to_all(grad_parts, "ctx", split_axis=0, concat_axis=0, tiled=True)
            held = merge_channels(back, held, tile, width)
        grads.append(held.reshape(tok_rows, width))
    grad_tokens = jnp.stack(grads)

    first_term, second_wide, twiddle_term = totals
    second_term = sum(
        second_wide[c * B : (c + 1) * B, c * B : (c + 1) * B] for c in range(pair)
    )
    own = jnp.stack([sum(s)[:, :3] for s in channel_sums])
    spread = jnp.zeros((tiles, ctx_size, share, 3), jnp.float32)
    spread = lax.dynamic_update_slice(spread, own[:, None], (0, me, 0, 0))
    channel_terms = spread.reshape(width, 3).T
    first_sum, second_sum, channel_sum = lax.psum(
        (first_term, second_term, channel_terms), ("dp", "ctx")
    )
    twiddle_sum = lax.psum(
        lax.psum_scatter(twiddle_term, "ctx", scatter_dimension=0, tiled=True), "dp"
    )
    total_seqs = seq_count * lax.axis_size("dp")
    first_norm = math.sqrt(total_seqs * B * width)
    second_norm = math.sqrt(total_seqs * A * width)
    twiddle_norm = math.sqrt(total_seqs * width)
    channel_norm = math.sqrt(total_seqs * A * B)
    return (
        grad_tokens,
        first_sum / first_norm,
        second_sum / second_norm,
        twiddle_sum / twiddle_norm,
        channel_sum[0] / channel_norm,
        channel_sum[1] / channel_norm,
        channel_sum[2] / channel_norm,
    )


def solution(mesh):
    return jax.shard_map(
        body,
        mesh=mesh,
        in_specs=(
            P("dp", "ctx", None),
            P("dp", "ctx", None),
            P(),
            P(),
            P("ctx", None),
            P(),
            P(),
            P(),
        ),
        out_specs=(P("dp", "ctx", None), P(), P(), P("ctx", None), P(), P(), P()),
        check_vma=False,
    )
```

```python
import functools
import math

import jax
import jax.numpy as jnp
from jax import lax
from jax.experimental import pallas as pl
from jax.experimental.pallas import tpu as pltpu
from jax.sharding import PartitionSpec as P

A = 256
B = 128
LANES = 128
VMEM_BYTES = 48 * 1024 * 1024


def dot(left, right, left_dim, right_dim):
    return lax.dot_general(
        left, right, (((left_dim,), (right_dim,)), ((), ())), preferred_element_type=jnp.float32
    )


def split_tile(tok_ref, cot_ref, out_ref, swap_ref, first_at, second_at):
    rows = tok_ref.shape[0]
    share = LANES // out_ref.shape[0]
    for at, ref in ((first_at, tok_ref), (second_at, cot_ref)):
        for row in range(rows):
            swap_ref[row * LANES : (row + 1) * LANES, :] = ref[row].astype(jnp.float32).T
        for channel in range(LANES):
            out_ref[channel // share, at + channel % share] = swap_ref[
                pl.ds(channel, rows, stride=LANES), :
            ].astype(jnp.bfloat16)


def split_kernel(tok_ref, cot_ref, out_ref, swap_ref):
    share = LANES // out_ref.shape[0]
    split_tile(tok_ref, cot_ref, out_ref, swap_ref, 0, share)


def split_twiddle_kernel(tok_ref, cot_ref, twiddle_ref, out_ref, swap_ref):
    share = LANES // out_ref.shape[0]
    split_tile(tok_ref, cot_ref, out_ref, swap_ref, 0, share)
    left = twiddle_ref[...]
    for plane in range(3):
        part = left.astype(jnp.bfloat16)
        left = left - part.astype(jnp.float32)
        for device in range(out_ref.shape[0]):
            out_ref[device, 2 * share + plane] = part


def split_channels(tokens, cotangent, tile, tiles, ctx_size, twiddle=None):
    rows = tokens.shape[0]
    step = min(16, rows)
    share = LANES // ctx_size
    block = pl.BlockSpec((step, B, LANES), lambda t, i: (i, 0, tile + t))
    if twiddle is None:
        kernel, given, specs = split_kernel, [tokens, cotangent], [block, block]
        planes = 2 * share
    else:
        kernel, given = split_twiddle_kernel, [tokens, cotangent, twiddle]
        specs = [block, block, pl.BlockSpec((step, B), lambda t, i: (i, 0))]
        planes = 2 * share + 3
    return pl.pallas_call(
        kernel,
        grid=(tiles, rows // step),
        in_specs=specs,
        out_specs=pl.BlockSpec((ctx_size, planes, step, B), lambda t, i: (0, t, i, 0)),
        out_shape=jax.ShapeDtypeStruct((ctx_size, tiles * planes, rows, B), jnp.bfloat16),
        scratch_shapes=[pltpu.VMEM((step * LANES, B), jnp.float32)],
        compiler_params=pltpu.CompilerParams(vmem_limit_bytes=VMEM_BYTES),
        cost_estimate=pl.CostEstimate(
            flops=0, bytes_accessed=8 * rows * B * LANES * tiles, transcendentals=0
        ),
    )(*given)


def merge_kernel(part_ref, *rest):
    out_ref, swap_ref = rest[-2:]
    devices, share, rows, _ = part_ref.shape
    for device in range(devices):
        for channel in range(share):
            at = (device * share + channel) * rows
            swap_ref[at : at + rows, :] = part_ref[device, channel].astype(jnp.float32)
    for row in range(rows):
        out_ref[row] = swap_ref[pl.ds(row, LANES, stride=rows), :].T.astype(jnp.bfloat16)


def merge_channels(parts, held, tile, width):
    devices, channels, rows, _ = parts.shape
    step = min(16, rows)
    share = LANES // devices
    tiles = channels // share
    given = [parts] if held is None else [parts, held]
    specs = [pl.BlockSpec((devices, share, step, B), lambda t, i: (0, t, i, 0))]
    if held is not None:
        specs.append(pl.BlockSpec(memory_space=pl.ANY))
    return pl.pallas_call(
        merge_kernel,
        grid=(tiles, rows // step),
        in_specs=specs,
        out_specs=pl.BlockSpec((step, B, LANES), lambda t, i: (i, 0, tile + t)),
        out_shape=jax.ShapeDtypeStruct((rows, B, width), jnp.bfloat16),
        scratch_shapes=[pltpu.VMEM((step * LANES, B), jnp.float32)],
        input_output_aliases={} if held is None else {1: 0},
        compiler_params=pltpu.CompilerParams(vmem_limit_bytes=VMEM_BYTES),
        cost_estimate=pl.CostEstimate(
            flops=0, bytes_accessed=4 * rows * B * LANES * tiles, transcendentals=0
        ),
    )(*given)


SECOND_AT = 2 * A
TWIDDLE_AT = SECOND_AT + B
CHANNEL_AT = TWIDDLE_AT + A


def mix_kernel(
    place_ref, gain_ref, bias_ref, skip_ref, tok_ref, cot_ref, first_ref, first_t_ref, second_ref,
    second_t_ref, twiddle_ref, *rest, tile, tile_count, has_sums,
):
    out_ref, sums_ref = rest[-2:]
    t, step = pl.program_id(0), pl.program_id(1)

    @pl.when((t == 0) & (step == 0))
    def _():
        sums_ref[...] = rest[0][...] if has_sums else jnp.zeros(sums_ref.shape, jnp.float32)

    devices, pair, rows, _ = tok_ref.shape
    lane_at = place_ref[0] + step * pair
    at = (tile + t) * LANES + lane_at

    def together(ref):
        return jnp.concatenate([ref[:, c].reshape(A, B) for c in range(pair)], axis=1)

    def spread(ref):
        lane = lax.broadcasted_iota(jnp.int32, (1, pair * B), 1)
        row = jnp.full((1, pair * B), ref[at], jnp.float32)
        for c in range(1, pair):
            row = jnp.where(lane >= c * B, ref[at + c], row)
        return row

    gain, bias, skip = spread(gain_ref), spread(bias_ref), spread(skip_ref)
    tok = together(tok_ref)
    inputs = tok.astype(jnp.float32)
    upstream = together(cot_ref).astype(jnp.float32)
    twiddle = jnp.concatenate([twiddle_ref[...]] * pair, axis=1)
    inner = dot(tok, second_t_ref[...], 1, 0)
    scaled = (inner * twiddle).astype(jnp.bfloat16)
    gate = jax.nn.sigmoid(gain * inputs + bias)
    grad_hidden = upstream * gate
    grad_outer = grad_hidden.astype(jnp.bfloat16)
    outer = dot(first_ref[...], scaled, 1, 0).astype(jnp.bfloat16).astype(jnp.float32)
    grad_scaled = dot(first_t_ref[...], grad_outer, 1, 0).astype(jnp.bfloat16).astype(jnp.float32)
    first_term = dot(grad_outer, scaled, 1, 1)
    for half in range(A // B):
        sums_ref[half * A : (half + 1) * A] += first_term[:, half * B : (half + 1) * B]
    hidden = outer + skip * inputs
    grad_pre = upstream * hidden * gate * (1.0 - gate)
    product = grad_scaled * inner
    sums_ref[TWIDDLE_AT:CHANNEL_AT] += sum(product[:, c * B : (c + 1) * B] for c in range(pair))
    grad_inner = (grad_scaled * twiddle).astype(jnp.bfloat16)
    second_term = dot(grad_inner, tok, 0, 0)
    sums_ref[SECOND_AT:TWIDDLE_AT] += sum(
        second_term[c * B : (c + 1) * B, c * B : (c + 1) * B] for c in range(pair)
    )
    grad_in = dot(grad_inner, second_ref[...], 1, 0)
    grad_in = (grad_in + grad_hidden * skip + grad_pre * gain).astype(jnp.bfloat16)
    for c in range(pair):
        out_ref[:, c] = grad_in[:, c * B : (c + 1) * B].reshape(devices, rows, B)
    lane = lax.broadcasted_iota(jnp.int32, (1, LANES), 1)
    for which, value in enumerate((grad_pre * inputs, grad_pre, grad_hidden * inputs)):
        total = jnp.sum(value, axis=0, keepdims=True)
        row = jnp.zeros((1, LANES), jnp.float32)
        for c in range(pair):
            channel = jnp.sum(total[:, c * B : (c + 1) * B], axis=1, keepdims=True)
            row = jnp.where(lane == lane_at + c, channel, row)
        sums_ref[pl.ds(CHANNEL_AT + which * tile_count + tile + t, 1), :] += row


def mix(parts, tile, tiles, planes, place, vectors, factors, sums, sum_rows, out_tiles, out_at, held):
    devices, _, rows, _ = parts.shape
    share = LANES // devices
    pair = factors[2].shape[0] // B
    steps = share // pair
    whole = lambda array: pl.BlockSpec(array.shape, lambda t, i: (0,) * array.ndim)
    tok_at = lambda t, i: (0, t * (planes // pair) + i, 0, 0)
    cot_at = lambda t, i: (0, t * (planes // pair) + steps + i, 0, 0)
    block = (devices, pair, rows, B)
    given = [place, *vectors, parts, parts, *factors]
    specs = [pl.BlockSpec(memory_space=pltpu.SMEM)] * 4
    specs += [pl.BlockSpec(block, tok_at), pl.BlockSpec(block, cot_at)]
    specs += [whole(f) for f in factors]
    aliases = {}
    if sums is not None:
        given.append(sums)
        specs.append(whole(sums))
    if held is not None:
        aliases[len(given)] = 0
        given.append(held)
        specs.append(pl.BlockSpec(memory_space=pl.ANY))
    tile_count = vectors[0].shape[0] // LANES
    return pl.pallas_call(
        functools.partial(
            mix_kernel, tile=tile, tile_count=tile_count, has_sums=sums is not None
        ),
        grid=(tiles, steps),
        in_specs=specs,
        out_specs=[
            pl.BlockSpec(block, lambda t, i: (0, (out_at + t) * steps + i, 0, 0)),
            pl.BlockSpec((sum_rows, LANES), lambda t, i: (0, 0)),
        ],
        out_shape=[
            jax.ShapeDtypeStruct((devices, out_tiles * share, rows, B), jnp.bfloat16),
            jax.ShapeDtypeStruct((sum_rows, LANES), jnp.float32),
        ],
        input_output_aliases=aliases,
        compiler_params=pltpu.CompilerParams(vmem_limit_bytes=VMEM_BYTES),
        cost_estimate=pl.CostEstimate(
            flops=tiles * share * A * B * 2 * 2304,
            bytes_accessed=tiles * share * A * B * 6,
            transcendentals=tiles * share * A * B * 2,
        ),
    )(*given)


def block_diagonal(square, count):
    zero = jnp.zeros_like(square)
    return jnp.concatenate(
        [
            jnp.concatenate([square if i == j else zero for j in range(count)], axis=1)
            for i in range(count)
        ],
        axis=0,
    )


def body(tokens, cotangent, first_factor, second_factor, twiddle, gate_gain, gate_bias, skip_gain):
    seq_count, tok_rows, width = tokens.shape
    ctx_size = lax.axis_size("ctx")
    dp_size = lax.axis_size("dp")
    share = LANES // ctx_size
    local_rows = tok_rows // B
    tiles = width // LANES
    pair = 2
    sent = [1, tiles - 2, 1]
    returned = [tiles - 1, 1]

    place = (lax.axis_index("ctx") * share).astype(jnp.int32).reshape(1)
    second = block_diagonal(second_factor, pair)
    second_t = block_diagonal(second_factor.T, pair)
    vectors = [gate_gain, gate_bias, skip_gain]
    used_rows = CHANNEL_AT + 3 * tiles
    sum_rows = -(-used_rows // (8 * dp_size)) * 8 * dp_size

    def exchange(parts):
        return lax.all_to_all(parts, "ctx", split_axis=0, concat_axis=0, tiled=True)

    sums = None
    factors = None
    grads = []
    for seq in range(seq_count):
        tok_blocks = tokens[seq].reshape(local_rows, B, width)
        cot_blocks = cotangent[seq].reshape(local_rows, B, width)
        arrived = []
        at = 0
        for count in sent:
            own = twiddle if at == 0 else None
            parts = exchange(split_channels(tok_blocks, cot_blocks, at, count, ctx_size, own))
            arrived.append((at, count, parts))
            at += count
        planes = arrived[0][2][:, 2 * share :].astype(jnp.float32)
        twiddle_all = (planes[:, 0] + planes[:, 1] + planes[:, 2]).reshape(A, B)
        factors = [first_factor, first_factor.T, second, second_t, twiddle_all]
        leaving = [None] * len(returned)
        for at, count, parts in arrived:
            back = 0 if at < returned[0] else 1
            out_at = at - back * returned[0]
            leaving[back], sums = mix(
                parts, at, count, 2 * share, place, vectors, factors, sums, sum_rows,
                returned[back], out_at, leaving[back],
            )
        held = None
        at = 0
        for count, grad_parts in zip(returned, leaving):
            held = merge_channels(exchange(grad_parts), held, at, width)
            at += count
        grads.append(held.reshape(tok_rows, width))
    grad_tokens = jnp.stack(grads)

    sums = lax.psum_scatter(sums, "dp", scatter_dimension=0, tiled=True)
    sums = lax.psum(sums, "ctx")
    sums = lax.all_gather(sums, "dp", axis=0, tiled=True)
    total_seqs = seq_count * dp_size
    first_norm = math.sqrt(total_seqs * B * width)
    second_norm = math.sqrt(total_seqs * A * width)
    twiddle_norm = math.sqrt(total_seqs * width)
    channel_norm = math.sqrt(total_seqs * A * B)
    first_sum = jnp.concatenate([sums[half * A : (half + 1) * A] for half in range(A // B)], axis=1)
    mine = TWIDDLE_AT + lax.axis_index("ctx") * local_rows
    twiddle_sum = lax.dynamic_slice_in_dim(sums, mine, local_rows, 0)
    channel_sum = sums[CHANNEL_AT:used_rows].reshape(3, width)
    return (
        grad_tokens,
        first_sum / first_norm,
        sums[SECOND_AT:TWIDDLE_AT] / second_norm,
        twiddle_sum / twiddle_norm,
        channel_sum[0] / channel_norm,
        channel_sum[1] / channel_norm,
        channel_sum[2] / channel_norm,
    )


def solution(mesh):
    return jax.shard_map(
        body,
        mesh=mesh,
        in_specs=(
            P("dp", "ctx", None),
            P("dp", "ctx", None),
            P(),
            P(),
            P("ctx", None),
            P(),
            P(),
            P(),
        ),
        out_specs=(P("dp", "ctx", None), P(), P(), P("ctx", None), P(), P(), P()),
        check_vma=False,
    )
```

```python
import functools
import math

import jax
import jax.numpy as jnp
from jax import lax
from jax.experimental import pallas as pl
from jax.experimental.pallas import tpu as pltpu
from jax.sharding import PartitionSpec as P

A = 256
B = 128
LANES = 128
VMEM_BYTES = 48 * 1024 * 1024


def dot(left, right, left_dim, right_dim):
    return lax.dot_general(
        left, right, (((left_dim,), (right_dim,)), ((), ())), preferred_element_type=jnp.float32
    )


def split_tile(tok_ref, cot_ref, out_ref, swap_ref, first_at, second_at):
    rows = tok_ref.shape[0]
    share = LANES // out_ref.shape[0]
    for at, ref in ((first_at, tok_ref), (second_at, cot_ref)):
        for row in range(rows):
            swap_ref[row * LANES : (row + 1) * LANES, :] = ref[row].astype(jnp.float32).T
        for channel in range(LANES):
            out_ref[channel // share, at + channel % share] = swap_ref[
                pl.ds(channel, rows, stride=LANES), :
            ].astype(jnp.bfloat16)


def split_kernel(tok_ref, cot_ref, out_ref, swap_ref):
    share = LANES // out_ref.shape[0]
    split_tile(tok_ref, cot_ref, out_ref, swap_ref, 0, share)


def split_twiddle_kernel(tok_ref, cot_ref, twiddle_ref, out_ref, swap_ref):
    share = LANES // out_ref.shape[0]
    split_tile(tok_ref, cot_ref, out_ref, swap_ref, 0, share)
    left = twiddle_ref[...]
    for plane in range(3):
        part = left.astype(jnp.bfloat16)
        left = left - part.astype(jnp.float32)
        for device in range(out_ref.shape[0]):
            out_ref[device, 2 * share + plane] = part


def split_channels(tokens, cotangent, tile, tiles, ctx_size, twiddle=None):
    rows = tokens.shape[0]
    step = min(16, rows)
    share = LANES // ctx_size
    block = pl.BlockSpec((step, B, LANES), lambda t, i: (i, 0, tile + t))
    if twiddle is None:
        kernel, given, specs = split_kernel, [tokens, cotangent], [block, block]
        planes = 2 * share
    else:
        kernel, given = split_twiddle_kernel, [tokens, cotangent, twiddle]
        specs = [block, block, pl.BlockSpec((step, B), lambda t, i: (i, 0))]
        planes = 2 * share + 3
    return pl.pallas_call(
        kernel,
        grid=(tiles, rows // step),
        in_specs=specs,
        out_specs=pl.BlockSpec((ctx_size, planes, step, B), lambda t, i: (0, t, i, 0)),
        out_shape=jax.ShapeDtypeStruct((ctx_size, tiles * planes, rows, B), jnp.bfloat16),
        scratch_shapes=[pltpu.VMEM((step * LANES, B), jnp.float32)],
        compiler_params=pltpu.CompilerParams(vmem_limit_bytes=VMEM_BYTES),
        cost_estimate=pl.CostEstimate(
            flops=0, bytes_accessed=8 * rows * B * LANES * tiles, transcendentals=0
        ),
    )(*given)


def merge_kernel(part_ref, *rest):
    out_ref, swap_ref = rest[-2:]
    devices, share, rows, _ = part_ref.shape
    for device in range(devices):
        for channel in range(share):
            at = (device * share + channel) * rows
            swap_ref[at : at + rows, :] = part_ref[device, channel].astype(jnp.float32)
    for row in range(rows):
        out_ref[row] = swap_ref[pl.ds(row, LANES, stride=rows), :].T.astype(jnp.bfloat16)


def merge_channels(parts, held, tile, width):
    devices, channels, rows, _ = parts.shape
    step = min(16, rows)
    share = LANES // devices
    tiles = channels // share
    given = [parts] if held is None else [parts, held]
    specs = [pl.BlockSpec((devices, share, step, B), lambda t, i: (0, t, i, 0))]
    if held is not None:
        specs.append(pl.BlockSpec(memory_space=pl.ANY))
    return pl.pallas_call(
        merge_kernel,
        grid=(tiles, rows // step),
        in_specs=specs,
        out_specs=pl.BlockSpec((step, B, LANES), lambda t, i: (i, 0, tile + t)),
        out_shape=jax.ShapeDtypeStruct((rows, B, width), jnp.bfloat16),
        scratch_shapes=[pltpu.VMEM((step * LANES, B), jnp.float32)],
        input_output_aliases={} if held is None else {1: 0},
        compiler_params=pltpu.CompilerParams(vmem_limit_bytes=VMEM_BYTES),
        cost_estimate=pl.CostEstimate(
            flops=0, bytes_accessed=4 * rows * B * LANES * tiles, transcendentals=0
        ),
    )(*given)


SECOND_AT = 2 * A
TWIDDLE_AT = SECOND_AT + B
CHANNEL_AT = TWIDDLE_AT + A


def mix_kernel(
    place_ref, gain_ref, bias_ref, skip_ref, tok_ref, cot_ref, first_ref, first_t_ref, second_ref,
    second_t_ref, twiddle_ref, *rest, tile, tile_count, has_sums,
):
    out_ref, sums_ref = rest[-2:]
    t, step = pl.program_id(0), pl.program_id(1)

    @pl.when((t == 0) & (step == 0))
    def _():
        sums_ref[...] = rest[0][...] if has_sums else jnp.zeros(sums_ref.shape, jnp.float32)

    devices, pair, rows, _ = tok_ref.shape
    lane_at = place_ref[0] + step * pair
    at = (tile + t) * LANES + lane_at

    def together(ref):
        return jnp.concatenate([ref[:, c].reshape(A, B) for c in range(pair)], axis=1)

    def spread(ref):
        lane = lax.broadcasted_iota(jnp.int32, (1, pair * B), 1)
        row = jnp.full((1, pair * B), ref[at], jnp.float32)
        for c in range(1, pair):
            row = jnp.where(lane >= c * B, ref[at + c], row)
        return row

    gain, bias, skip = spread(gain_ref), spread(bias_ref), spread(skip_ref)
    tok = together(tok_ref)
    inputs = tok.astype(jnp.float32)
    upstream = together(cot_ref).astype(jnp.float32)
    twiddle = jnp.concatenate([twiddle_ref[...]] * pair, axis=1)
    inner = dot(tok, second_t_ref[...], 1, 0)
    scaled = (inner * twiddle).astype(jnp.bfloat16)
    gate = jax.nn.sigmoid(gain * inputs + bias)
    grad_hidden = upstream * gate
    grad_outer = grad_hidden.astype(jnp.bfloat16)
    outer = dot(first_ref[...], scaled, 1, 0).astype(jnp.bfloat16).astype(jnp.float32)
    grad_scaled = dot(first_t_ref[...], grad_outer, 1, 0).astype(jnp.bfloat16).astype(jnp.float32)
    first_term = dot(grad_outer, scaled, 1, 1)
    for half in range(A // B):
        sums_ref[half * A : (half + 1) * A] += first_term[:, half * B : (half + 1) * B]
    hidden = outer + skip * inputs
    grad_pre = upstream * hidden * gate * (1.0 - gate)
    product = grad_scaled * inner
    sums_ref[TWIDDLE_AT:CHANNEL_AT] += sum(product[:, c * B : (c + 1) * B] for c in range(pair))
    grad_inner = (grad_scaled * twiddle).astype(jnp.bfloat16)
    second_term = dot(grad_inner, tok, 0, 0)
    sums_ref[SECOND_AT:TWIDDLE_AT] += sum(
        second_term[c * B : (c + 1) * B, c * B : (c + 1) * B] for c in range(pair)
    )
    grad_in = dot(grad_inner, second_ref[...], 1, 0)
    grad_in = (grad_in + grad_hidden * skip + grad_pre * gain).astype(jnp.bfloat16)
    for c in range(pair):
        out_ref[:, c] = grad_in[:, c * B : (c + 1) * B].reshape(devices, rows, B)
    lane = lax.broadcasted_iota(jnp.int32, (1, LANES), 1)
    for which, value in enumerate((grad_pre * inputs, grad_pre, grad_hidden * inputs)):
        total = jnp.sum(value, axis=0, keepdims=True)
        row = jnp.zeros((1, LANES), jnp.float32)
        for c in range(pair):
            channel = jnp.sum(total[:, c * B : (c + 1) * B], axis=1, keepdims=True)
            row = jnp.where(lane == lane_at + c, channel, row)
        sums_ref[pl.ds(CHANNEL_AT + which * tile_count + tile + t, 1), :] += row


def mix(parts, tile, tiles, planes, place, vectors, factors, sums, sum_rows, out_tiles, out_at, held):
    devices, _, rows, _ = parts.shape
    share = LANES // devices
    pair = factors[2].shape[0] // B
    steps = share // pair
    whole = lambda array: pl.BlockSpec(array.shape, lambda t, i: (0,) * array.ndim)
    tok_at = lambda t, i: (0, t * (planes // pair) + i, 0, 0)
    cot_at = lambda t, i: (0, t * (planes // pair) + steps + i, 0, 0)
    block = (devices, pair, rows, B)
    given = [place, *vectors, parts, parts, *factors]
    specs = [pl.BlockSpec(memory_space=pltpu.SMEM)] * 4
    specs += [pl.BlockSpec(block, tok_at), pl.BlockSpec(block, cot_at)]
    specs += [whole(f) for f in factors]
    aliases = {}
    if sums is not None:
        given.append(sums)
        specs.append(whole(sums))
    if held is not None:
        aliases[len(given)] = 0
        given.append(held)
        specs.append(pl.BlockSpec(memory_space=pl.ANY))
    tile_count = vectors[0].shape[0] // LANES
    return pl.pallas_call(
        functools.partial(
            mix_kernel, tile=tile, tile_count=tile_count, has_sums=sums is not None
        ),
        grid=(tiles, steps),
        in_specs=specs,
        out_specs=[
            pl.BlockSpec(block, lambda t, i: (0, (out_at + t) * steps + i, 0, 0)),
            pl.BlockSpec((sum_rows, LANES), lambda t, i: (0, 0)),
        ],
        out_shape=[
            jax.ShapeDtypeStruct((devices, out_tiles * share, rows, B), jnp.bfloat16),
            jax.ShapeDtypeStruct((sum_rows, LANES), jnp.float32),
        ],
        input_output_aliases=aliases,
        compiler_params=pltpu.CompilerParams(vmem_limit_bytes=VMEM_BYTES),
        cost_estimate=pl.CostEstimate(
            flops=tiles * share * A * B * 2 * 2304,
            bytes_accessed=tiles * share * A * B * 6,
            transcendentals=tiles * share * A * B * 2,
        ),
    )(*given)


def block_diagonal(square, count):
    zero = jnp.zeros_like(square)
    return jnp.concatenate(
        [
            jnp.concatenate([square if i == j else zero for j in range(count)], axis=1)
            for i in range(count)
        ],
        axis=0,
    )


def body(tokens, cotangent, first_factor, second_factor, twiddle, gate_gain, gate_bias, skip_gain):
    seq_count, tok_rows, width = tokens.shape
    ctx_size = lax.axis_size("ctx")
    dp_size = lax.axis_size("dp")
    share = LANES // ctx_size
    local_rows = tok_rows // B
    tiles = width // LANES
    pair = 2
    sent = [1, tiles - 2, 1]
    returned = [tiles - 1, 1]

    place = (lax.axis_index("ctx") * share).astype(jnp.int32).reshape(1)
    second = block_diagonal(second_factor, pair)
    second_t = block_diagonal(second_factor.T, pair)
    vectors = [gate_gain, gate_bias, skip_gain]
    used_rows = CHANNEL_AT + 3 * tiles
    sum_rows = -(-used_rows // (8 * dp_size)) * 8 * dp_size

    def exchange(parts):
        return lax.all_to_all(parts, "ctx", split_axis=0, concat_axis=0, tiled=True)

    sums = None
    factors = None
    grads = []
    for seq in range(seq_count):
        tok_blocks = tokens[seq].reshape(local_rows, B, width)
        cot_blocks = cotangent[seq].reshape(local_rows, B, width)
        arrived = []
        at = 0
        for count in sent:
            own = twiddle if at == 0 else None
            parts = exchange(split_channels(tok_blocks, cot_blocks, at, count, ctx_size, own))
            arrived.append((at, count, parts))
            at += count
        planes = arrived[0][2][:, 2 * share :].astype(jnp.float32)
        twiddle_all = (planes[:, 0] + planes[:, 1] + planes[:, 2]).reshape(A, B)
        factors = [first_factor, first_factor.T, second, second_t, twiddle_all]
        leaving = [None] * len(returned)
        for at, count, parts in arrived:
            back = 0 if at < returned[0] else 1
            out_at = at - back * returned[0]
            leaving[back], sums = mix(
                parts, at, count, 2 * share, place, vectors, factors, sums, sum_rows,
                returned[back], out_at, leaving[back],
            )
        held = None
        at = 0
        for count, grad_parts in zip(returned, leaving):
            held = merge_channels(exchange(grad_parts), held, at, width)
            at += count
        grads.append(held.reshape(tok_rows, width))
    grad_tokens = jnp.stack(grads)

    own_rows = sum_rows // dp_size
    sums = lax.dynamic_slice_in_dim(
        lax.all_gather(sums, "dp"), lax.axis_index("dp") * own_rows, own_rows, 1
    )
    sums = jnp.sum(lax.all_gather(jnp.sum(sums, axis=0), "ctx"), axis=0)
    sums = lax.all_gather(sums, "dp", axis=0, tiled=True)
    total_seqs = seq_count * dp_size
    first_norm = math.sqrt(total_seqs * B * width)
    second_norm = math.sqrt(total_seqs * A * width)
    twiddle_norm = math.sqrt(total_seqs * width)
    channel_norm = math.sqrt(total_seqs * A * B)
    first_sum = jnp.concatenate([sums[half * A : (half + 1) * A] for half in range(A // B)], axis=1)
    mine = TWIDDLE_AT + lax.axis_index("ctx") * local_rows
    twiddle_sum = lax.dynamic_slice_in_dim(sums, mine, local_rows, 0)
    channel_sum = sums[CHANNEL_AT:used_rows].reshape(3, width)
    return (
        grad_tokens,
        first_sum / first_norm,
        sums[SECOND_AT:TWIDDLE_AT] / second_norm,
        twiddle_sum / twiddle_norm,
        channel_sum[0] / channel_norm,
        channel_sum[1] / channel_norm,
        channel_sum[2] / channel_norm,
    )


def solution(mesh):
    return jax.shard_map(
        body,
        mesh=mesh,
        in_specs=(
            P("dp", "ctx", None),
            P("dp", "ctx", None),
            P(),
            P(),
            P("ctx", None),
            P(),
            P(),
            P(),
        ),
        out_specs=(P("dp", "ctx", None), P(), P(), P("ctx", None), P(), P(), P()),
        check_vma=False,
    )
```

```python
import functools
import math

import jax
import jax.numpy as jnp
from jax import lax
from jax.experimental import pallas as pl
from jax.experimental.pallas import tpu as pltpu
from jax.sharding import PartitionSpec as P

A = 256
B = 128
LANES = 128
VMEM_BYTES = 48 * 1024 * 1024


def dot(left, right, left_dim, right_dim):
    return lax.dot_general(
        left, right, (((left_dim,), (right_dim,)), ((), ())), preferred_element_type=jnp.float32
    )


def split_tile(first_channel, tok_ref, cot_ref, out_refs, swap_ref):
    rows = tok_ref.shape[0]
    share = LANES // len(out_refs)
    for which, ref in enumerate((tok_ref, cot_ref)):
        for row in range(rows):
            swap_ref[row * LANES : (row + 1) * LANES, :] = ref[row].astype(jnp.float32).T
        for shift, out_ref in enumerate(out_refs):
            start = (first_channel + shift * share) % LANES
            for channel in range(share):
                out_ref[which * share + channel] = swap_ref[
                    pl.ds(start + channel, rows, stride=LANES), :
                ].astype(jnp.bfloat16)


def split_kernel(place_ref, tok_ref, cot_ref, *rest):
    split_tile(place_ref[0], tok_ref, cot_ref, rest[:-1], rest[-1])


def split_twiddle_kernel(place_ref, tok_ref, cot_ref, twiddle_ref, *rest):
    out_refs = rest[:-1]
    split_tile(place_ref[0], tok_ref, cot_ref, out_refs, rest[-1])
    share = LANES // len(out_refs)
    left = twiddle_ref[...]
    for plane in range(3):
        part = left.astype(jnp.bfloat16)
        left = left - part.astype(jnp.float32)
        for out_ref in out_refs:
            out_ref[2 * share + plane] = part


def split_channels(place, tokens, cotangent, tile, tiles, ctx_size, twiddle=None):
    rows = tokens.shape[0]
    step = min(16, rows)
    share = LANES // ctx_size
    block = pl.BlockSpec((step, B, LANES), lambda t, i: (i, 0, tile + t))
    specs = [pl.BlockSpec(memory_space=pltpu.SMEM), block, block]
    if twiddle is None:
        kernel, given = split_kernel, [place, tokens, cotangent]
        planes = 2 * share
    else:
        kernel, given = split_twiddle_kernel, [place, tokens, cotangent, twiddle]
        specs.append(pl.BlockSpec((step, B), lambda t, i: (i, 0)))
        planes = 2 * share + 3
    return pl.pallas_call(
        kernel,
        grid=(tiles, rows // step),
        in_specs=specs,
        out_specs=[pl.BlockSpec((planes, step, B), lambda t, i: (t, i, 0))] * ctx_size,
        out_shape=[jax.ShapeDtypeStruct((tiles * planes, rows, B), jnp.bfloat16)] * ctx_size,
        scratch_shapes=[pltpu.VMEM((step * LANES, B), jnp.float32)],
        compiler_params=pltpu.CompilerParams(vmem_limit_bytes=VMEM_BYTES),
        cost_estimate=pl.CostEstimate(
            flops=0, bytes_accessed=8 * rows * B * LANES * tiles, transcendentals=0
        ),
    )(*given)


def merge_kernel(devices, place_ref, *rest):
    part_refs, out_ref, swap_ref = rest[:devices], rest[-2], rest[-1]
    share, rows, _ = part_refs[0].shape
    for shift, part_ref in enumerate(part_refs):
        start = (place_ref[0] + shift * share) % LANES
        for channel in range(share):
            at = pl.multiple_of((start + channel) * rows, rows)
            swap_ref[pl.ds(at, rows), :] = part_ref[channel].astype(jnp.float32)
    for row in range(rows):
        out_ref[row] = swap_ref[pl.ds(row, LANES, stride=rows), :].T.astype(jnp.bfloat16)


def merge_channels(place, parts, held, tile, width):
    devices = len(parts)
    channels, rows, _ = parts[0].shape
    step = min(16, rows)
    share = LANES // devices
    tiles = channels // share
    given = [place, *parts]
    specs = [pl.BlockSpec(memory_space=pltpu.SMEM)]
    specs += [pl.BlockSpec((share, step, B), lambda t, i: (t, i, 0))] * devices
    if held is not None:
        given.append(held)
        specs.append(pl.BlockSpec(memory_space=pl.ANY))
    return pl.pallas_call(
        functools.partial(merge_kernel, devices),
        grid=(tiles, rows // step),
        in_specs=specs,
        out_specs=pl.BlockSpec((step, B, LANES), lambda t, i: (i, 0, tile + t)),
        out_shape=jax.ShapeDtypeStruct((rows, B, width), jnp.bfloat16),
        scratch_shapes=[pltpu.VMEM((step * LANES, B), jnp.float32)],
        input_output_aliases={} if held is None else {devices + 1: 0},
        compiler_params=pltpu.CompilerParams(vmem_limit_bytes=VMEM_BYTES),
        cost_estimate=pl.CostEstimate(
            flops=0, bytes_accessed=4 * rows * B * LANES * tiles, transcendentals=0
        ),
    )(*given)


SECOND_AT = 2 * A
TWIDDLE_AT = SECOND_AT + B
CHANNEL_AT = TWIDDLE_AT + A


def mix_kernel(
    place_ref, gain_ref, bias_ref, skip_ref, *rest, devices, tile, tile_count, has_sums
):
    tok_refs, cot_refs, rest = rest[:devices], rest[devices : 2 * devices], rest[2 * devices :]
    first_ref, first_t_ref, second_ref, second_t_ref, twiddle_ref, *rest = rest
    out_refs, (sums_ref, tok_all, cot_all) = rest[-3 - devices : -3], rest[-3:]
    t, step = pl.program_id(0), pl.program_id(1)

    @pl.when((t == 0) & (step == 0))
    def _():
        sums_ref[...] = rest[0][...] if has_sums else jnp.zeros(sums_ref.shape, jnp.float32)

    pair, rows, _ = tok_refs[0].shape
    share = LANES // devices
    lane_at = place_ref[0] + step * pair
    at = (tile + t) * LANES + lane_at

    def rows_from(shift):
        source = (place_ref[0] // share - shift + devices) % devices
        return pl.ds(pl.multiple_of(source * rows, rows), rows)

    for refs, whole in ((tok_refs, tok_all), (cot_refs, cot_all)):
        for shift, ref in enumerate(refs):
            for c in range(pair):
                whole[rows_from(shift), c * B : (c + 1) * B] = ref[c].astype(jnp.float32)

    def spread(ref):
        lane = lax.broadcasted_iota(jnp.int32, (1, pair * B), 1)
        row = jnp.full((1, pair * B), ref[at], jnp.float32)
        for c in range(1, pair):
            row = jnp.where(lane >= c * B, ref[at + c], row)
        return row

    gain, bias, skip = spread(gain_ref), spread(bias_ref), spread(skip_ref)
    inputs = tok_all[...]
    tok = inputs.astype(jnp.bfloat16)
    upstream = cot_all[...]
    twiddle = jnp.concatenate([twiddle_ref[...]] * pair, axis=1)
    inner = dot(tok, second_t_ref[...], 1, 0)
    scaled = (inner * twiddle).astype(jnp.bfloat16)
    gate = jax.nn.sigmoid(gain * inputs + bias)
    grad_hidden = upstream * gate
    grad_outer = grad_hidden.astype(jnp.bfloat16)
    outer = dot(first_ref[...], scaled, 1, 0).astype(jnp.bfloat16).astype(jnp.float32)
    grad_scaled = dot(first_t_ref[...], grad_outer, 1, 0).astype(jnp.bfloat16).astype(jnp.float32)
    first_term = dot(grad_outer, scaled, 1, 1)
    for half in range(A // B):
        sums_ref[half * A : (half + 1) * A] += first_term[:, half * B : (half + 1) * B]
    hidden = outer + skip * inputs
    grad_pre = upstream * hidden * gate * (1.0 - gate)
    product = grad_scaled * inner
    sums_ref[TWIDDLE_AT:CHANNEL_AT] += sum(product[:, c * B : (c + 1) * B] for c in range(pair))
    grad_inner = (grad_scaled * twiddle).astype(jnp.bfloat16)
    second_term = dot(grad_inner, tok, 0, 0)
    sums_ref[SECOND_AT:TWIDDLE_AT] += sum(
        second_term[c * B : (c + 1) * B, c * B : (c + 1) * B] for c in range(pair)
    )
    lane = lax.broadcasted_iota(jnp.int32, (1, LANES), 1)
    for which, value in enumerate((grad_pre * inputs, grad_pre, grad_hidden * inputs)):
        total = jnp.sum(value, axis=0, keepdims=True)
        row = jnp.zeros((1, LANES), jnp.float32)
        for c in range(pair):
            channel = jnp.sum(total[:, c * B : (c + 1) * B], axis=1, keepdims=True)
            row = jnp.where(lane == lane_at + c, channel, row)
        sums_ref[pl.ds(CHANNEL_AT + which * tile_count + tile + t, 1), :] += row
    grad_in = dot(grad_inner, second_ref[...], 1, 0)
    tok_all[...] = grad_in + grad_hidden * skip + grad_pre * gain
    for shift, out_ref in enumerate(out_refs):
        for c in range(pair):
            out_ref[c] = tok_all[rows_from(shift), c * B : (c + 1) * B].astype(jnp.bfloat16)


def mix(parts, tile, tiles, planes, place, vectors, factors, sums, sum_rows, out_tiles, out_at, held):
    devices = len(parts)
    rows = parts[0].shape[1]
    share = LANES // devices
    pair = factors[2].shape[0] // B
    steps = share // pair
    whole = lambda array: pl.BlockSpec(array.shape, lambda t, i: (0,) * array.ndim)
    tok_at = lambda t, i: (t * (planes // pair) + i, 0, 0)
    cot_at = lambda t, i: (t * (planes // pair) + steps + i, 0, 0)
    block = (pair, rows, B)
    given = [place, *vectors, *parts, *parts, *factors]
    specs = [pl.BlockSpec(memory_space=pltpu.SMEM)] * 4
    specs += [pl.BlockSpec(block, tok_at)] * devices + [pl.BlockSpec(block, cot_at)] * devices
    specs += [whole(f) for f in factors]
    aliases = {}
    if sums is not None:
        given.append(sums)
        specs.append(whole(sums))
    if held is not None:
        for shift, array in enumerate(held):
            aliases[len(given)] = shift
            given.append(array)
            specs.append(pl.BlockSpec(memory_space=pl.ANY))
    tile_count = vectors[0].shape[0] // LANES
    *leaving, sums = pl.pallas_call(
        functools.partial(
            mix_kernel, devices=devices, tile=tile, tile_count=tile_count,
            has_sums=sums is not None,
        ),
        grid=(tiles, steps),
        in_specs=specs,
        out_specs=[pl.BlockSpec(block, lambda t, i: ((out_at + t) * steps + i, 0, 0))] * devices
        + [pl.BlockSpec((sum_rows, LANES), lambda t, i: (0, 0))],
        out_shape=[jax.ShapeDtypeStruct((out_tiles * share, rows, B), jnp.bfloat16)] * devices
        + [jax.ShapeDtypeStruct((sum_rows, LANES), jnp.float32)],
        scratch_shapes=[pltpu.VMEM((A, pair * B), jnp.float32)] * 2,
        input_output_aliases=aliases,
        compiler_params=pltpu.CompilerParams(vmem_limit_bytes=VMEM_BYTES),
        cost_estimate=pl.CostEstimate(
            flops=tiles * share * A * B * 2 * 2304,
            bytes_accessed=tiles * share * A * B * 6,
            transcendentals=tiles * share * A * B * 2,
        ),
    )(*given)
    return leaving, sums


def block_diagonal(square, count):
    zero = jnp.zeros_like(square)
    return jnp.concatenate(
        [
            jnp.concatenate([square if i == j else zero for j in range(count)], axis=1)
            for i in range(count)
        ],
        axis=0,
    )


def body(tokens, cotangent, first_factor, second_factor, twiddle, gate_gain, gate_bias, skip_gain):
    seq_count, tok_rows, width = tokens.shape
    ctx_size = lax.axis_size("ctx")
    dp_size = lax.axis_size("dp")
    share = LANES // ctx_size
    local_rows = tok_rows // B
    tiles = width // LANES
    pair = 2
    sent = [1, tiles - 2, 1]
    returned = [tiles - 1, 1]

    place = (lax.axis_index("ctx") * share).astype(jnp.int32).reshape(1)
    second = block_diagonal(second_factor, pair)
    second_t = block_diagonal(second_factor.T, pair)
    vectors = [gate_gain, gate_bias, skip_gain]
    used_rows = CHANNEL_AT + 3 * tiles
    sum_rows = -(-used_rows // (8 * dp_size)) * 8 * dp_size

    def exchange(parts, sign):
        moved = [parts[0]]
        for shift in range(1, ctx_size):
            pairs = [(i, (i + sign * shift) % ctx_size) for i in range(ctx_size)]
            moved.append(lax.ppermute(parts[shift], "ctx", pairs))
        return moved

    sums = None
    factors = None
    grads = []
    for seq in range(seq_count):
        tok_blocks = tokens[seq].reshape(local_rows, B, width)
        cot_blocks = cotangent[seq].reshape(local_rows, B, width)
        arrived = []
        at = 0
        for count in sent:
            own = twiddle if at == 0 else None
            parts = split_channels(place, tok_blocks, cot_blocks, at, count, ctx_size, own)
            arrived.append((at, count, exchange(parts, 1)))
            at += count
        planes = jnp.stack([part[2 * share :] for part in arrived[0][2]]).astype(jnp.float32)
        planes = (planes[:, 0] + planes[:, 1] + planes[:, 2]).reshape(A, B)
        planes = planes.reshape(ctx_size, local_rows, B)[::-1]
        planes = jnp.concatenate([planes, planes], axis=0)
        turn = ctx_size - 1 - lax.axis_index("ctx")
        twiddle_all = lax.dynamic_slice_in_dim(planes, turn, ctx_size, 0).reshape(A, B)
        factors = [first_factor, first_factor.T, second, second_t, twiddle_all]
        leaving = [None] * len(returned)
        for at, count, parts in arrived:
            back = 0 if at < returned[0] else 1
            out_at = at - back * returned[0]
            leaving[back], sums = mix(
                parts, at, count, 2 * share, place, vectors, factors, sums, sum_rows,
                returned[back], out_at, leaving[back],
            )
        held = None
        at = 0
        for count, grad_parts in zip(returned, leaving):
            held = merge_channels(place, exchange(grad_parts, -1), held, at, width)
            at += count
        grads.append(held.reshape(tok_rows, width))
    grad_tokens = jnp.stack(grads)

    own_rows = sum_rows // dp_size
    bit = 1
    while bit < dp_size:
        sums = sums + lax.ppermute(sums, "dp", [(i, i ^ bit) for i in range(dp_size)])
        bit *= 2
    sums = lax.dynamic_slice_in_dim(sums, lax.axis_index("dp") * own_rows, own_rows, 0)
    sums = jnp.sum(lax.all_gather(sums, "ctx"), axis=0)
    sums = lax.all_gather(sums, "dp", axis=0, tiled=True)
    total_seqs = seq_count * dp_size
    first_norm = math.sqrt(total_seqs * B * width)
    second_norm = math.sqrt(total_seqs * A * width)
    twiddle_norm = math.sqrt(total_seqs * width)
    channel_norm = math.sqrt(total_seqs * A * B)
    first_sum = jnp.concatenate([sums[half * A : (half + 1) * A] for half in range(A // B)], axis=1)
    mine = TWIDDLE_AT + lax.axis_index("ctx") * local_rows
    twiddle_sum = lax.dynamic_slice_in_dim(sums, mine, local_rows, 0)
    channel_sum = sums[CHANNEL_AT:used_rows].reshape(3, width)
    return (
        grad_tokens,
        first_sum / first_norm,
        sums[SECOND_AT:TWIDDLE_AT] / second_norm,
        twiddle_sum / twiddle_norm,
        channel_sum[0] / channel_norm,
        channel_sum[1] / channel_norm,
        channel_sum[2] / channel_norm,
    )


def solution(mesh):
    return jax.shard_map(
        body,
        mesh=mesh,
        in_specs=(
            P("dp", "ctx", None),
            P("dp", "ctx", None),
            P(),
            P(),
            P("ctx", None),
            P(),
            P(),
            P(),
        ),
        out_specs=(P("dp", "ctx", None), P(), P(), P("ctx", None), P(), P(), P()),
        check_vma=False,
    )
```

```python
import functools
import math

import jax
import jax.numpy as jnp
from jax import lax
from jax.experimental import pallas as pl
from jax.experimental.pallas import tpu as pltpu
from jax.sharding import PartitionSpec as P

A = 256
B = 128
LANES = 128
VMEM_BYTES = 48 * 1024 * 1024


def dot(left, right, left_dim, right_dim):
    return lax.dot_general(
        left, right, (((left_dim,), (right_dim,)), ((), ())), preferred_element_type=jnp.float32
    )


def views(refs, rotated):
    return list(refs) if rotated else [refs[0].at[i] for i in range(refs[0].shape[0])]


def split_tile(first_channel, tok_ref, cot_ref, out_refs, swap_ref):
    rows = tok_ref.shape[0]
    share = LANES // len(out_refs)
    for which, ref in enumerate((tok_ref, cot_ref)):
        for row in range(rows):
            swap_ref[row * LANES : (row + 1) * LANES, :] = ref[row].astype(jnp.float32).T
        for slot, out_ref in enumerate(out_refs):
            start = (first_channel + slot * share) % LANES
            for channel in range(share):
                out_ref[which * share + channel] = swap_ref[
                    pl.ds(start + channel, rows, stride=LANES), :
                ].astype(jnp.bfloat16)


def split_kernel(place_ref, tok_ref, cot_ref, *rest, rotated):
    first_channel = place_ref[0] if rotated else 0
    split_tile(first_channel, tok_ref, cot_ref, views(rest[:-1], rotated), rest[-1])


def split_twiddle_kernel(place_ref, tok_ref, cot_ref, twiddle_ref, *rest, rotated):
    split_kernel(place_ref, tok_ref, cot_ref, *rest, rotated=rotated)
    out_refs = views(rest[:-1], rotated)
    share = LANES // len(out_refs)
    left = twiddle_ref[...]
    for plane in range(3):
        part = left.astype(jnp.bfloat16)
        left = left - part.astype(jnp.float32)
        for out_ref in out_refs:
            out_ref[2 * share + plane] = part


def part_specs(devices, rotated, block, index):
    if rotated:
        return [pl.BlockSpec(block, index)] * devices
    return [pl.BlockSpec((devices, *block), lambda *at: (0, *index(*at)))]


def part_shapes(devices, rotated, shape):
    if rotated:
        return [jax.ShapeDtypeStruct(shape, jnp.bfloat16)] * devices
    return [jax.ShapeDtypeStruct((devices, *shape), jnp.bfloat16)]


def split_channels(place, tokens, cotangent, tile, tiles, devices, rotated, twiddle=None):
    rows = tokens.shape[0]
    step = min(16, rows)
    share = LANES // devices
    block = pl.BlockSpec((step, B, LANES), lambda t, i: (i, 0, tile + t))
    specs = [pl.BlockSpec(memory_space=pltpu.SMEM), block, block]
    if twiddle is None:
        kernel, given = split_kernel, [place, tokens, cotangent]
        planes = 2 * share
    else:
        kernel, given = split_twiddle_kernel, [place, tokens, cotangent, twiddle]
        specs.append(pl.BlockSpec((step, B), lambda t, i: (i, 0)))
        planes = 2 * share + 3
    return pl.pallas_call(
        functools.partial(kernel, rotated=rotated),
        grid=(tiles, rows // step),
        in_specs=specs,
        out_specs=part_specs(devices, rotated, (planes, step, B), lambda t, i: (t, i, 0)),
        out_shape=part_shapes(devices, rotated, (tiles * planes, rows, B)),
        scratch_shapes=[pltpu.VMEM((step * LANES, B), jnp.float32)],
        compiler_params=pltpu.CompilerParams(vmem_limit_bytes=VMEM_BYTES),
        cost_estimate=pl.CostEstimate(
            flops=0, bytes_accessed=8 * rows * B * LANES * tiles, transcendentals=0
        ),
    )(*given)


def merge_kernel(place_ref, *rest, parts, rotated):
    part_refs, out_ref, swap_ref = views(rest[:parts], rotated), rest[-2], rest[-1]
    share, rows, _ = part_refs[0].shape
    for slot, part_ref in enumerate(part_refs):
        start = (place_ref[0] + slot * share) % LANES if rotated else slot * share
        for channel in range(share):
            at = pl.multiple_of((start + channel) * rows, rows)
            swap_ref[pl.ds(at, rows), :] = part_ref[channel].astype(jnp.float32)
    for row in range(rows):
        out_ref[row] = swap_ref[pl.ds(row, LANES, stride=rows), :].T.astype(jnp.bfloat16)


def merge_channels(place, parts, held, tile, tiles, devices, rotated, width, after):
    rows = parts[0].shape[-2]
    step = min(16, rows)
    share = LANES // devices
    given = [place, *parts]
    specs = [pl.BlockSpec(memory_space=pltpu.SMEM)]
    specs += part_specs(devices, rotated, (share, step, B), lambda t, i: (t, i, 0))
    for array in (held, after):
        if array is not None:
            given.append(array)
            specs.append(pl.BlockSpec(memory_space=pl.ANY))
    return pl.pallas_call(
        functools.partial(merge_kernel, parts=len(parts), rotated=rotated),
        grid=(tiles, rows // step),
        in_specs=specs,
        out_specs=pl.BlockSpec((step, B, LANES), lambda t, i: (i, 0, tile + t)),
        out_shape=jax.ShapeDtypeStruct((rows, B, width), jnp.bfloat16),
        scratch_shapes=[pltpu.VMEM((step * LANES, B), jnp.float32)],
        input_output_aliases={} if held is None else {len(parts) + 1: 0},
        compiler_params=pltpu.CompilerParams(vmem_limit_bytes=VMEM_BYTES),
        cost_estimate=pl.CostEstimate(
            flops=0, bytes_accessed=4 * rows * B * LANES * tiles, transcendentals=0
        ),
    )(*given)


SECOND_AT = 2 * A
TWIDDLE_AT = SECOND_AT + B
CHANNEL_AT = TWIDDLE_AT + A


def mix_kernel(
    place_ref, gain_ref, bias_ref, skip_ref, *rest, parts, tile, tile_count, rotated
):
    tok_refs = views(rest[:parts], rotated)
    cot_refs = views(rest[parts : 2 * parts], rotated)
    first_ref, first_t_ref, second_ref, second_t_ref, twiddle_ref = rest[2 * parts : 2 * parts + 5]
    out_refs = views(rest[2 * parts + 5 : 3 * parts + 5], rotated)
    sums_ref, tok_all, cot_all = rest[-3:]
    t, step = pl.program_id(0), pl.program_id(1)

    @pl.when((t == 0) & (step == 0))
    def _():
        sums_ref[...] = jnp.zeros(sums_ref.shape, jnp.float32)

    devices = len(tok_refs)
    pair, rows, _ = tok_refs[0].shape
    share = LANES // devices
    lane_at = place_ref[0] + step * pair
    at = (tile + t) * LANES + lane_at

    def rows_from(shift):
        if not rotated:
            return slice(shift * rows, (shift + 1) * rows)
        source = (place_ref[0] // share - shift + devices) % devices
        return pl.ds(pl.multiple_of(source * rows, rows), rows)

    for refs, whole in ((tok_refs, tok_all), (cot_refs, cot_all)):
        for shift, ref in enumerate(refs):
            for c in range(pair):
                whole[rows_from(shift), c * B : (c + 1) * B] = ref[c].astype(jnp.float32)

    def spread(ref):
        lane = lax.broadcasted_iota(jnp.int32, (1, pair * B), 1)
        row = jnp.full((1, pair * B), ref[at], jnp.float32)
        for c in range(1, pair):
            row = jnp.where(lane >= c * B, ref[at + c], row)
        return row

    gain, bias, skip = spread(gain_ref), spread(bias_ref), spread(skip_ref)
    inputs = tok_all[...]
    tok = inputs.astype(jnp.bfloat16)
    upstream = cot_all[...]
    twiddle = jnp.concatenate([twiddle_ref[...]] * pair, axis=1)
    inner = dot(tok, second_t_ref[...], 1, 0)
    scaled = (inner * twiddle).astype(jnp.bfloat16)
    gate = jax.nn.sigmoid(gain * inputs + bias)
    grad_hidden = upstream * gate
    grad_outer = grad_hidden.astype(jnp.bfloat16)
    outer = dot(first_ref[...], scaled, 1, 0).astype(jnp.bfloat16).astype(jnp.float32)
    grad_scaled = dot(first_t_ref[...], grad_outer, 1, 0).astype(jnp.bfloat16).astype(jnp.float32)
    first_term = dot(grad_outer, scaled, 1, 1)
    for half in range(A // B):
        sums_ref[half * A : (half + 1) * A] += first_term[:, half * B : (half + 1) * B]
    hidden = outer + skip * inputs
    grad_pre = upstream * hidden * gate * (1.0 - gate)
    product = grad_scaled * inner
    sums_ref[TWIDDLE_AT:CHANNEL_AT] += sum(product[:, c * B : (c + 1) * B] for c in range(pair))
    grad_inner = (grad_scaled * twiddle).astype(jnp.bfloat16)
    second_term = dot(grad_inner, tok, 0, 0)
    sums_ref[SECOND_AT:TWIDDLE_AT] += sum(
        second_term[c * B : (c + 1) * B, c * B : (c + 1) * B] for c in range(pair)
    )
    lane = lax.broadcasted_iota(jnp.int32, (1, LANES), 1)
    for which, value in enumerate((grad_pre * inputs, grad_pre, grad_hidden * inputs)):
        total = jnp.sum(value, axis=0, keepdims=True)
        row = jnp.zeros((1, LANES), jnp.float32)
        for c in range(pair):
            channel = jnp.sum(total[:, c * B : (c + 1) * B], axis=1, keepdims=True)
            row = jnp.where(lane == lane_at + c, channel, row)
        sums_ref[pl.ds(CHANNEL_AT + which * tile_count + tile + t, 1), :] += row
    grad_in = dot(grad_inner, second_ref[...], 1, 0)
    tok_all[...] = grad_in + grad_hidden * skip + grad_pre * gain
    for shift, out_ref in enumerate(out_refs):
        for c in range(pair):
            out_ref[c] = tok_all[rows_from(shift), c * B : (c + 1) * B].astype(jnp.bfloat16)


def mix(parts, tile, tiles, planes, place, vectors, factors, sum_rows, devices, rotated):
    rows = parts[0].shape[-2]
    share = LANES // devices
    pair = factors[2].shape[0] // B
    steps = share // pair
    whole = lambda array: pl.BlockSpec(array.shape, lambda t, i: (0,) * array.ndim)
    tok_at = lambda t, i: (t * (planes // pair) + i, 0, 0)
    cot_at = lambda t, i: (t * (planes // pair) + steps + i, 0, 0)
    block = (pair, rows, B)
    tile_count = vectors[0].shape[0] // LANES
    *leaving, sums = pl.pallas_call(
        functools.partial(
            mix_kernel, parts=len(parts), tile=tile, tile_count=tile_count, rotated=rotated
        ),
        grid=(tiles, steps),
        in_specs=[pl.BlockSpec(memory_space=pltpu.SMEM)] * 4
        + part_specs(devices, rotated, block, tok_at)
        + part_specs(devices, rotated, block, cot_at)
        + [whole(f) for f in factors],
        out_specs=part_specs(devices, rotated, block, lambda t, i: (t * steps + i, 0, 0))
        + [pl.BlockSpec((sum_rows, LANES), lambda t, i: (0, 0))],
        out_shape=part_shapes(devices, rotated, (tiles * share, rows, B))
        + [jax.ShapeDtypeStruct((sum_rows, LANES), jnp.float32)],
        scratch_shapes=[pltpu.VMEM((A, pair * B), jnp.float32)] * 2,
        compiler_params=pltpu.CompilerParams(vmem_limit_bytes=VMEM_BYTES),
        cost_estimate=pl.CostEstimate(
            flops=tiles * share * A * B * 2 * 7000,
            bytes_accessed=tiles * share * A * B * 6,
            transcendentals=tiles * share * A * B * 2,
        ),
    )(place, *vectors, *parts, *parts, *factors)
    return leaving, sums


def block_diagonal(square, count):
    zero = jnp.zeros_like(square)
    return jnp.concatenate(
        [
            jnp.concatenate([square if i == j else zero for j in range(count)], axis=1)
            for i in range(count)
        ],
        axis=0,
    )


def body(tokens, cotangent, first_factor, second_factor, twiddle, gate_gain, gate_bias, skip_gain):
    seq_count, tok_rows, width = tokens.shape
    ctx_size = lax.axis_size("ctx")
    dp_size = lax.axis_size("dp")
    share = LANES // ctx_size
    local_rows = tok_rows // B
    tiles = width // LANES
    pair = 2
    half = tiles // 2
    groups = [(0, 1, False), (half, tiles - half, True), (1, half - 1, False)]
    merge_order = [0, 1, 2]

    place = (lax.axis_index("ctx") * share).astype(jnp.int32).reshape(1)
    second = block_diagonal(second_factor, pair)
    second_t = block_diagonal(second_factor.T, pair)
    vectors = [gate_gain, gate_bias, skip_gain]
    used_rows = CHANNEL_AT + 3 * tiles
    sum_rows = -(-used_rows // (8 * dp_size)) * 8 * dp_size

    def exchange(parts, sign, rotated):
        if not rotated:
            return [lax.all_to_all(parts[0], "ctx", split_axis=0, concat_axis=0, tiled=True)]
        moved = [parts[0]]
        for shift in range(1, ctx_size):
            pairs = [(i, (i + sign * shift) % ctx_size) for i in range(ctx_size)]
            moved.append(lax.ppermute(parts[shift], "ctx", pairs))
        return moved

    sums = jnp.zeros((sum_rows, LANES), jnp.float32)
    leaving = []
    for seq in range(seq_count):
        tok_blocks = tokens[seq].reshape(local_rows, B, width)
        cot_blocks = cotangent[seq].reshape(local_rows, B, width)
        arrived = []
        for at, count, rotated in groups:
            own = twiddle if at == 0 else None
            parts = split_channels(
                place, tok_blocks, cot_blocks, at, count, ctx_size, rotated, own
            )
            arrived.append(exchange(parts, 1, rotated))
        planes = arrived[0][0][:, 2 * share :].astype(jnp.float32)
        twiddle_all = (planes[:, 0] + planes[:, 1] + planes[:, 2]).reshape(A, B)
        factors = [first_factor, first_factor.T, second, second_t, twiddle_all]
        for (at, count, rotated), parts in zip(groups, arrived):
            parts, own_sums = mix(
                parts, at, count, 2 * share, place, vectors, factors, sum_rows, ctx_size, rotated
            )
            leaving.append(parts)
            sums = sums + own_sums

    own_rows = sum_rows // dp_size
    bit = 1
    while bit < dp_size:
        sums = sums + lax.ppermute(sums, "dp", [(i, i ^ bit) for i in range(dp_size)])
        bit *= 2
    sums = lax.dynamic_slice_in_dim(sums, lax.axis_index("dp") * own_rows, own_rows, 0)
    sums = jnp.sum(lax.all_gather(sums, "ctx"), axis=0)
    sums = lax.all_gather(sums, "dp", axis=0, tiled=True)

    grads = []
    for seq in range(seq_count):
        held = None
        for which in merge_order:
            at, count, rotated = groups[which]
            parts = exchange(leaving[seq * len(groups) + which], -1, rotated)
            after = sums if which == merge_order[-1] else None
            held = merge_channels(
                place, parts, held, at, count, ctx_size, rotated, width, after
            )
        grads.append(held.reshape(tok_rows, width))
    grad_tokens = jnp.stack(grads)

    total_seqs = seq_count * dp_size
    first_norm = math.sqrt(total_seqs * B * width)
    second_norm = math.sqrt(total_seqs * A * width)
    twiddle_norm = math.sqrt(total_seqs * width)
    channel_norm = math.sqrt(total_seqs * A * B)
    first_sum = jnp.concatenate([sums[half * A : (half + 1) * A] for half in range(A // B)], axis=1)
    mine = TWIDDLE_AT + lax.axis_index("ctx") * local_rows
    twiddle_sum = lax.dynamic_slice_in_dim(sums, mine, local_rows, 0)
    channel_sum = sums[CHANNEL_AT:used_rows].reshape(3, width)
    return (
        grad_tokens,
        first_sum / first_norm,
        sums[SECOND_AT:TWIDDLE_AT] / second_norm,
        twiddle_sum / twiddle_norm,
        channel_sum[0] / channel_norm,
        channel_sum[1] / channel_norm,
        channel_sum[2] / channel_norm,
    )


def solution(mesh):
    return jax.shard_map(
        body,
        mesh=mesh,
        in_specs=(
            P("dp", "ctx", None),
            P("dp", "ctx", None),
            P(),
            P(),
            P("ctx", None),
            P(),
            P(),
            P(),
        ),
        out_specs=(P("dp", "ctx", None), P(), P(), P("ctx", None), P(), P(), P()),
        check_vma=False,
    )
```

```python
import functools
import math

import jax
import jax.numpy as jnp
from jax import lax
from jax.experimental import pallas as pl
from jax.experimental.pallas import tpu as pltpu
from jax.sharding import PartitionSpec as P

A = 256
B = 128
LANES = 128
VMEM_BYTES = 48 * 1024 * 1024


def dot(left, right, left_dim, right_dim):
    return lax.dot_general(
        left, right, (((left_dim,), (right_dim,)), ((), ())), preferred_element_type=jnp.float32
    )


def views(refs, rotated):
    return list(refs) if rotated else [refs[0].at[i] for i in range(refs[0].shape[0])]


def split_tile(first_channel, tok_ref, cot_ref, out_refs, swap_ref):
    rows = tok_ref.shape[0]
    share = LANES // len(out_refs)
    for which, ref in enumerate((tok_ref, cot_ref)):
        for row in range(rows):
            swap_ref[row * LANES : (row + 1) * LANES, :] = ref[row].astype(jnp.float32).T
        for slot, out_ref in enumerate(out_refs):
            start = (first_channel + slot * share) % LANES
            for channel in range(share):
                out_ref[which * share + channel] = swap_ref[
                    pl.ds(start + channel, rows, stride=LANES), :
                ].astype(jnp.bfloat16)


def split_kernel(place_ref, tok_ref, cot_ref, *rest, rotated):
    first_channel = place_ref[0] if rotated else 0
    split_tile(first_channel, tok_ref, cot_ref, views(rest[:-1], rotated), rest[-1])


def split_twiddle_kernel(place_ref, tok_ref, cot_ref, twiddle_ref, *rest, rotated):
    split_kernel(place_ref, tok_ref, cot_ref, *rest, rotated=rotated)
    out_refs = views(rest[:-1], rotated)
    share = LANES // len(out_refs)
    left = twiddle_ref[...]
    for plane in range(3):
        part = left.astype(jnp.bfloat16)
        left = left - part.astype(jnp.float32)
        for out_ref in out_refs:
            out_ref[2 * share + plane] = part


def part_specs(devices, rotated, block, index):
    if rotated:
        return [pl.BlockSpec(block, index)] * devices
    return [pl.BlockSpec((devices, *block), lambda *at: (0, *index(*at)))]


def part_shapes(devices, rotated, shape):
    if rotated:
        return [jax.ShapeDtypeStruct(shape, jnp.bfloat16)] * devices
    return [jax.ShapeDtypeStruct((devices, *shape), jnp.bfloat16)]


def split_channels(place, tokens, cotangent, tile, tiles, devices, rotated, twiddle=None):
    rows = tokens.shape[0]
    step = min(16, rows)
    share = LANES // devices
    block = pl.BlockSpec((step, B, LANES), lambda t, i: (i, 0, tile + t))
    specs = [pl.BlockSpec(memory_space=pltpu.SMEM), block, block]
    if twiddle is None:
        kernel, given = split_kernel, [place, tokens, cotangent]
        planes = 2 * share
    else:
        kernel, given = split_twiddle_kernel, [place, tokens, cotangent, twiddle]
        specs.append(pl.BlockSpec((step, B), lambda t, i: (i, 0)))
        planes = 2 * share + 3
    return pl.pallas_call(
        functools.partial(kernel, rotated=rotated),
        grid=(tiles, rows // step),
        in_specs=specs,
        out_specs=part_specs(devices, rotated, (planes, step, B), lambda t, i: (t, i, 0)),
        out_shape=part_shapes(devices, rotated, (tiles * planes, rows, B)),
        scratch_shapes=[pltpu.VMEM((step * LANES, B), jnp.float32)],
        compiler_params=pltpu.CompilerParams(vmem_limit_bytes=VMEM_BYTES),
        cost_estimate=pl.CostEstimate(flops=1, bytes_accessed=16 * rows * B * LANES * tiles, transcendentals=0),
    )(*given)


def merge_kernel(place_ref, *rest, parts, rotated):
    part_refs, out_ref, swap_ref = views(rest[:parts], rotated), rest[-2], rest[-1]
    share, rows, _ = part_refs[0].shape
    for slot, part_ref in enumerate(part_refs):
        start = (place_ref[0] + slot * share) % LANES if rotated else slot * share
        for channel in range(share):
            at = pl.multiple_of((start + channel) * rows, rows)
            swap_ref[pl.ds(at, rows), :] = part_ref[channel].astype(jnp.float32)
    for row in range(rows):
        out_ref[row] = swap_ref[pl.ds(row, LANES, stride=rows), :].T.astype(jnp.bfloat16)


def merge_channels(place, parts, held, tile, tiles, devices, rotated, width, after):
    rows = parts[0].shape[-2]
    step = min(16, rows)
    share = LANES // devices
    given = [place, *parts]
    specs = [pl.BlockSpec(memory_space=pltpu.SMEM)]
    specs += part_specs(devices, rotated, (share, step, B), lambda t, i: (t, i, 0))
    for array in after if held is None else [held, *after]:
        given.append(array)
        specs.append(pl.BlockSpec(memory_space=pl.ANY))
    return pl.pallas_call(
        functools.partial(merge_kernel, parts=len(parts), rotated=rotated),
        grid=(tiles, rows // step),
        in_specs=specs,
        out_specs=pl.BlockSpec((step, B, LANES), lambda t, i: (i, 0, tile + t)),
        out_shape=jax.ShapeDtypeStruct((rows, B, width), jnp.bfloat16),
        scratch_shapes=[pltpu.VMEM((step * LANES, B), jnp.float32)],
        input_output_aliases={} if held is None else {len(parts) + 1: 0},
        compiler_params=pltpu.CompilerParams(vmem_limit_bytes=VMEM_BYTES),
        cost_estimate=pl.CostEstimate(flops=1, bytes_accessed=8 * rows * B * LANES * tiles, transcendentals=0),
    )(*given)


SECOND_AT = 2 * A
TWIDDLE_AT = SECOND_AT + B
CHANNEL_AT = TWIDDLE_AT + A


def mix_kernel(
    place_ref, gain_ref, bias_ref, skip_ref, *rest, parts, tile, tile_count, rotated
):
    tok_refs = views(rest[:parts], rotated)
    cot_refs = views(rest[parts : 2 * parts], rotated)
    first_ref, first_t_ref, second_ref, second_t_ref, twiddle_ref = rest[2 * parts : 2 * parts + 5]
    out_refs = views(rest[-3 - parts : -3], rotated)
    sums_ref, tok_all, cot_all = rest[-3:]
    t, step = pl.program_id(0), pl.program_id(1)

    @pl.when((t == 0) & (step == 0))
    def _():
        sums_ref[...] = jnp.zeros(sums_ref.shape, jnp.float32)

    devices = len(tok_refs)
    pair, rows, _ = tok_refs[0].shape
    share = LANES // devices
    lane_at = place_ref[0] + step * pair
    at = (tile + t) * LANES + lane_at

    def rows_from(shift):
        if not rotated:
            return slice(shift * rows, (shift + 1) * rows)
        source = (place_ref[0] // share - shift + devices) % devices
        return pl.ds(pl.multiple_of(source * rows, rows), rows)

    for refs, whole in ((tok_refs, tok_all), (cot_refs, cot_all)):
        for shift, ref in enumerate(refs):
            for c in range(pair):
                whole[rows_from(shift), c * B : (c + 1) * B] = ref[c].astype(jnp.float32)

    def spread(ref):
        lane = lax.broadcasted_iota(jnp.int32, (1, pair * B), 1)
        row = jnp.full((1, pair * B), ref[at], jnp.float32)
        for c in range(1, pair):
            row = jnp.where(lane >= c * B, ref[at + c], row)
        return row

    gain, bias, skip = spread(gain_ref), spread(bias_ref), spread(skip_ref)
    inputs = tok_all[...]
    tok = inputs.astype(jnp.bfloat16)
    upstream = cot_all[...]
    twiddle = jnp.concatenate([twiddle_ref[...]] * pair, axis=1)
    inner = dot(tok, second_t_ref[...], 1, 0)
    scaled = (inner * twiddle).astype(jnp.bfloat16)
    gate = jax.nn.sigmoid(gain * inputs + bias)
    grad_hidden = upstream * gate
    grad_outer = grad_hidden.astype(jnp.bfloat16)
    outer = dot(first_ref[...], scaled, 1, 0).astype(jnp.bfloat16).astype(jnp.float32)
    grad_scaled = dot(first_t_ref[...], grad_outer, 1, 0).astype(jnp.bfloat16).astype(jnp.float32)
    first_term = dot(grad_outer, scaled, 1, 1)
    for half in range(A // B):
        sums_ref[half * A : (half + 1) * A] += first_term[:, half * B : (half + 1) * B]
    hidden = outer + skip * inputs
    grad_pre = upstream * hidden * gate * (1.0 - gate)
    product = grad_scaled * inner
    sums_ref[TWIDDLE_AT:CHANNEL_AT] += sum(product[:, c * B : (c + 1) * B] for c in range(pair))
    grad_inner = (grad_scaled * twiddle).astype(jnp.bfloat16)
    second_term = dot(grad_inner, tok, 0, 0)
    sums_ref[SECOND_AT:TWIDDLE_AT] += sum(
        second_term[c * B : (c + 1) * B, c * B : (c + 1) * B] for c in range(pair)
    )
    lane = lax.broadcasted_iota(jnp.int32, (1, LANES), 1)
    for which, value in enumerate((grad_pre * inputs, grad_pre, grad_hidden * inputs)):
        total = jnp.sum(value, axis=0, keepdims=True)
        row = jnp.zeros((1, LANES), jnp.float32)
        for c in range(pair):
            channel = jnp.sum(total[:, c * B : (c + 1) * B], axis=1, keepdims=True)
            row = jnp.where(lane == lane_at + c, channel, row)
        sums_ref[pl.ds(CHANNEL_AT + which * tile_count + tile + t, 1), :] += row
    grad_in = dot(grad_inner, second_ref[...], 1, 0)
    tok_all[...] = grad_in + grad_hidden * skip + grad_pre * gain
    for shift, out_ref in enumerate(out_refs):
        for c in range(pair):
            out_ref[c] = tok_all[rows_from(shift), c * B : (c + 1) * B].astype(jnp.bfloat16)


def mix(parts, tile, tiles, planes, place, vectors, factors, sum_rows, devices, rotated, after):
    rows = parts[0].shape[-2]
    share = LANES // devices
    pair = factors[2].shape[0] // B
    steps = share // pair
    whole = lambda array: pl.BlockSpec(array.shape, lambda t, i: (0,) * array.ndim)
    tok_at = lambda t, i: (t * (planes // pair) + i, 0, 0)
    cot_at = lambda t, i: (t * (planes // pair) + steps + i, 0, 0)
    block = (pair, rows, B)
    tile_count = vectors[0].shape[0] // LANES
    *leaving, sums = pl.pallas_call(
        functools.partial(
            mix_kernel, parts=len(parts), tile=tile, tile_count=tile_count, rotated=rotated
        ),
        grid=(tiles, steps),
        in_specs=[pl.BlockSpec(memory_space=pltpu.SMEM)] * 4
        + part_specs(devices, rotated, block, tok_at)
        + part_specs(devices, rotated, block, cot_at)
        + [whole(f) for f in factors]
        + [pl.BlockSpec(memory_space=pl.ANY)] * len(after),
        out_specs=part_specs(devices, rotated, block, lambda t, i: (t * steps + i, 0, 0))
        + [pl.BlockSpec((sum_rows, LANES), lambda t, i: (0, 0))],
        out_shape=part_shapes(devices, rotated, (tiles * share, rows, B))
        + [jax.ShapeDtypeStruct((sum_rows, LANES), jnp.float32)],
        scratch_shapes=[pltpu.VMEM((A, pair * B), jnp.float32)] * 2,
        compiler_params=pltpu.CompilerParams(vmem_limit_bytes=VMEM_BYTES),
        cost_estimate=pl.CostEstimate(flops=tiles * share * A * B * 16000, bytes_accessed=1024, transcendentals=0),
    )(place, *vectors, *parts, *parts, *factors, *after)
    return leaving, sums


def add_kernel(*refs):
    total = refs[0][...]
    for ref in refs[1:-1]:
        total += ref[...]
    refs[-1][...] = total


def add(terms):
    vmem = pl.BlockSpec(memory_space=pltpu.VMEM)
    return pl.pallas_call(
        add_kernel,
        in_specs=[vmem] * len(terms),
        out_specs=vmem,
        out_shape=jax.ShapeDtypeStruct(terms[0].shape, terms[0].dtype),
        cost_estimate=pl.CostEstimate(flops=1, bytes_accessed=1024, transcendentals=0),
    )(*terms)


def hold(arrays, after):
    anywhere = pl.BlockSpec(memory_space=pl.ANY)
    return pl.pallas_call(
        lambda *refs: None,
        in_specs=[anywhere] * (len(arrays) + 1),
        out_specs=[anywhere] * len(arrays),
        out_shape=[jax.ShapeDtypeStruct(a.shape, a.dtype) for a in arrays],
        input_output_aliases={i: i for i in range(len(arrays))},
        cost_estimate=pl.CostEstimate(flops=1, bytes_accessed=1024, transcendentals=0),
    )(*arrays, after)


def block_diagonal(square, count):
    zero = jnp.zeros_like(square)
    return jnp.concatenate(
        [
            jnp.concatenate([square if i == j else zero for j in range(count)], axis=1)
            for i in range(count)
        ],
        axis=0,
    )


def sum_over_mesh(sums, beside):
    beside = list(beside)

    def exchange_with(array, axis, bit):
        if beside:
            (array,) = hold([array], beside.pop(0))
        size = lax.axis_size(axis)
        return array, lax.ppermute(array, axis, [(i, i ^ bit) for i in range(size)])

    dp = lax.axis_index("dp")
    bits = [1 << k for k in range(lax.axis_size("dp").bit_length() - 1)]
    for bit in reversed(bits):
        halves = sums.reshape(2, -1, LANES)
        high = (dp & bit) != 0
        _, other = exchange_with(jnp.where(high, halves[0], halves[1]), "dp", bit)
        sums = jnp.where(high, halves[1], halves[0]) + other
    bit = 1
    while bit < lax.axis_size("ctx"):
        sums, other = exchange_with(sums, "ctx", bit)
        sums = sums + other
        bit *= 2
    for bit in bits:
        sums, other = exchange_with(sums, "dp", bit)
        high = (dp & bit) != 0
        sums = jnp.concatenate([jnp.where(high, other, sums), jnp.where(high, sums, other)])
    return sums


def body(tokens, cotangent, first_factor, second_factor, twiddle, gate_gain, gate_bias, skip_gain):
    seq_count, tok_rows, width = tokens.shape
    ctx_size = lax.axis_size("ctx")
    dp_size = lax.axis_size("dp")
    share = LANES // ctx_size
    local_rows = tok_rows // B
    tiles = width // LANES
    pair = 2
    groups = [(0, 1, True), (1, tiles - 2, True), (tiles - 1, 1, True)]

    place = (lax.axis_index("ctx") * share).astype(jnp.int32).reshape(1)
    second = block_diagonal(second_factor, pair)
    second_t = block_diagonal(second_factor.T, pair)
    vectors = [gate_gain, gate_bias, skip_gain]
    used_rows = CHANNEL_AT + 3 * tiles
    sum_rows = -(-used_rows // (8 * dp_size)) * 8 * dp_size

    def exchange(parts, sign, rotated):
        if not rotated:
            return [lax.all_to_all(parts[0], "ctx", split_axis=0, concat_axis=0, tiled=True)]
        moved = [parts[0]]
        for shift in range(1, ctx_size):
            pairs = [(i, (i + sign * shift) % ctx_size) for i in range(ctx_size)]
            moved.append(lax.ppermute(parts[shift], "ctx", pairs))
        return moved

    terms = []
    leaving = []
    for seq in range(seq_count):
        tok_blocks = tokens[seq].reshape(local_rows, B, width)
        cot_blocks = cotangent[seq].reshape(local_rows, B, width)
        arrived = []
        for at, count, rotated in groups:
            own = twiddle if at == 0 else None
            parts = split_channels(
                place, tok_blocks, cot_blocks, at, count, ctx_size, rotated, own
            )
            if arrived:
                parts = hold(parts, arrived[-1][1])
            arrived.append(exchange(parts, 1, rotated))
        planes = [part[..., 2 * share :, :, :].astype(jnp.float32) for part in arrived[0]]
        planes = jnp.stack(planes).reshape(ctx_size, 3, local_rows, B)
        twiddle_all = planes[:, 0] + planes[:, 1] + planes[:, 2]
        if groups[0][2]:
            twice = jnp.concatenate([twiddle_all[::-1]] * 2, axis=0)
            turn = ctx_size - 1 - lax.axis_index("ctx")
            twiddle_all = lax.dynamic_slice_in_dim(twice, turn, ctx_size, 0)
        twiddle_all = twiddle_all.reshape(A, B)
        factors = [first_factor, first_factor.T, second, second_t, twiddle_all]
        returned = []
        for which, ((at, count, rotated), parts) in enumerate(zip(groups, arrived)):
            last = which == len(groups) - 1
            parts, own_sums = mix(
                parts, at, count, 2 * share, place, vectors, factors, sum_rows, ctx_size, rotated,
                [*returned[0], returned[1][1]] if last else [],
            )
            returned.append(parts if last else exchange(parts, -1, rotated))
            terms.append(own_sums)
        leaving.append(returned)

    sums = sum_over_mesh(add(terms), leaving[-1][1][2:])

    grads = []
    for returned in leaving:
        returned[-1] = exchange(returned[-1], -1, True)
        held = None
        for which, ((at, count, rotated), parts) in enumerate(zip(groups, returned)):
            after = [returned[-1][1]] if which == len(groups) - 2 else []
            held = merge_channels(
                place, parts, held, at, count, ctx_size, rotated, width, after
            )
        grads.append(held.reshape(tok_rows, width))
    grad_tokens = jnp.stack(grads)

    total_seqs = seq_count * dp_size
    first_norm = math.sqrt(total_seqs * B * width)
    second_norm = math.sqrt(total_seqs * A * width)
    twiddle_norm = math.sqrt(total_seqs * width)
    channel_norm = math.sqrt(total_seqs * A * B)
    first_sum = jnp.concatenate([sums[half * A : (half + 1) * A] for half in range(A // B)], axis=1)
    mine = TWIDDLE_AT + lax.axis_index("ctx") * local_rows
    twiddle_sum = lax.dynamic_slice_in_dim(sums, mine, local_rows, 0)
    channel_sum = sums[CHANNEL_AT:used_rows].reshape(3, width)
    return (
        grad_tokens,
        first_sum / first_norm,
        sums[SECOND_AT:TWIDDLE_AT] / second_norm,
        twiddle_sum / twiddle_norm,
        channel_sum[0] / channel_norm,
        channel_sum[1] / channel_norm,
        channel_sum[2] / channel_norm,
    )


def solution(mesh):
    return jax.shard_map(
        body,
        mesh=mesh,
        in_specs=(
            P("dp", "ctx", None),
            P("dp", "ctx", None),
            P(),
            P(),
            P("ctx", None),
            P(),
            P(),
            P(),
        ),
        out_specs=(P("dp", "ctx", None), P(), P(), P("ctx", None), P(), P(), P()),
        check_vma=False,
    )
```

```python
import functools
import math

import jax
import jax.numpy as jnp
from jax import lax
from jax.experimental import pallas as pl
from jax.experimental.pallas import tpu as pltpu
from jax.sharding import PartitionSpec as P

A = 256
B = 128
LANES = 128
VMEM_BYTES = 48 * 1024 * 1024


def dot(left, right, left_dim, right_dim):
    return lax.dot_general(
        left, right, (((left_dim,), (right_dim,)), ((), ())), preferred_element_type=jnp.float32
    )


def views(refs, rotated):
    return list(refs) if rotated else [refs[0].at[i] for i in range(refs[0].shape[0])]


def split_tile(first_channel, tok_ref, cot_ref, out_refs, swap_ref):
    rows = tok_ref.shape[0]
    share = LANES // len(out_refs)
    for which, ref in enumerate((tok_ref, cot_ref)):
        for row in range(rows):
            swap_ref[row * LANES : (row + 1) * LANES, :] = ref[row].astype(jnp.float32).T
        for slot, out_ref in enumerate(out_refs):
            start = (first_channel + slot * share) % LANES
            for channel in range(share):
                out_ref[which * share + channel] = swap_ref[
                    pl.ds(start + channel, rows, stride=LANES), :
                ].astype(jnp.bfloat16)


def split_kernel(place_ref, tok_ref, cot_ref, *rest, rotated):
    first_channel = place_ref[0] if rotated else 0
    split_tile(first_channel, tok_ref, cot_ref, views(rest[:-1], rotated), rest[-1])


def split_twiddle_kernel(place_ref, tok_ref, cot_ref, twiddle_ref, *rest, rotated):
    split_kernel(place_ref, tok_ref, cot_ref, *rest, rotated=rotated)
    out_refs = views(rest[:-1], rotated)
    share = LANES // len(out_refs)
    left = twiddle_ref[...]
    for plane in range(3):
        part = left.astype(jnp.bfloat16)
        left = left - part.astype(jnp.float32)
        for out_ref in out_refs:
            out_ref[2 * share + plane] = part


def part_specs(devices, rotated, block, index):
    if rotated:
        return [pl.BlockSpec(block, index)] * devices
    return [pl.BlockSpec((devices, *block), lambda *at: (0, *index(*at)))]


def part_shapes(devices, rotated, shape):
    if rotated:
        return [jax.ShapeDtypeStruct(shape, jnp.bfloat16)] * devices
    return [jax.ShapeDtypeStruct((devices, *shape), jnp.bfloat16)]


def split_channels(place, tokens, cotangent, tile, tiles, devices, rotated, twiddle=None):
    rows = tokens.shape[0]
    step = min(16, rows)
    share = LANES // devices
    block = pl.BlockSpec((step, B, LANES), lambda t, i: (i, 0, tile + t))
    specs = [pl.BlockSpec(memory_space=pltpu.SMEM), block, block]
    if twiddle is None:
        kernel, given = split_kernel, [place, tokens, cotangent]
        planes = 2 * share
    else:
        kernel, given = split_twiddle_kernel, [place, tokens, cotangent, twiddle]
        specs.append(pl.BlockSpec((step, B), lambda t, i: (i, 0)))
        planes = 2 * share + 3
    return pl.pallas_call(
        functools.partial(kernel, rotated=rotated),
        grid=(tiles, rows // step),
        in_specs=specs,
        out_specs=part_specs(devices, rotated, (planes, step, B), lambda t, i: (t, i, 0)),
        out_shape=part_shapes(devices, rotated, (tiles * planes, rows, B)),
        scratch_shapes=[pltpu.VMEM((step * LANES, B), jnp.float32)],
        compiler_params=pltpu.CompilerParams(vmem_limit_bytes=VMEM_BYTES),
        cost_estimate=pl.CostEstimate(flops=1, bytes_accessed=16 * rows * B * LANES * tiles, transcendentals=0),
    )(*given)


def merge_kernel(place_ref, *rest, parts, rotated):
    part_refs, out_ref, swap_ref = views(rest[:parts], rotated), rest[-2], rest[-1]
    share, rows, _ = part_refs[0].shape
    for slot, part_ref in enumerate(part_refs):
        start = (place_ref[0] + slot * share) % LANES if rotated else slot * share
        for channel in range(share):
            at = pl.multiple_of((start + channel) * rows, rows)
            swap_ref[pl.ds(at, rows), :] = part_ref[channel].astype(jnp.float32)
    for row in range(rows):
        out_ref[row] = swap_ref[pl.ds(row, LANES, stride=rows), :].T.astype(jnp.bfloat16)


def merge_channels(place, parts, held, tile, tiles, devices, rotated, width, after):
    rows = parts[0].shape[-2]
    step = min(16, rows)
    share = LANES // devices
    given = [place, *parts]
    specs = [pl.BlockSpec(memory_space=pltpu.SMEM)]
    specs += part_specs(devices, rotated, (share, step, B), lambda t, i: (t, i, 0))
    for array in after if held is None else [held, *after]:
        given.append(array)
        specs.append(pl.BlockSpec(memory_space=pl.ANY))
    return pl.pallas_call(
        functools.partial(merge_kernel, parts=len(parts), rotated=rotated),
        grid=(tiles, rows // step),
        in_specs=specs,
        out_specs=pl.BlockSpec((step, B, LANES), lambda t, i: (i, 0, tile + t)),
        out_shape=jax.ShapeDtypeStruct((rows, B, width), jnp.bfloat16),
        scratch_shapes=[pltpu.VMEM((step * LANES, B), jnp.float32)],
        input_output_aliases={} if held is None else {len(parts) + 1: 0},
        compiler_params=pltpu.CompilerParams(vmem_limit_bytes=VMEM_BYTES),
        cost_estimate=pl.CostEstimate(flops=1, bytes_accessed=8 * rows * B * LANES * tiles, transcendentals=0),
    )(*given)


SECOND_AT = 2 * A
TWIDDLE_AT = SECOND_AT + B
CHANNEL_AT = TWIDDLE_AT + A


def mix_kernel(
    place_ref, gain_ref, bias_ref, skip_ref, *rest, parts, tile, tile_count, rotated
):
    tok_refs = views(rest[:parts], rotated)
    cot_refs = views(rest[parts : 2 * parts], rotated)
    first_ref, first_t_ref, second_ref, second_t_ref, twiddle_ref = rest[2 * parts : 2 * parts + 5]
    out_refs = views(rest[-3 - parts : -3], rotated)
    sums_ref, tok_all, cot_all = rest[-3:]
    t, step = pl.program_id(0), pl.program_id(1)

    @pl.when((t == 0) & (step == 0))
    def _():
        sums_ref[...] = jnp.zeros(sums_ref.shape, jnp.float32)

    devices = len(tok_refs)
    pair, rows, _ = tok_refs[0].shape
    share = LANES // devices
    lane_at = place_ref[0] + step * pair
    at = (tile + t) * LANES + lane_at

    def rows_from(shift):
        if not rotated:
            return slice(shift * rows, (shift + 1) * rows)
        source = (place_ref[0] // share - shift + devices) % devices
        return pl.ds(pl.multiple_of(source * rows, rows), rows)

    for refs, whole in ((tok_refs, tok_all), (cot_refs, cot_all)):
        for shift, ref in enumerate(refs):
            for c in range(pair):
                whole[rows_from(shift), c * B : (c + 1) * B] = ref[c].astype(jnp.float32)

    def spread(ref):
        lane = lax.broadcasted_iota(jnp.int32, (1, pair * B), 1)
        row = jnp.full((1, pair * B), ref[at], jnp.float32)
        for c in range(1, pair):
            row = jnp.where(lane >= c * B, ref[at + c], row)
        return row

    gain, bias, skip = spread(gain_ref), spread(bias_ref), spread(skip_ref)
    inputs = tok_all[...]
    tok = inputs.astype(jnp.bfloat16)
    upstream = cot_all[...]
    twiddle = jnp.concatenate([twiddle_ref[...]] * pair, axis=1)
    inner = dot(tok, second_t_ref[...], 1, 0)
    scaled = (inner * twiddle).astype(jnp.bfloat16)
    gate = jax.nn.sigmoid(gain * inputs + bias)
    grad_hidden = upstream * gate
    grad_outer = grad_hidden.astype(jnp.bfloat16)
    outer = dot(first_ref[...], scaled, 1, 0).astype(jnp.bfloat16).astype(jnp.float32)
    grad_scaled = dot(first_t_ref[...], grad_outer, 1, 0).astype(jnp.bfloat16).astype(jnp.float32)
    first_term = dot(grad_outer, scaled, 1, 1)
    for half in range(A // B):
        sums_ref[half * A : (half + 1) * A] += first_term[:, half * B : (half + 1) * B]
    hidden = outer + skip * inputs
    grad_pre = upstream * hidden * gate * (1.0 - gate)
    product = grad_scaled * inner
    sums_ref[TWIDDLE_AT:CHANNEL_AT] += sum(product[:, c * B : (c + 1) * B] for c in range(pair))
    grad_inner = (grad_scaled * twiddle).astype(jnp.bfloat16)
    second_term = dot(grad_inner, tok, 0, 0)
    sums_ref[SECOND_AT:TWIDDLE_AT] += sum(
        second_term[c * B : (c + 1) * B, c * B : (c + 1) * B] for c in range(pair)
    )
    lane = lax.broadcasted_iota(jnp.int32, (1, LANES), 1)
    for which, value in enumerate((grad_pre * inputs, grad_pre, grad_hidden * inputs)):
        total = jnp.sum(value, axis=0, keepdims=True)
        row = jnp.zeros((1, LANES), jnp.float32)
        for c in range(pair):
            channel = jnp.sum(total[:, c * B : (c + 1) * B], axis=1, keepdims=True)
            row = jnp.where(lane == lane_at + c, channel, row)
        sums_ref[pl.ds(CHANNEL_AT + which * tile_count + tile + t, 1), :] += row
    grad_in = dot(grad_inner, second_ref[...], 1, 0)
    tok_all[...] = grad_in + grad_hidden * skip + grad_pre * gain
    for shift, out_ref in enumerate(out_refs):
        for c in range(pair):
            out_ref[c] = tok_all[rows_from(shift), c * B : (c + 1) * B].astype(jnp.bfloat16)


def mix(parts, tile, tiles, planes, place, vectors, factors, sum_rows, devices, rotated, after):
    rows = parts[0].shape[-2]
    share = LANES // devices
    pair = factors[2].shape[0] // B
    steps = share // pair
    whole = lambda array: pl.BlockSpec(array.shape, lambda t, i: (0,) * array.ndim)
    tok_at = lambda t, i: (t * (planes // pair) + i, 0, 0)
    cot_at = lambda t, i: (t * (planes // pair) + steps + i, 0, 0)
    block = (pair, rows, B)
    tile_count = vectors[0].shape[0] // LANES
    *leaving, sums = pl.pallas_call(
        functools.partial(
            mix_kernel, parts=len(parts), tile=tile, tile_count=tile_count, rotated=rotated
        ),
        grid=(tiles, steps),
        in_specs=[pl.BlockSpec(memory_space=pltpu.SMEM)] * 4
        + part_specs(devices, rotated, block, tok_at)
        + part_specs(devices, rotated, block, cot_at)
        + [whole(f) for f in factors]
        + [pl.BlockSpec(memory_space=pl.ANY)] * len(after),
        out_specs=part_specs(devices, rotated, block, lambda t, i: (t * steps + i, 0, 0))
        + [pl.BlockSpec((sum_rows, LANES), lambda t, i: (0, 0))],
        out_shape=part_shapes(devices, rotated, (tiles * share, rows, B))
        + [jax.ShapeDtypeStruct((sum_rows, LANES), jnp.float32)],
        scratch_shapes=[pltpu.VMEM((A, pair * B), jnp.float32)] * 2,
        compiler_params=pltpu.CompilerParams(vmem_limit_bytes=VMEM_BYTES),
        cost_estimate=pl.CostEstimate(flops=tiles * share * A * B * 16000, bytes_accessed=1024, transcendentals=0),
    )(place, *vectors, *parts, *parts, *factors, *after)
    return leaving, sums


def add_kernel(*refs):
    total = refs[0][...]
    for ref in refs[1:-1]:
        total += ref[...]
    refs[-1][...] = total


def add(terms):
    vmem = pl.BlockSpec(memory_space=pltpu.VMEM)
    return pl.pallas_call(
        add_kernel,
        in_specs=[vmem] * len(terms),
        out_specs=vmem,
        out_shape=jax.ShapeDtypeStruct(terms[0].shape, terms[0].dtype),
        cost_estimate=pl.CostEstimate(flops=1, bytes_accessed=1024, transcendentals=0),
    )(*terms)


def hold(arrays, after):
    anywhere = pl.BlockSpec(memory_space=pl.ANY)
    return pl.pallas_call(
        lambda *refs: None,
        in_specs=[anywhere] * (len(arrays) + len(after)),
        out_specs=[anywhere] * len(arrays),
        out_shape=[jax.ShapeDtypeStruct(a.shape, a.dtype) for a in arrays],
        input_output_aliases={i: i for i in range(len(arrays))},
        cost_estimate=pl.CostEstimate(flops=1, bytes_accessed=1024, transcendentals=0),
    )(*arrays, *after)


def block_diagonal(square, count):
    zero = jnp.zeros_like(square)
    return jnp.concatenate(
        [
            jnp.concatenate([square if i == j else zero for j in range(count)], axis=1)
            for i in range(count)
        ],
        axis=0,
    )


def sum_over_mesh(sums):
    dp = lax.axis_index("dp")
    size = lax.axis_size("dp")
    for bit in reversed([1 << k for k in range(size.bit_length() - 1)]):
        halves = sums.reshape(2, -1, LANES)
        high = (dp & bit) != 0
        sent = jnp.where(high, halves[0], halves[1])
        kept = jnp.where(high, halves[1], halves[0])
        sums = kept + lax.ppermute(sent, "dp", [(i, i ^ bit) for i in range(size)])
    sums = jnp.sum(lax.all_gather(sums, "ctx"), axis=0)
    return lax.all_gather(sums, "dp", axis=0, tiled=True)


def body(tokens, cotangent, first_factor, second_factor, twiddle, gate_gain, gate_bias, skip_gain):
    seq_count, tok_rows, width = tokens.shape
    ctx_size = lax.axis_size("ctx")
    dp_size = lax.axis_size("dp")
    share = LANES // ctx_size
    local_rows = tok_rows // B
    tiles = width // LANES
    pair = 2
    half = tiles // 2
    groups = [(0, 1, False), (half, tiles - half, True), (1, half - 1, False)]
    merge_order = [0, 1, 2]

    place = (lax.axis_index("ctx") * share).astype(jnp.int32).reshape(1)
    second = block_diagonal(second_factor, pair)
    second_t = block_diagonal(second_factor.T, pair)
    vectors = [gate_gain, gate_bias, skip_gain]
    used_rows = CHANNEL_AT + 3 * tiles
    sum_rows = -(-used_rows // (8 * dp_size)) * 8 * dp_size

    def exchange(parts, sign, rotated):
        if not rotated:
            return [lax.all_to_all(parts[0], "ctx", split_axis=0, concat_axis=0, tiled=True)]
        moved = [parts[0]]
        for shift in range(1, ctx_size):
            pairs = [(i, (i + sign * shift) % ctx_size) for i in range(ctx_size)]
            moved.append(lax.ppermute(parts[shift], "ctx", pairs))
        return moved

    terms = []
    leaving = []
    for seq in range(seq_count):
        tok_blocks = tokens[seq].reshape(local_rows, B, width)
        cot_blocks = cotangent[seq].reshape(local_rows, B, width)
        arrived = []
        for at, count, rotated in groups:
            own = twiddle if at == 0 else None
            parts = split_channels(
                place, tok_blocks, cot_blocks, at, count, ctx_size, rotated, own
            )
            if len(arrived) == 2:
                parts = hold(parts, arrived[1][1:6])
            arrived.append(exchange(parts, 1, rotated))
        planes = [part[..., 2 * share :, :, :].astype(jnp.float32) for part in arrived[0]]
        planes = jnp.stack(planes).reshape(ctx_size, 3, local_rows, B)
        twiddle_all = planes[:, 0] + planes[:, 1] + planes[:, 2]
        if groups[0][2]:
            twice = jnp.concatenate([twiddle_all[::-1]] * 2, axis=0)
            turn = ctx_size - 1 - lax.axis_index("ctx")
            twiddle_all = lax.dynamic_slice_in_dim(twice, turn, ctx_size, 0)
        twiddle_all = twiddle_all.reshape(A, B)
        factors = [first_factor, first_factor.T, second, second_t, twiddle_all]
        returned = []
        for which, ((at, count, rotated), parts) in enumerate(zip(groups, arrived)):
            after = returned[1][1:] if which == 2 else []
            parts, own_sums = mix(
                parts, at, count, 2 * share, place, vectors, factors, sum_rows, ctx_size, rotated,
                after,
            )
            returned.append(exchange(parts, -1, rotated))
            terms.append(own_sums)
        leaving.append(returned)

    sums = sum_over_mesh(add(terms))
    grads = []
    for returned in leaving:
        held = None
        for which in merge_order:
            at, count, rotated = groups[which]
            after = [sums] if which == merge_order[-1] else []
            held = merge_channels(
                place, returned[which], held, at, count, ctx_size, rotated, width, after
            )
        grads.append(held.reshape(tok_rows, width))
    grad_tokens = jnp.stack(grads)

    total_seqs = seq_count * dp_size
    first_norm = math.sqrt(total_seqs * B * width)
    second_norm = math.sqrt(total_seqs * A * width)
    twiddle_norm = math.sqrt(total_seqs * width)
    channel_norm = math.sqrt(total_seqs * A * B)
    first_sum = jnp.concatenate([sums[half * A : (half + 1) * A] for half in range(A // B)], axis=1)
    mine = TWIDDLE_AT + lax.axis_index("ctx") * local_rows
    twiddle_sum = lax.dynamic_slice_in_dim(sums, mine, local_rows, 0)
    channel_sum = sums[CHANNEL_AT:used_rows].reshape(3, width)
    return (
        grad_tokens,
        first_sum / first_norm,
        sums[SECOND_AT:TWIDDLE_AT] / second_norm,
        twiddle_sum / twiddle_norm,
        channel_sum[0] / channel_norm,
        channel_sum[1] / channel_norm,
        channel_sum[2] / channel_norm,
    )


def solution(mesh):
    return jax.shard_map(
        body,
        mesh=mesh,
        in_specs=(
            P("dp", "ctx", None),
            P("dp", "ctx", None),
            P(),
            P(),
            P("ctx", None),
            P(),
            P(),
            P(),
        ),
        out_specs=(P("dp", "ctx", None), P(), P(), P("ctx", None), P(), P(), P()),
        check_vma=False,
    )
```

```python
import functools
import math

import jax
import jax.numpy as jnp
from jax import lax
from jax.experimental import pallas as pl
from jax.experimental.pallas import tpu as pltpu
from jax.sharding import PartitionSpec as P

A = 256
B = 128
LANES = 128
RETURN_FIRST = 4
VMEM_BYTES = 48 * 1024 * 1024


def dot(left, right, left_dim, right_dim):
    return lax.dot_general(
        left, right, (((left_dim,), (right_dim,)), ((), ())), preferred_element_type=jnp.float32
    )


def views(refs, rotated):
    return list(refs) if rotated else [refs[0].at[i] for i in range(refs[0].shape[0])]


def split_tile(first_channel, tok_ref, cot_ref, out_refs, swap_ref):
    rows = tok_ref.shape[0]
    share = LANES // len(out_refs)
    for which, ref in enumerate((tok_ref, cot_ref)):
        for row in range(rows):
            swap_ref[row * LANES : (row + 1) * LANES, :] = ref[row].astype(jnp.float32).T
        for slot, out_ref in enumerate(out_refs):
            start = (first_channel + slot * share) % LANES
            for channel in range(share):
                out_ref[which * share + channel] = swap_ref[
                    pl.ds(start + channel, rows, stride=LANES), :
                ].astype(jnp.bfloat16)


def split_kernel(place_ref, tok_ref, cot_ref, *rest, rotated):
    first_channel = place_ref[0] if rotated else 0
    split_tile(first_channel, tok_ref, cot_ref, views(rest[:-1], rotated), rest[-1])


def split_twiddle_kernel(place_ref, tok_ref, cot_ref, twiddle_ref, *rest, rotated):
    split_kernel(place_ref, tok_ref, cot_ref, *rest, rotated=rotated)
    out_refs = views(rest[:-1], rotated)
    share = LANES // len(out_refs)
    left = twiddle_ref[...]
    for plane in range(3):
        part = left.astype(jnp.bfloat16)
        left = left - part.astype(jnp.float32)
        for out_ref in out_refs:
            out_ref[2 * share + plane] = part


def part_specs(devices, rotated, block, index):
    if rotated:
        return [pl.BlockSpec(block, index)] * devices
    return [pl.BlockSpec((devices, *block), lambda *at: (0, *index(*at)))]


def part_shapes(devices, rotated, shape):
    if rotated:
        return [jax.ShapeDtypeStruct(shape, jnp.bfloat16)] * devices
    return [jax.ShapeDtypeStruct((devices, *shape), jnp.bfloat16)]


def split_channels(place, tokens, cotangent, tile, tiles, devices, rotated, twiddle=None):
    rows = tokens.shape[0]
    step = min(16, rows)
    share = LANES // devices
    block = pl.BlockSpec((step, B, LANES), lambda t, i: (i, 0, tile + t))
    specs = [pl.BlockSpec(memory_space=pltpu.SMEM), block, block]
    if twiddle is None:
        kernel, given = split_kernel, [place, tokens, cotangent]
        planes = 2 * share
    else:
        kernel, given = split_twiddle_kernel, [place, tokens, cotangent, twiddle]
        specs.append(pl.BlockSpec((step, B), lambda t, i: (i, 0)))
        planes = 2 * share + 3
    return pl.pallas_call(
        functools.partial(kernel, rotated=rotated),
        grid=(tiles, rows // step),
        in_specs=specs,
        out_specs=part_specs(devices, rotated, (planes, step, B), lambda t, i: (t, i, 0)),
        out_shape=part_shapes(devices, rotated, (tiles * planes, rows, B)),
        scratch_shapes=[pltpu.VMEM((step * LANES, B), jnp.float32)],
        compiler_params=pltpu.CompilerParams(vmem_limit_bytes=VMEM_BYTES),
        cost_estimate=pl.CostEstimate(flops=1, bytes_accessed=16 * rows * B * LANES * tiles, transcendentals=0),
    )(*given)


def merge_kernel(place_ref, *rest, parts, rotated):
    part_refs, out_ref, swap_ref = views(rest[:parts], rotated), rest[-2], rest[-1]
    share, rows, _ = part_refs[0].shape
    for slot, part_ref in enumerate(part_refs):
        start = (place_ref[0] + slot * share) % LANES if rotated else slot * share
        for channel in range(share):
            at = pl.multiple_of((start + channel) * rows, rows)
            swap_ref[pl.ds(at, rows), :] = part_ref[channel].astype(jnp.float32)
    for row in range(rows):
        out_ref[row] = swap_ref[pl.ds(row, LANES, stride=rows), :].T.astype(jnp.bfloat16)


def merge_channels(place, parts, held, tile, tiles, devices, rotated, width, after):
    rows = parts[0].shape[-2]
    step = min(16, rows)
    share = LANES // devices
    given = [place, *parts]
    specs = [pl.BlockSpec(memory_space=pltpu.SMEM)]
    specs += part_specs(devices, rotated, (share, step, B), lambda t, i: (t, i, 0))
    for array in after if held is None else [held, *after]:
        given.append(array)
        specs.append(pl.BlockSpec(memory_space=pl.ANY))
    return pl.pallas_call(
        functools.partial(merge_kernel, parts=len(parts), rotated=rotated),
        grid=(tiles, rows // step),
        in_specs=specs,
        out_specs=pl.BlockSpec((step, B, LANES), lambda t, i: (i, 0, tile + t)),
        out_shape=jax.ShapeDtypeStruct((rows, B, width), jnp.bfloat16),
        scratch_shapes=[pltpu.VMEM((step * LANES, B), jnp.float32)],
        input_output_aliases={} if held is None else {len(parts) + 1: 0},
        compiler_params=pltpu.CompilerParams(vmem_limit_bytes=VMEM_BYTES),
        cost_estimate=pl.CostEstimate(flops=1, bytes_accessed=8 * rows * B * LANES * tiles, transcendentals=0),
    )(*given)


SECOND_AT = 2 * A
TWIDDLE_AT = SECOND_AT + B
CHANNEL_AT = TWIDDLE_AT + A


def mix_kernel(
    place_ref, gain_ref, bias_ref, skip_ref, *rest, parts, tile, tile_count, rotated
):
    tok_refs = views(rest[:parts], rotated)
    cot_refs = views(rest[parts : 2 * parts], rotated)
    first_ref, first_t_ref, second_ref, second_t_ref, twiddle_ref = rest[2 * parts : 2 * parts + 5]
    out_refs = views(rest[-3 - parts : -3], rotated)
    sums_ref, tok_all, cot_all = rest[-3:]
    t, step = pl.program_id(0), pl.program_id(1)

    @pl.when((t == 0) & (step == 0))
    def _():
        sums_ref[...] = jnp.zeros(sums_ref.shape, jnp.float32)

    devices = len(tok_refs)
    pair, rows, _ = tok_refs[0].shape
    share = LANES // devices
    lane_at = place_ref[0] + step * pair
    at = (tile + t) * LANES + lane_at

    def rows_from(shift):
        if not rotated:
            return slice(shift * rows, (shift + 1) * rows)
        source = (place_ref[0] // share - shift + devices) % devices
        return pl.ds(pl.multiple_of(source * rows, rows), rows)

    for refs, whole in ((tok_refs, tok_all), (cot_refs, cot_all)):
        for shift, ref in enumerate(refs):
            for c in range(pair):
                whole[rows_from(shift), c * B : (c + 1) * B] = ref[c].astype(jnp.float32)

    def spread(ref):
        lane = lax.broadcasted_iota(jnp.int32, (1, pair * B), 1)
        row = jnp.full((1, pair * B), ref[at], jnp.float32)
        for c in range(1, pair):
            row = jnp.where(lane >= c * B, ref[at + c], row)
        return row

    gain, bias, skip = spread(gain_ref), spread(bias_ref), spread(skip_ref)
    inputs = tok_all[...]
    tok = inputs.astype(jnp.bfloat16)
    upstream = cot_all[...]
    twiddle = jnp.concatenate([twiddle_ref[...]] * pair, axis=1)
    inner = dot(tok, second_t_ref[...], 1, 0)
    scaled = (inner * twiddle).astype(jnp.bfloat16)
    gate = jax.nn.sigmoid(gain * inputs + bias)
    grad_hidden = upstream * gate
    grad_outer = grad_hidden.astype(jnp.bfloat16)
    outer = dot(first_ref[...], scaled, 1, 0).astype(jnp.bfloat16).astype(jnp.float32)
    grad_scaled = dot(first_t_ref[...], grad_outer, 1, 0).astype(jnp.bfloat16).astype(jnp.float32)
    first_term = dot(grad_outer, scaled, 1, 1)
    for half in range(A // B):
        sums_ref[half * A : (half + 1) * A] += first_term[:, half * B : (half + 1) * B]
    hidden = outer + skip * inputs
    grad_pre = upstream * hidden * gate * (1.0 - gate)
    product = grad_scaled * inner
    sums_ref[TWIDDLE_AT:CHANNEL_AT] += sum(product[:, c * B : (c + 1) * B] for c in range(pair))
    grad_inner = (grad_scaled * twiddle).astype(jnp.bfloat16)
    second_term = dot(grad_inner, tok, 0, 0)
    sums_ref[SECOND_AT:TWIDDLE_AT] += sum(
        second_term[c * B : (c + 1) * B, c * B : (c + 1) * B] for c in range(pair)
    )
    lane = lax.broadcasted_iota(jnp.int32, (1, LANES), 1)
    for which, value in enumerate((grad_pre * inputs, grad_pre, grad_hidden * inputs)):
        total = jnp.sum(value, axis=0, keepdims=True)
        row = jnp.zeros((1, LANES), jnp.float32)
        for c in range(pair):
            channel = jnp.sum(total[:, c * B : (c + 1) * B], axis=1, keepdims=True)
            row = jnp.where(lane == lane_at + c, channel, row)
        sums_ref[pl.ds(CHANNEL_AT + which * tile_count + tile + t, 1), :] += row
    grad_in = dot(grad_inner, second_ref[...], 1, 0)
    tok_all[...] = grad_in + grad_hidden * skip + grad_pre * gain
    for shift, out_ref in enumerate(out_refs):
        for c in range(pair):
            out_ref[c] = tok_all[rows_from(shift), c * B : (c + 1) * B].astype(jnp.bfloat16)


def mix(parts, tile, tiles, planes, place, vectors, factors, sum_rows, devices, rotated, after):
    rows = parts[0].shape[-2]
    share = LANES // devices
    pair = factors[2].shape[0] // B
    steps = share // pair
    whole = lambda array: pl.BlockSpec(array.shape, lambda t, i: (0,) * array.ndim)
    tok_at = lambda t, i: (t * (planes // pair) + i, 0, 0)
    cot_at = lambda t, i: (t * (planes // pair) + steps + i, 0, 0)
    block = (pair, rows, B)
    tile_count = vectors[0].shape[0] // LANES
    *leaving, sums = pl.pallas_call(
        functools.partial(
            mix_kernel, parts=len(parts), tile=tile, tile_count=tile_count, rotated=rotated
        ),
        grid=(tiles, steps),
        in_specs=[pl.BlockSpec(memory_space=pltpu.SMEM)] * 4
        + part_specs(devices, rotated, block, tok_at)
        + part_specs(devices, rotated, block, cot_at)
        + [whole(f) for f in factors]
        + [pl.BlockSpec(memory_space=pl.ANY)] * len(after),
        out_specs=part_specs(devices, rotated, block, lambda t, i: (t * steps + i, 0, 0))
        + [pl.BlockSpec((sum_rows, LANES), lambda t, i: (0, 0))],
        out_shape=part_shapes(devices, rotated, (tiles * share, rows, B))
        + [jax.ShapeDtypeStruct((sum_rows, LANES), jnp.float32)],
        scratch_shapes=[pltpu.VMEM((A, pair * B), jnp.float32)] * 2,
        compiler_params=pltpu.CompilerParams(vmem_limit_bytes=VMEM_BYTES),
        cost_estimate=pl.CostEstimate(flops=tiles * share * A * B * 16000, bytes_accessed=1024, transcendentals=0),
    )(place, *vectors, *parts, *parts, *factors, *after)
    return leaving, sums


def add_kernel(*refs, count):
    total = refs[0][...]
    for ref in refs[1:count]:
        total += ref[...]
    refs[-1][...] = total


def add(terms, after):
    vmem = pl.BlockSpec(memory_space=pltpu.VMEM)
    return pl.pallas_call(
        functools.partial(add_kernel, count=len(terms)),
        in_specs=[vmem] * len(terms) + [pl.BlockSpec(memory_space=pl.ANY)] * len(after),
        out_specs=vmem,
        out_shape=jax.ShapeDtypeStruct(terms[0].shape, terms[0].dtype),
        cost_estimate=pl.CostEstimate(flops=1, bytes_accessed=1024, transcendentals=0),
    )(*terms, *after)


def hold(arrays, after):
    anywhere = pl.BlockSpec(memory_space=pl.ANY)
    return pl.pallas_call(
        lambda *refs: None,
        in_specs=[anywhere] * (len(arrays) + len(after)),
        out_specs=[anywhere] * len(arrays),
        out_shape=[jax.ShapeDtypeStruct(a.shape, a.dtype) for a in arrays],
        input_output_aliases={i: i for i in range(len(arrays))},
        cost_estimate=pl.CostEstimate(flops=1, bytes_accessed=1024, transcendentals=0),
    )(*arrays, *after)


def block_diagonal(square, count):
    zero = jnp.zeros_like(square)
    return jnp.concatenate(
        [
            jnp.concatenate([square if i == j else zero for j in range(count)], axis=1)
            for i in range(count)
        ],
        axis=0,
    )


def sum_over_mesh(sums):
    dp = lax.axis_index("dp")
    size = lax.axis_size("dp")
    for bit in reversed([1 << k for k in range(size.bit_length() - 1)]):
        halves = sums.reshape(2, -1, LANES)
        high = (dp & bit) != 0
        sent = jnp.where(high, halves[0], halves[1])
        kept = jnp.where(high, halves[1], halves[0])
        sums = kept + lax.ppermute(sent, "dp", [(i, i ^ bit) for i in range(size)])
    sums = jnp.sum(lax.all_gather(sums, "ctx"), axis=0)
    return lax.all_gather(sums, "dp", axis=0, tiled=True)


def body(tokens, cotangent, first_factor, second_factor, twiddle, gate_gain, gate_bias, skip_gain):
    seq_count, tok_rows, width = tokens.shape
    ctx_size = lax.axis_size("ctx")
    dp_size = lax.axis_size("dp")
    share = LANES // ctx_size
    local_rows = tok_rows // B
    tiles = width // LANES
    pair = 2
    groups = [(0, 1, False), (1, tiles - 2, True), (tiles - 1, 1, False)]

    place = (lax.axis_index("ctx") * share).astype(jnp.int32).reshape(1)
    second = block_diagonal(second_factor, pair)
    second_t = block_diagonal(second_factor.T, pair)
    vectors = [gate_gain, gate_bias, skip_gain]
    used_rows = CHANNEL_AT + 3 * tiles
    sum_rows = -(-used_rows // (8 * dp_size)) * 8 * dp_size

    def exchange(parts, sign, rotated):
        if not rotated:
            return [lax.all_to_all(parts[0], "ctx", split_axis=0, concat_axis=0, tiled=True)]
        moved = [parts[0]]
        for shift in range(1, ctx_size):
            pairs = [(i, (i + sign * shift) % ctx_size) for i in range(ctx_size)]
            moved.append(lax.ppermute(parts[shift], "ctx", pairs))
        return moved

    terms = []
    leaving = []
    for seq in range(seq_count):
        tok_blocks = tokens[seq].reshape(local_rows, B, width)
        cot_blocks = cotangent[seq].reshape(local_rows, B, width)
        split = []
        for at, count, rotated in groups:
            own = twiddle if at == 0 else None
            split.append(
                split_channels(place, tok_blocks, cot_blocks, at, count, ctx_size, rotated, own)
            )
        arrived = [exchange(split[0], 1, False), exchange(split[1], 1, True)]
        planes = arrived[0][0][:, 2 * share :].astype(jnp.float32)
        twiddle_all = (planes[:, 0] + planes[:, 1] + planes[:, 2]).reshape(A, B)
        factors = [first_factor, first_factor.T, second, second_t, twiddle_all]
        returned = []
        for which, (at, count, rotated) in enumerate(groups):
            if which == 2:
                parts = hold(split[2], returned[0] + arrived[1][1:])
                arrived.append(exchange(parts, 1, rotated))
            parts, own_sums = mix(
                arrived[which], at, count, 2 * share, place, vectors, factors, sum_rows, ctx_size,
                rotated, [],
            )
            returned.append(exchange(parts, -1, rotated))
            terms.append(own_sums)
        leaving.append(returned)

    begun = [part for returned in leaving for part in returned[1][1:RETURN_FIRST]]
    sums = sum_over_mesh(add(terms, begun))
    grads = []
    for returned in leaving:
        held = None
        for which, (at, count, rotated) in enumerate(groups):
            after = [sums] if which == 2 else []
            held = merge_channels(
                place, returned[which], held, at, count, ctx_size, rotated, width, after
            )
        grads.append(held.reshape(tok_rows, width))
    grad_tokens = jnp.stack(grads)

    total_seqs = seq_count * dp_size
    first_norm = math.sqrt(total_seqs * B * width)
    second_norm = math.sqrt(total_seqs * A * width)
    twiddle_norm = math.sqrt(total_seqs * width)
    channel_norm = math.sqrt(total_seqs * A * B)
    first_sum = jnp.concatenate([sums[half * A : (half + 1) * A] for half in range(A // B)], axis=1)
    mine = TWIDDLE_AT + lax.axis_index("ctx") * local_rows
    twiddle_sum = lax.dynamic_slice_in_dim(sums, mine, local_rows, 0)
    channel_sum = sums[CHANNEL_AT:used_rows].reshape(3, width)
    return (
        grad_tokens,
        first_sum / first_norm,
        sums[SECOND_AT:TWIDDLE_AT] / second_norm,
        twiddle_sum / twiddle_norm,
        channel_sum[0] / channel_norm,
        channel_sum[1] / channel_norm,
        channel_sum[2] / channel_norm,
    )


def solution(mesh):
    return jax.shard_map(
        body,
        mesh=mesh,
        in_specs=(
            P("dp", "ctx", None),
            P("dp", "ctx", None),
            P(),
            P(),
            P("ctx", None),
            P(),
            P(),
            P(),
        ),
        out_specs=(P("dp", "ctx", None), P(), P(), P("ctx", None), P(), P(), P()),
        check_vma=False,
    )
```

```python
import functools
import math

import jax
import jax.numpy as jnp
from jax import lax
from jax.experimental import pallas as pl
from jax.experimental.pallas import tpu as pltpu
from jax.sharding import PartitionSpec as P

A = 256
B = 128
LANES = 128
VMEM_BYTES = 48 * 1024 * 1024


def dot(left, right, left_dim, right_dim):
    return lax.dot_general(
        left, right, (((left_dim,), (right_dim,)), ((), ())), preferred_element_type=jnp.float32
    )


def views(refs, rotated):
    return list(refs) if rotated else [refs[0].at[i] for i in range(refs[0].shape[0])]


def split_tile(first_channel, tok_ref, cot_ref, out_refs, swap_ref):
    rows = tok_ref.shape[0]
    share = LANES // len(out_refs)
    for which, ref in enumerate((tok_ref, cot_ref)):
        for row in range(rows):
            swap_ref[row * LANES : (row + 1) * LANES, :] = ref[row].astype(jnp.float32).T
        for slot, out_ref in enumerate(out_refs):
            start = (first_channel + slot * share) % LANES
            for channel in range(share):
                out_ref[which * share + channel] = swap_ref[
                    pl.ds(start + channel, rows, stride=LANES), :
                ].astype(jnp.bfloat16)


def split_kernel(place_ref, tok_ref, cot_ref, *rest, rotated):
    first_channel = place_ref[0] if rotated else 0
    split_tile(first_channel, tok_ref, cot_ref, views(rest[:-1], rotated), rest[-1])


def split_twiddle_kernel(place_ref, tok_ref, cot_ref, twiddle_ref, *rest, rotated):
    split_kernel(place_ref, tok_ref, cot_ref, *rest, rotated=rotated)
    out_refs = views(rest[:-1], rotated)
    share = LANES // len(out_refs)
    left = twiddle_ref[...]
    for plane in range(3):
        part = left.astype(jnp.bfloat16)
        left = left - part.astype(jnp.float32)
        for out_ref in out_refs:
            out_ref[2 * share + plane] = part


def part_specs(devices, rotated, block, index):
    if rotated:
        return [pl.BlockSpec(block, index)] * devices
    return [pl.BlockSpec((devices, *block), lambda *at: (0, *index(*at)))]


def part_shapes(devices, rotated, shape):
    if rotated:
        return [jax.ShapeDtypeStruct(shape, jnp.bfloat16)] * devices
    return [jax.ShapeDtypeStruct((devices, *shape), jnp.bfloat16)]


def split_channels(place, tokens, cotangent, tile, tiles, devices, rotated, twiddle=None):
    rows = tokens.shape[0]
    step = min(16, rows)
    share = LANES // devices
    block = pl.BlockSpec((step, B, LANES), lambda t, i: (i, 0, tile + t))
    specs = [pl.BlockSpec(memory_space=pltpu.SMEM), block, block]
    if twiddle is None:
        kernel, given = split_kernel, [place, tokens, cotangent]
        planes = 2 * share
    else:
        kernel, given = split_twiddle_kernel, [place, tokens, cotangent, twiddle]
        specs.append(pl.BlockSpec((step, B), lambda t, i: (i, 0)))
        planes = 2 * share + 3
    return pl.pallas_call(
        functools.partial(kernel, rotated=rotated),
        grid=(tiles, rows // step),
        in_specs=specs,
        out_specs=part_specs(devices, rotated, (planes, step, B), lambda t, i: (t, i, 0)),
        out_shape=part_shapes(devices, rotated, (tiles * planes, rows, B)),
        scratch_shapes=[pltpu.VMEM((step * LANES, B), jnp.float32)],
        compiler_params=pltpu.CompilerParams(vmem_limit_bytes=VMEM_BYTES),
        cost_estimate=pl.CostEstimate(flops=1, bytes_accessed=16 * rows * B * LANES * tiles, transcendentals=0),
    )(*given)


def merge_kernel(place_ref, *rest, parts, rotated):
    part_refs, out_ref, swap_ref = views(rest[:parts], rotated), rest[-2], rest[-1]
    share, rows, _ = part_refs[0].shape
    for slot, part_ref in enumerate(part_refs):
        start = (place_ref[0] + slot * share) % LANES if rotated else slot * share
        for channel in range(share):
            at = pl.multiple_of((start + channel) * rows, rows)
            swap_ref[pl.ds(at, rows), :] = part_ref[channel].astype(jnp.float32)
    for row in range(rows):
        out_ref[row] = swap_ref[pl.ds(row, LANES, stride=rows), :].T.astype(jnp.bfloat16)


def merge_channels(place, parts, held, tile, tiles, devices, rotated, width, after):
    rows = parts[0].shape[-2]
    step = min(16, rows)
    share = LANES // devices
    given = [place, *parts]
    specs = [pl.BlockSpec(memory_space=pltpu.SMEM)]
    specs += part_specs(devices, rotated, (share, step, B), lambda t, i: (t, i, 0))
    for array in after if held is None else [held, *after]:
        given.append(array)
        specs.append(pl.BlockSpec(memory_space=pl.ANY))
    return pl.pallas_call(
        functools.partial(merge_kernel, parts=len(parts), rotated=rotated),
        grid=(tiles, rows // step),
        in_specs=specs,
        out_specs=pl.BlockSpec((step, B, LANES), lambda t, i: (i, 0, tile + t)),
        out_shape=jax.ShapeDtypeStruct((rows, B, width), jnp.bfloat16),
        scratch_shapes=[pltpu.VMEM((step * LANES, B), jnp.float32)],
        input_output_aliases={} if held is None else {len(parts) + 1: 0},
        compiler_params=pltpu.CompilerParams(vmem_limit_bytes=VMEM_BYTES),
        cost_estimate=pl.CostEstimate(flops=1, bytes_accessed=8 * rows * B * LANES * tiles, transcendentals=0),
    )(*given)


SECOND_AT = 2 * A
TWIDDLE_AT = SECOND_AT + B
CHANNEL_AT = TWIDDLE_AT + A


def mix_kernel(
    place_ref, gain_ref, bias_ref, skip_ref, *rest, parts, tile, tile_count, rotated
):
    tok_refs = views(rest[:parts], rotated)
    cot_refs = views(rest[parts : 2 * parts], rotated)
    first_ref, first_t_ref, second_ref, second_t_ref, twiddle_ref = rest[2 * parts : 2 * parts + 5]
    out_refs = views(rest[-3 - parts : -3], rotated)
    sums_ref, tok_all, cot_all = rest[-3:]
    t, step = pl.program_id(0), pl.program_id(1)

    @pl.when((t == 0) & (step == 0))
    def _():
        sums_ref[...] = jnp.zeros(sums_ref.shape, jnp.float32)

    devices = len(tok_refs)
    pair, rows, _ = tok_refs[0].shape
    share = LANES // devices
    lane_at = place_ref[0] + step * pair
    at = (tile + t) * LANES + lane_at

    def rows_from(shift):
        if not rotated:
            return slice(shift * rows, (shift + 1) * rows)
        source = (place_ref[0] // share - shift + devices) % devices
        return pl.ds(pl.multiple_of(source * rows, rows), rows)

    for refs, whole in ((tok_refs, tok_all), (cot_refs, cot_all)):
        for shift, ref in enumerate(refs):
            for c in range(pair):
                whole[rows_from(shift), c * B : (c + 1) * B] = ref[c].astype(jnp.float32)

    def spread(ref):
        lane = lax.broadcasted_iota(jnp.int32, (1, pair * B), 1)
        row = jnp.full((1, pair * B), ref[at], jnp.float32)
        for c in range(1, pair):
            row = jnp.where(lane >= c * B, ref[at + c], row)
        return row

    gain, bias, skip = spread(gain_ref), spread(bias_ref), spread(skip_ref)
    inputs = tok_all[...]
    tok = inputs.astype(jnp.bfloat16)
    upstream = cot_all[...]
    twiddle = jnp.concatenate([twiddle_ref[...]] * pair, axis=1)
    inner = dot(tok, second_t_ref[...], 1, 0)
    scaled = (inner * twiddle).astype(jnp.bfloat16)
    gate = jax.nn.sigmoid(gain * inputs + bias)
    grad_hidden = upstream * gate
    grad_outer = grad_hidden.astype(jnp.bfloat16)
    outer = dot(first_ref[...], scaled, 1, 0).astype(jnp.bfloat16).astype(jnp.float32)
    grad_scaled = dot(first_t_ref[...], grad_outer, 1, 0).astype(jnp.bfloat16).astype(jnp.float32)
    first_term = dot(grad_outer, scaled, 1, 1)
    for half in range(A // B):
        sums_ref[half * A : (half + 1) * A] += first_term[:, half * B : (half + 1) * B]
    hidden = outer + skip * inputs
    grad_pre = upstream * hidden * gate * (1.0 - gate)
    product = grad_scaled * inner
    sums_ref[TWIDDLE_AT:CHANNEL_AT] += sum(product[:, c * B : (c + 1) * B] for c in range(pair))
    grad_inner = (grad_scaled * twiddle).astype(jnp.bfloat16)
    second_term = dot(grad_inner, tok, 0, 0)
    sums_ref[SECOND_AT:TWIDDLE_AT] += sum(
        second_term[c * B : (c + 1) * B, c * B : (c + 1) * B] for c in range(pair)
    )
    lane = lax.broadcasted_iota(jnp.int32, (1, LANES), 1)
    for which, value in enumerate((grad_pre * inputs, grad_pre, grad_hidden * inputs)):
        total = jnp.sum(value, axis=0, keepdims=True)
        row = jnp.zeros((1, LANES), jnp.float32)
        for c in range(pair):
            channel = jnp.sum(total[:, c * B : (c + 1) * B], axis=1, keepdims=True)
            row = jnp.where(lane == lane_at + c, channel, row)
        sums_ref[pl.ds(CHANNEL_AT + which * tile_count + tile + t, 1), :] += row
    grad_in = dot(grad_inner, second_ref[...], 1, 0)
    tok_all[...] = grad_in + grad_hidden * skip + grad_pre * gain
    for shift, out_ref in enumerate(out_refs):
        for c in range(pair):
            out_ref[c] = tok_all[rows_from(shift), c * B : (c + 1) * B].astype(jnp.bfloat16)


def mix(parts, tile, tiles, planes, place, vectors, factors, sum_rows, devices, rotated, after):
    rows = parts[0].shape[-2]
    share = LANES // devices
    pair = factors[2].shape[0] // B
    steps = share // pair
    whole = lambda array: pl.BlockSpec(array.shape, lambda t, i: (0,) * array.ndim)
    tok_at = lambda t, i: (t * (planes // pair) + i, 0, 0)
    cot_at = lambda t, i: (t * (planes // pair) + steps + i, 0, 0)
    block = (pair, rows, B)
    tile_count = vectors[0].shape[0] // LANES
    *leaving, sums = pl.pallas_call(
        functools.partial(
            mix_kernel, parts=len(parts), tile=tile, tile_count=tile_count, rotated=rotated
        ),
        grid=(tiles, steps),
        in_specs=[pl.BlockSpec(memory_space=pltpu.SMEM)] * 4
        + part_specs(devices, rotated, block, tok_at)
        + part_specs(devices, rotated, block, cot_at)
        + [whole(f) for f in factors]
        + [pl.BlockSpec(memory_space=pl.ANY)] * len(after),
        out_specs=part_specs(devices, rotated, block, lambda t, i: (t * steps + i, 0, 0))
        + [pl.BlockSpec((sum_rows, LANES), lambda t, i: (0, 0))],
        out_shape=part_shapes(devices, rotated, (tiles * share, rows, B))
        + [jax.ShapeDtypeStruct((sum_rows, LANES), jnp.float32)],
        scratch_shapes=[pltpu.VMEM((A, pair * B), jnp.float32)] * 2,
        compiler_params=pltpu.CompilerParams(vmem_limit_bytes=VMEM_BYTES),
        cost_estimate=pl.CostEstimate(flops=tiles * share * A * B * 16000, bytes_accessed=1024, transcendentals=0),
    )(place, *vectors, *parts, *parts, *factors, *after)
    return leaving, sums


def add_kernel(*refs, count):
    total = refs[0][...]
    for ref in refs[1:count]:
        total += ref[...]
    refs[-1][...] = total


def add(terms, after):
    vmem = pl.BlockSpec(memory_space=pltpu.VMEM)
    return pl.pallas_call(
        functools.partial(add_kernel, count=len(terms)),
        in_specs=[vmem] * len(terms) + [pl.BlockSpec(memory_space=pl.ANY)] * len(after),
        out_specs=vmem,
        out_shape=jax.ShapeDtypeStruct(terms[0].shape, terms[0].dtype),
        cost_estimate=pl.CostEstimate(flops=1, bytes_accessed=1024, transcendentals=0),
    )(*terms, *after)


def hold(arrays, after):
    anywhere = pl.BlockSpec(memory_space=pl.ANY)
    return pl.pallas_call(
        lambda *refs: None,
        in_specs=[anywhere] * (len(arrays) + len(after)),
        out_specs=[anywhere] * len(arrays),
        out_shape=[jax.ShapeDtypeStruct(a.shape, a.dtype) for a in arrays],
        input_output_aliases={i: i for i in range(len(arrays))},
        cost_estimate=pl.CostEstimate(flops=1, bytes_accessed=1024, transcendentals=0),
    )(*arrays, *after)


def block_diagonal(square, count):
    zero = jnp.zeros_like(square)
    return jnp.concatenate(
        [
            jnp.concatenate([square if i == j else zero for j in range(count)], axis=1)
            for i in range(count)
        ],
        axis=0,
    )


def sum_over_mesh(sums, after):
    dp = lax.axis_index("dp")
    size = lax.axis_size("dp")
    for bit in reversed([1 << k for k in range(size.bit_length() - 1)]):
        halves = sums.reshape(2, -1, LANES)
        high = (dp & bit) != 0
        sent = jnp.where(high, halves[0], halves[1])
        kept = jnp.where(high, halves[1], halves[0])
        sums = kept + lax.ppermute(sent, "dp", [(i, i ^ bit) for i in range(size)])
    (sums,) = hold([sums], after)
    sums = jnp.sum(lax.all_gather(sums, "ctx"), axis=0)
    return lax.all_gather(sums, "dp", axis=0, tiled=True)


def body(tokens, cotangent, first_factor, second_factor, twiddle, gate_gain, gate_bias, skip_gain):
    seq_count, tok_rows, width = tokens.shape
    ctx_size = lax.axis_size("ctx")
    dp_size = lax.axis_size("dp")
    share = LANES // ctx_size
    local_rows = tok_rows // B
    tiles = width // LANES
    pair = 2
    half = tiles // 2
    groups = [(0, 1, False), (half, tiles - half, True), (1, half - 1, False)]

    place = (lax.axis_index("ctx") * share).astype(jnp.int32).reshape(1)
    second = block_diagonal(second_factor, pair)
    second_t = block_diagonal(second_factor.T, pair)
    vectors = [gate_gain, gate_bias, skip_gain]
    used_rows = CHANNEL_AT + 3 * tiles
    sum_rows = -(-used_rows // (8 * dp_size)) * 8 * dp_size

    def exchange(parts, sign, rotated):
        if not rotated:
            return [lax.all_to_all(parts[0], "ctx", split_axis=0, concat_axis=0, tiled=True)]
        moved = [parts[0]]
        for shift in range(1, ctx_size):
            pairs = [(i, (i + sign * shift) % ctx_size) for i in range(ctx_size)]
            moved.append(lax.ppermute(parts[shift], "ctx", pairs))
        return moved

    terms = []
    leaving = []
    for seq in range(seq_count):
        tok_blocks = tokens[seq].reshape(local_rows, B, width)
        cot_blocks = cotangent[seq].reshape(local_rows, B, width)
        split = []
        for at, count, rotated in groups:
            own = twiddle if at == 0 else None
            split.append(
                split_channels(place, tok_blocks, cot_blocks, at, count, ctx_size, rotated, own)
            )
        arrived = [exchange(p, 1, group[2]) for p, group in zip(split, groups)]
        planes = arrived[0][0][:, 2 * share :].astype(jnp.float32)
        twiddle_all = (planes[:, 0] + planes[:, 1] + planes[:, 2]).reshape(A, B)
        factors = [first_factor, first_factor.T, second, second_t, twiddle_all]
        returned = []
        for which, (at, count, rotated) in enumerate(groups):
            parts, own_sums = mix(
                arrived[which], at, count, 2 * share, place, vectors, factors, sum_rows, ctx_size,
                rotated, [],
            )
            if which == 2:
                parts = hold(parts, arrived[1][1:])
            returned.append(exchange(parts, -1, rotated))
            terms.append(own_sums)
        leaving.append(returned)

    sums = sum_over_mesh(add(terms, []), [part for r in leaving for part in r[1][-2:]])
    grads = []
    for returned in leaving:
        held = None
        for which in (0, 2, 1):
            at, count, rotated = groups[which]
            after = [sums] if which else []
            held = merge_channels(
                place, returned[which], held, at, count, ctx_size, rotated, width, after
            )
        grads.append(held.reshape(tok_rows, width))
    grad_tokens = jnp.stack(grads)

    total_seqs = seq_count * dp_size
    first_norm = math.sqrt(total_seqs * B * width)
    second_norm = math.sqrt(total_seqs * A * width)
    twiddle_norm = math.sqrt(total_seqs * width)
    channel_norm = math.sqrt(total_seqs * A * B)
    first_sum = jnp.concatenate([sums[half * A : (half + 1) * A] for half in range(A // B)], axis=1)
    mine = TWIDDLE_AT + lax.axis_index("ctx") * local_rows
    twiddle_sum = lax.dynamic_slice_in_dim(sums, mine, local_rows, 0)
    channel_sum = sums[CHANNEL_AT:used_rows].reshape(3, width)
    return (
        grad_tokens,
        first_sum / first_norm,
        sums[SECOND_AT:TWIDDLE_AT] / second_norm,
        twiddle_sum / twiddle_norm,
        channel_sum[0] / channel_norm,
        channel_sum[1] / channel_norm,
        channel_sum[2] / channel_norm,
    )


def solution(mesh):
    return jax.shard_map(
        body,
        mesh=mesh,
        in_specs=(
            P("dp", "ctx", None),
            P("dp", "ctx", None),
            P(),
            P(),
            P("ctx", None),
            P(),
            P(),
            P(),
        ),
        out_specs=(P("dp", "ctx", None), P(), P(), P("ctx", None), P(), P(), P()),
        check_vma=False,
    )
```

```python
import functools
import math

import jax
import jax.numpy as jnp
from jax import lax
from jax.experimental import pallas as pl
from jax.experimental.pallas import tpu as pltpu
from jax.sharding import PartitionSpec as P

A = 256
B = 128
LANES = 128
VMEM_BYTES = 48 * 1024 * 1024


def dot(left, right, left_dim, right_dim):
    return lax.dot_general(
        left, right, (((left_dim,), (right_dim,)), ((), ())), preferred_element_type=jnp.float32
    )


def views(refs, rotated):
    return list(refs) if rotated else [refs[0].at[i] for i in range(refs[0].shape[0])]


def split_tile(first_channel, tok_ref, cot_ref, out_refs, swap_ref):
    rows = tok_ref.shape[0]
    share = LANES // len(out_refs)
    for which, ref in enumerate((tok_ref, cot_ref)):
        for row in range(rows):
            swap_ref[row * LANES : (row + 1) * LANES, :] = ref[row].astype(jnp.float32).T
        for slot, out_ref in enumerate(out_refs):
            start = (first_channel + slot * share) % LANES
            for channel in range(share):
                out_ref[which * share + channel] = swap_ref[
                    pl.ds(start + channel, rows, stride=LANES), :
                ].astype(jnp.bfloat16)


def split_kernel(place_ref, tok_ref, cot_ref, *rest, rotated):
    first_channel = place_ref[0] if rotated else 0
    split_tile(first_channel, tok_ref, cot_ref, views(rest[:-1], rotated), rest[-1])


def split_twiddle_kernel(place_ref, tok_ref, cot_ref, twiddle_ref, *rest, rotated):
    split_kernel(place_ref, tok_ref, cot_ref, *rest, rotated=rotated)
    out_refs = views(rest[:-1], rotated)
    share = LANES // len(out_refs)
    left = twiddle_ref[...]
    for plane in range(3):
        part = left.astype(jnp.bfloat16)
        left = left - part.astype(jnp.float32)
        for out_ref in out_refs:
            out_ref[2 * share + plane] = part


def part_specs(devices, rotated, block, index):
    if rotated:
        return [pl.BlockSpec(block, index)] * devices
    return [pl.BlockSpec((devices, *block), lambda *at: (0, *index(*at)))]


def part_shapes(devices, rotated, shape):
    if rotated:
        return [jax.ShapeDtypeStruct(shape, jnp.bfloat16)] * devices
    return [jax.ShapeDtypeStruct((devices, *shape), jnp.bfloat16)]


def split_channels(place, tokens, cotangent, tile, tiles, devices, rotated, twiddle=None):
    rows = tokens.shape[0]
    step = min(16, rows)
    share = LANES // devices
    block = pl.BlockSpec((step, B, LANES), lambda t, i: (i, 0, tile + t))
    specs = [pl.BlockSpec(memory_space=pltpu.SMEM), block, block]
    if twiddle is None:
        kernel, given = split_kernel, [place, tokens, cotangent]
        planes = 2 * share
    else:
        kernel, given = split_twiddle_kernel, [place, tokens, cotangent, twiddle]
        specs.append(pl.BlockSpec((step, B), lambda t, i: (i, 0)))
        planes = 2 * share + 3
    return pl.pallas_call(
        functools.partial(kernel, rotated=rotated),
        grid=(tiles, rows // step),
        in_specs=specs,
        out_specs=part_specs(devices, rotated, (planes, step, B), lambda t, i: (t, i, 0)),
        out_shape=part_shapes(devices, rotated, (tiles * planes, rows, B)),
        scratch_shapes=[pltpu.VMEM((step * LANES, B), jnp.float32)],
        compiler_params=pltpu.CompilerParams(vmem_limit_bytes=VMEM_BYTES),
        cost_estimate=pl.CostEstimate(flops=1, bytes_accessed=16 * rows * B * LANES * tiles, transcendentals=0),
    )(*given)


def merge_kernel(place_ref, *rest, parts, rotated):
    part_refs, out_ref, swap_ref = views(rest[:parts], rotated), rest[-2], rest[-1]
    share, rows, _ = part_refs[0].shape
    for slot, part_ref in enumerate(part_refs):
        start = (place_ref[0] + slot * share) % LANES if rotated else slot * share
        for channel in range(share):
            at = pl.multiple_of((start + channel) * rows, rows)
            swap_ref[pl.ds(at, rows), :] = part_ref[channel].astype(jnp.float32)
    for row in range(rows):
        out_ref[row] = swap_ref[pl.ds(row, LANES, stride=rows), :].T.astype(jnp.bfloat16)


def merge_channels(place, parts, held, tile, tiles, devices, rotated, width, after):
    rows = parts[0].shape[-2]
    step = min(16, rows)
    share = LANES // devices
    given = [place, *parts]
    specs = [pl.BlockSpec(memory_space=pltpu.SMEM)]
    specs += part_specs(devices, rotated, (share, step, B), lambda t, i: (t, i, 0))
    for array in after if held is None else [held, *after]:
        given.append(array)
        specs.append(pl.BlockSpec(memory_space=pl.ANY))
    return pl.pallas_call(
        functools.partial(merge_kernel, parts=len(parts), rotated=rotated),
        grid=(tiles, rows // step),
        in_specs=specs,
        out_specs=pl.BlockSpec((step, B, LANES), lambda t, i: (i, 0, tile + t)),
        out_shape=jax.ShapeDtypeStruct((rows, B, width), jnp.bfloat16),
        scratch_shapes=[pltpu.VMEM((step * LANES, B), jnp.float32)],
        input_output_aliases={} if held is None else {len(parts) + 1: 0},
        compiler_params=pltpu.CompilerParams(vmem_limit_bytes=VMEM_BYTES),
        cost_estimate=pl.CostEstimate(flops=1, bytes_accessed=8 * rows * B * LANES * tiles, transcendentals=0),
    )(*given)


SECOND_AT = 2 * A
TWIDDLE_AT = SECOND_AT + B
CHANNEL_AT = TWIDDLE_AT + A


def mix_kernel(
    place_ref, gain_ref, bias_ref, skip_ref, *rest, parts, tile, tile_count, rotated
):
    tok_refs = views(rest[:parts], rotated)
    cot_refs = views(rest[parts : 2 * parts], rotated)
    first_ref, first_t_ref, second_ref, second_t_ref, twiddle_ref = rest[2 * parts : 2 * parts + 5]
    out_refs = views(rest[-3 - parts : -3], rotated)
    sums_ref, tok_all, cot_all = rest[-3:]
    t, step = pl.program_id(0), pl.program_id(1)

    @pl.when((t == 0) & (step == 0))
    def _():
        sums_ref[...] = jnp.zeros(sums_ref.shape, jnp.float32)

    devices = len(tok_refs)
    pair, rows, _ = tok_refs[0].shape
    share = LANES // devices
    lane_at = place_ref[0] + step * pair
    at = (tile + t) * LANES + lane_at

    def rows_from(shift):
        if not rotated:
            return slice(shift * rows, (shift + 1) * rows)
        source = (place_ref[0] // share - shift + devices) % devices
        return pl.ds(pl.multiple_of(source * rows, rows), rows)

    for refs, whole in ((tok_refs, tok_all), (cot_refs, cot_all)):
        for shift, ref in enumerate(refs):
            for c in range(pair):
                whole[rows_from(shift), c * B : (c + 1) * B] = ref[c].astype(jnp.float32)

    def spread(ref):
        lane = lax.broadcasted_iota(jnp.int32, (1, pair * B), 1)
        row = jnp.full((1, pair * B), ref[at], jnp.float32)
        for c in range(1, pair):
            row = jnp.where(lane >= c * B, ref[at + c], row)
        return row

    gain, bias, skip = spread(gain_ref), spread(bias_ref), spread(skip_ref)
    inputs = tok_all[...]
    tok = inputs.astype(jnp.bfloat16)
    upstream = cot_all[...]
    twiddle = jnp.concatenate([twiddle_ref[...]] * pair, axis=1)
    inner = dot(tok, second_t_ref[...], 1, 0)
    scaled = (inner * twiddle).astype(jnp.bfloat16)
    gate = jax.nn.sigmoid(gain * inputs + bias)
    grad_hidden = upstream * gate
    grad_outer = grad_hidden.astype(jnp.bfloat16)
    outer = dot(first_ref[...], scaled, 1, 0).astype(jnp.bfloat16).astype(jnp.float32)
    grad_scaled = dot(first_t_ref[...], grad_outer, 1, 0).astype(jnp.bfloat16).astype(jnp.float32)
    first_term = dot(grad_outer, scaled, 1, 1)
    for half in range(A // B):
        sums_ref[half * A : (half + 1) * A] += first_term[:, half * B : (half + 1) * B]
    hidden = outer + skip * inputs
    grad_pre = upstream * hidden * gate * (1.0 - gate)
    product = grad_scaled * inner
    sums_ref[TWIDDLE_AT:CHANNEL_AT] += sum(product[:, c * B : (c + 1) * B] for c in range(pair))
    grad_inner = (grad_scaled * twiddle).astype(jnp.bfloat16)
    second_term = dot(grad_inner, tok, 0, 0)
    sums_ref[SECOND_AT:TWIDDLE_AT] += sum(
        second_term[c * B : (c + 1) * B, c * B : (c + 1) * B] for c in range(pair)
    )
    lane = lax.broadcasted_iota(jnp.int32, (1, LANES), 1)
    for which, value in enumerate((grad_pre * inputs, grad_pre, grad_hidden * inputs)):
        total = jnp.sum(value, axis=0, keepdims=True)
        row = jnp.zeros((1, LANES), jnp.float32)
        for c in range(pair):
            channel = jnp.sum(total[:, c * B : (c + 1) * B], axis=1, keepdims=True)
            row = jnp.where(lane == lane_at + c, channel, row)
        sums_ref[pl.ds(CHANNEL_AT + which * tile_count + tile + t, 1), :] += row
    grad_in = dot(grad_inner, second_ref[...], 1, 0)
    tok_all[...] = grad_in + grad_hidden * skip + grad_pre * gain
    for shift, out_ref in enumerate(out_refs):
        for c in range(pair):
            out_ref[c] = tok_all[rows_from(shift), c * B : (c + 1) * B].astype(jnp.bfloat16)


def mix(parts, tile, tiles, planes, place, vectors, factors, sum_rows, devices, rotated, after):
    rows = parts[0].shape[-2]
    share = LANES // devices
    pair = factors[2].shape[0] // B
    steps = share // pair
    whole = lambda array: pl.BlockSpec(array.shape, lambda t, i: (0,) * array.ndim)
    tok_at = lambda t, i: (t * (planes // pair) + i, 0, 0)
    cot_at = lambda t, i: (t * (planes // pair) + steps + i, 0, 0)
    block = (pair, rows, B)
    tile_count = vectors[0].shape[0] // LANES
    *leaving, sums = pl.pallas_call(
        functools.partial(
            mix_kernel, parts=len(parts), tile=tile, tile_count=tile_count, rotated=rotated
        ),
        grid=(tiles, steps),
        in_specs=[pl.BlockSpec(memory_space=pltpu.SMEM)] * 4
        + part_specs(devices, rotated, block, tok_at)
        + part_specs(devices, rotated, block, cot_at)
        + [whole(f) for f in factors]
        + [pl.BlockSpec(memory_space=pl.ANY)] * len(after),
        out_specs=part_specs(devices, rotated, block, lambda t, i: (t * steps + i, 0, 0))
        + [pl.BlockSpec((sum_rows, LANES), lambda t, i: (0, 0))],
        out_shape=part_shapes(devices, rotated, (tiles * share, rows, B))
        + [jax.ShapeDtypeStruct((sum_rows, LANES), jnp.float32)],
        scratch_shapes=[pltpu.VMEM((A, pair * B), jnp.float32)] * 2,
        compiler_params=pltpu.CompilerParams(vmem_limit_bytes=VMEM_BYTES),
        cost_estimate=pl.CostEstimate(flops=tiles * share * A * B * 16000, bytes_accessed=1024, transcendentals=0),
    )(place, *vectors, *parts, *parts, *factors, *after)
    return leaving, sums


def add_kernel(*refs, count):
    total = refs[0][...]
    for ref in refs[1:count]:
        total += ref[...]
    refs[-1][...] = total


def add(terms, after):
    vmem = pl.BlockSpec(memory_space=pltpu.VMEM)
    return pl.pallas_call(
        functools.partial(add_kernel, count=len(terms)),
        in_specs=[vmem] * len(terms) + [pl.BlockSpec(memory_space=pl.ANY)] * len(after),
        out_specs=vmem,
        out_shape=jax.ShapeDtypeStruct(terms[0].shape, terms[0].dtype),
        cost_estimate=pl.CostEstimate(flops=1, bytes_accessed=1024, transcendentals=0),
    )(*terms, *after)


def hold(arrays, after):
    anywhere = pl.BlockSpec(memory_space=pl.ANY)
    return pl.pallas_call(
        lambda *refs: None,
        in_specs=[anywhere] * (len(arrays) + len(after)),
        out_specs=[anywhere] * len(arrays),
        out_shape=[jax.ShapeDtypeStruct(a.shape, a.dtype) for a in arrays],
        input_output_aliases={i: i for i in range(len(arrays))},
        cost_estimate=pl.CostEstimate(flops=1, bytes_accessed=1024, transcendentals=0),
    )(*arrays, *after)


def block_diagonal(square, count):
    zero = jnp.zeros_like(square)
    return jnp.concatenate(
        [
            jnp.concatenate([square if i == j else zero for j in range(count)], axis=1)
            for i in range(count)
        ],
        axis=0,
    )


def sum_over_mesh(sums, after):
    size = lax.axis_size("dp")
    dp = lax.axis_index("dp")
    bits = [1 << k for k in range(size.bit_length() - 1)]

    def exchange_with(array, bit):
        return lax.ppermute(array, "dp", [(i, i ^ bit) for i in range(size)])

    for bit in reversed(bits):
        halves = sums.reshape(2, -1, LANES)
        high = (dp & bit) != 0
        other = exchange_with(jnp.where(high, halves[0], halves[1]), bit)
        sums = jnp.where(high, halves[1], halves[0]) + other
    (sums,) = hold([sums], after)
    sums = own = jnp.sum(lax.all_gather(sums, "ctx"), axis=0)
    for bit in bits:
        other = exchange_with(sums, bit)
        high = (dp & bit) != 0
        sums = jnp.concatenate([jnp.where(high, other, sums), jnp.where(high, sums, other)])
    return sums, own


def body(tokens, cotangent, first_factor, second_factor, twiddle, gate_gain, gate_bias, skip_gain):
    seq_count, tok_rows, width = tokens.shape
    ctx_size = lax.axis_size("ctx")
    dp_size = lax.axis_size("dp")
    share = LANES // ctx_size
    local_rows = tok_rows // B
    tiles = width // LANES
    pair = 2
    half = tiles // 2
    groups = [(0, 1, True), (1, half - 1, False), (half, tiles - half, True)]

    place = (lax.axis_index("ctx") * share).astype(jnp.int32).reshape(1)
    second = block_diagonal(second_factor, pair)
    second_t = block_diagonal(second_factor.T, pair)
    vectors = [gate_gain, gate_bias, skip_gain]
    used_rows = CHANNEL_AT + 3 * tiles
    sum_rows = -(-used_rows // (8 * dp_size)) * 8 * dp_size

    def exchange(parts, sign, rotated):
        if not rotated:
            return [lax.all_to_all(parts[0], "ctx", split_axis=0, concat_axis=0, tiled=True)]
        moved = [parts[0]]
        for shift in range(1, ctx_size):
            pairs = [(i, (i + sign * shift) % ctx_size) for i in range(ctx_size)]
            moved.append(lax.ppermute(parts[shift], "ctx", pairs))
        return moved

    terms = []
    leaving = []
    for seq in range(seq_count):
        tok_blocks = tokens[seq].reshape(local_rows, B, width)
        cot_blocks = cotangent[seq].reshape(local_rows, B, width)
        split = []
        for at, count, rotated in groups:
            own = twiddle if at == 0 else None
            split.append(
                split_channels(place, tok_blocks, cot_blocks, at, count, ctx_size, rotated, own)
            )
        arrived = [exchange(p, 1, group[2]) for p, group in zip(split, groups)]
        planes = jnp.stack([part[2 * share :] for part in arrived[0]]).astype(jnp.float32)
        planes = planes[:, 0] + planes[:, 1] + planes[:, 2]
        twice = jnp.concatenate([planes[::-1]] * 2, axis=0)
        turn = ctx_size - 1 - lax.axis_index("ctx")
        twiddle_all = lax.dynamic_slice_in_dim(twice, turn, ctx_size, 0).reshape(A, B)
        factors = [first_factor, first_factor.T, second, second_t, twiddle_all]
        returned = []
        for which, (at, count, rotated) in enumerate(groups):
            parts, own_sums = mix(
                arrived[which], at, count, 2 * share, place, vectors, factors, sum_rows, ctx_size,
                rotated, [],
            )
            if which == 1:
                parts = hold(parts, arrived[2][1:])
            returned.append(exchange(parts, -1, rotated))
            terms.append(own_sums)
        leaving.append(returned)

    sums, own_sums = sum_over_mesh(add(terms, []), [part for r in leaving for part in r[2][-2:]])
    grads = []
    for returned in leaving:
        held = None
        for which in (0, 1, 2):
            at, count, rotated = groups[which]
            after = [own_sums] if which else []
            held = merge_channels(
                place, returned[which], held, at, count, ctx_size, rotated, width, after
            )
        grads.append(held.reshape(tok_rows, width))
    grad_tokens = jnp.stack(grads)

    total_seqs = seq_count * dp_size
    first_norm = math.sqrt(total_seqs * B * width)
    second_norm = math.sqrt(total_seqs * A * width)
    twiddle_norm = math.sqrt(total_seqs * width)
    channel_norm = math.sqrt(total_seqs * A * B)
    first_sum = jnp.concatenate([sums[half * A : (half + 1) * A] for half in range(A // B)], axis=1)
    mine = TWIDDLE_AT + lax.axis_index("ctx") * local_rows
    twiddle_sum = lax.dynamic_slice_in_dim(sums, mine, local_rows, 0)
    channel_sum = sums[CHANNEL_AT:used_rows].reshape(3, width)
    return (
        grad_tokens,
        first_sum / first_norm,
        sums[SECOND_AT:TWIDDLE_AT] / second_norm,
        twiddle_sum / twiddle_norm,
        channel_sum[0] / channel_norm,
        channel_sum[1] / channel_norm,
        channel_sum[2] / channel_norm,
    )


def solution(mesh):
    return jax.shard_map(
        body,
        mesh=mesh,
        in_specs=(
            P("dp", "ctx", None),
            P("dp", "ctx", None),
            P(),
            P(),
            P("ctx", None),
            P(),
            P(),
            P(),
        ),
        out_specs=(P("dp", "ctx", None), P(), P(), P("ctx", None), P(), P(), P()),
        check_vma=False,
    )
```

```python
import functools
import math

import jax
import jax.numpy as jnp
from jax import lax
from jax.experimental import pallas as pl
from jax.experimental.pallas import tpu as pltpu
from jax.sharding import PartitionSpec as P

A = 256
B = 128
LANES = 128
VMEM_BYTES = 48 * 1024 * 1024


def dot(left, right, left_dim, right_dim):
    return lax.dot_general(
        left, right, (((left_dim,), (right_dim,)), ((), ())), preferred_element_type=jnp.float32
    )


def views(refs, rotated):
    return list(refs) if rotated else [refs[0].at[i] for i in range(refs[0].shape[0])]


def split_tile(first_channel, tok_ref, cot_ref, out_refs, swap_ref):
    rows = tok_ref.shape[0]
    share = LANES // len(out_refs)
    for which, ref in enumerate((tok_ref, cot_ref)):
        for row in range(rows):
            swap_ref[row * LANES : (row + 1) * LANES, :] = ref[row].astype(jnp.float32).T
        for slot, out_ref in enumerate(out_refs):
            start = (first_channel + slot * share) % LANES
            for channel in range(share):
                out_ref[which * share + channel] = swap_ref[
                    pl.ds(start + channel, rows, stride=LANES), :
                ].astype(jnp.bfloat16)


def split_kernel(place_ref, tok_ref, cot_ref, *rest, rotated):
    first_channel = place_ref[0] if rotated else 0
    split_tile(first_channel, tok_ref, cot_ref, views(rest[:-1], rotated), rest[-1])


def split_twiddle_kernel(place_ref, tok_ref, cot_ref, twiddle_ref, *rest, rotated):
    split_kernel(place_ref, tok_ref, cot_ref, *rest, rotated=rotated)
    out_refs = views(rest[:-1], rotated)
    share = LANES // len(out_refs)
    left = twiddle_ref[...]
    for plane in range(3):
        part = left.astype(jnp.bfloat16)
        left = left - part.astype(jnp.float32)
        for out_ref in out_refs:
            out_ref[2 * share + plane] = part


def part_specs(devices, rotated, block, index):
    if rotated:
        return [pl.BlockSpec(block, index)] * devices
    return [pl.BlockSpec((devices, *block), lambda *at: (0, *index(*at)))]


def part_shapes(devices, rotated, shape):
    if rotated:
        return [jax.ShapeDtypeStruct(shape, jnp.bfloat16)] * devices
    return [jax.ShapeDtypeStruct((devices, *shape), jnp.bfloat16)]


def split_channels(place, tokens, cotangent, tile, tiles, devices, rotated, twiddle=None):
    rows = tokens.shape[0]
    step = min(16, rows)
    share = LANES // devices
    block = pl.BlockSpec((step, B, LANES), lambda t, i: (i, 0, tile + t))
    specs = [pl.BlockSpec(memory_space=pltpu.SMEM), block, block]
    if twiddle is None:
        kernel, given = split_kernel, [place, tokens, cotangent]
        planes = 2 * share
    else:
        kernel, given = split_twiddle_kernel, [place, tokens, cotangent, twiddle]
        specs.append(pl.BlockSpec((step, B), lambda t, i: (i, 0)))
        planes = 2 * share + 3
    return pl.pallas_call(
        functools.partial(kernel, rotated=rotated),
        grid=(tiles, rows // step),
        in_specs=specs,
        out_specs=part_specs(devices, rotated, (planes, step, B), lambda t, i: (t, i, 0)),
        out_shape=part_shapes(devices, rotated, (tiles * planes, rows, B)),
        scratch_shapes=[pltpu.VMEM((step * LANES, B), jnp.float32)],
        compiler_params=pltpu.CompilerParams(vmem_limit_bytes=VMEM_BYTES),
        cost_estimate=pl.CostEstimate(flops=1, bytes_accessed=16 * rows * B * LANES * tiles, transcendentals=0),
    )(*given)


def merge_kernel(place_ref, *rest, parts, rotated):
    part_refs, out_ref, swap_ref = views(rest[:parts], rotated), rest[-2], rest[-1]
    share, rows, _ = part_refs[0].shape
    for slot, part_ref in enumerate(part_refs):
        start = (place_ref[0] + slot * share) % LANES if rotated else slot * share
        for channel in range(share):
            at = pl.multiple_of((start + channel) * rows, rows)
            swap_ref[pl.ds(at, rows), :] = part_ref[channel].astype(jnp.float32)
    for row in range(rows):
        out_ref[row] = swap_ref[pl.ds(row, LANES, stride=rows), :].T.astype(jnp.bfloat16)


def merge_channels(place, parts, held, tile, tiles, devices, rotated, width, after):
    rows = parts[0].shape[-2]
    step = min(16, rows)
    share = LANES // devices
    given = [place, *parts]
    specs = [pl.BlockSpec(memory_space=pltpu.SMEM)]
    specs += part_specs(devices, rotated, (share, step, B), lambda t, i: (t, i, 0))
    for array in after if held is None else [held, *after]:
        given.append(array)
        specs.append(pl.BlockSpec(memory_space=pl.ANY))
    return pl.pallas_call(
        functools.partial(merge_kernel, parts=len(parts), rotated=rotated),
        grid=(tiles, rows // step),
        in_specs=specs,
        out_specs=pl.BlockSpec((step, B, LANES), lambda t, i: (i, 0, tile + t)),
        out_shape=jax.ShapeDtypeStruct((rows, B, width), jnp.bfloat16),
        scratch_shapes=[pltpu.VMEM((step * LANES, B), jnp.float32)],
        input_output_aliases={} if held is None else {len(parts) + 1: 0},
        compiler_params=pltpu.CompilerParams(vmem_limit_bytes=VMEM_BYTES),
        cost_estimate=pl.CostEstimate(flops=1, bytes_accessed=8 * rows * B * LANES * tiles, transcendentals=0),
    )(*given)


SECOND_AT = 2 * A
TWIDDLE_AT = SECOND_AT + B
CHANNEL_AT = TWIDDLE_AT + A


def mix_kernel(
    place_ref, gain_ref, bias_ref, skip_ref, *rest, parts, tile, tile_count, rotated
):
    tok_refs = views(rest[:parts], rotated)
    cot_refs = views(rest[parts : 2 * parts], rotated)
    first_ref, first_t_ref, second_ref, second_t_ref, twiddle_ref = rest[2 * parts : 2 * parts + 5]
    out_refs = views(rest[-3 - parts : -3], rotated)
    sums_ref, tok_all, cot_all = rest[-3:]
    t, step = pl.program_id(0), pl.program_id(1)

    @pl.when((t == 0) & (step == 0))
    def _():
        sums_ref[...] = jnp.zeros(sums_ref.shape, jnp.float32)

    devices = len(tok_refs)
    pair, rows, _ = tok_refs[0].shape
    share = LANES // devices
    lane_at = place_ref[0] + step * pair
    at = (tile + t) * LANES + lane_at

    def rows_from(shift):
        if not rotated:
            return slice(shift * rows, (shift + 1) * rows)
        source = (place_ref[0] // share - shift + devices) % devices
        return pl.ds(pl.multiple_of(source * rows, rows), rows)

    for refs, whole in ((tok_refs, tok_all), (cot_refs, cot_all)):
        for shift, ref in enumerate(refs):
            for c in range(pair):
                whole[rows_from(shift), c * B : (c + 1) * B] = ref[c].astype(jnp.float32)

    def spread(ref):
        lane = lax.broadcasted_iota(jnp.int32, (1, pair * B), 1)
        row = jnp.full((1, pair * B), ref[at], jnp.float32)
        for c in range(1, pair):
            row = jnp.where(lane >= c * B, ref[at + c], row)
        return row

    gain, bias, skip = spread(gain_ref), spread(bias_ref), spread(skip_ref)
    inputs = tok_all[...]
    tok = inputs.astype(jnp.bfloat16)
    upstream = cot_all[...]
    twiddle = jnp.concatenate([twiddle_ref[...]] * pair, axis=1)
    inner = dot(tok, second_t_ref[...], 1, 0)
    scaled = (inner * twiddle).astype(jnp.bfloat16)
    gate = jax.nn.sigmoid(gain * inputs + bias)
    grad_hidden = upstream * gate
    grad_outer = grad_hidden.astype(jnp.bfloat16)
    outer = dot(first_ref[...], scaled, 1, 0).astype(jnp.bfloat16).astype(jnp.float32)
    grad_scaled = dot(first_t_ref[...], grad_outer, 1, 0).astype(jnp.bfloat16).astype(jnp.float32)
    first_term = dot(grad_outer, scaled, 1, 1)
    for half in range(A // B):
        sums_ref[half * A : (half + 1) * A] += first_term[:, half * B : (half + 1) * B]
    hidden = outer + skip * inputs
    grad_pre = upstream * hidden * gate * (1.0 - gate)
    product = grad_scaled * inner
    sums_ref[TWIDDLE_AT:CHANNEL_AT] += sum(product[:, c * B : (c + 1) * B] for c in range(pair))
    grad_inner = (grad_scaled * twiddle).astype(jnp.bfloat16)
    second_term = dot(grad_inner, tok, 0, 0)
    sums_ref[SECOND_AT:TWIDDLE_AT] += sum(
        second_term[c * B : (c + 1) * B, c * B : (c + 1) * B] for c in range(pair)
    )
    lane = lax.broadcasted_iota(jnp.int32, (1, LANES), 1)
    for which, value in enumerate((grad_pre * inputs, grad_pre, grad_hidden * inputs)):
        total = jnp.sum(value, axis=0, keepdims=True)
        row = jnp.zeros((1, LANES), jnp.float32)
        for c in range(pair):
            channel = jnp.sum(total[:, c * B : (c + 1) * B], axis=1, keepdims=True)
            row = jnp.where(lane == lane_at + c, channel, row)
        sums_ref[pl.ds(CHANNEL_AT + which * tile_count + tile + t, 1), :] += row
    grad_in = dot(grad_inner, second_ref[...], 1, 0)
    tok_all[...] = grad_in + grad_hidden * skip + grad_pre * gain
    for shift, out_ref in enumerate(out_refs):
        for c in range(pair):
            out_ref[c] = tok_all[rows_from(shift), c * B : (c + 1) * B].astype(jnp.bfloat16)


def mix(parts, tile, tiles, planes, place, vectors, factors, sum_rows, devices, rotated, after):
    rows = parts[0].shape[-2]
    share = LANES // devices
    pair = factors[2].shape[0] // B
    steps = share // pair
    whole = lambda array: pl.BlockSpec(array.shape, lambda t, i: (0,) * array.ndim)
    tok_at = lambda t, i: (t * (planes // pair) + i, 0, 0)
    cot_at = lambda t, i: (t * (planes // pair) + steps + i, 0, 0)
    block = (pair, rows, B)
    tile_count = vectors[0].shape[0] // LANES
    *leaving, sums = pl.pallas_call(
        functools.partial(
            mix_kernel, parts=len(parts), tile=tile, tile_count=tile_count, rotated=rotated
        ),
        grid=(tiles, steps),
        in_specs=[pl.BlockSpec(memory_space=pltpu.SMEM)] * 4
        + part_specs(devices, rotated, block, tok_at)
        + part_specs(devices, rotated, block, cot_at)
        + [whole(f) for f in factors]
        + [pl.BlockSpec(memory_space=pl.ANY)] * len(after),
        out_specs=part_specs(devices, rotated, block, lambda t, i: (t * steps + i, 0, 0))
        + [pl.BlockSpec((sum_rows, LANES), lambda t, i: (0, 0))],
        out_shape=part_shapes(devices, rotated, (tiles * share, rows, B))
        + [jax.ShapeDtypeStruct((sum_rows, LANES), jnp.float32)],
        scratch_shapes=[pltpu.VMEM((A, pair * B), jnp.float32)] * 2,
        compiler_params=pltpu.CompilerParams(vmem_limit_bytes=VMEM_BYTES),
        cost_estimate=pl.CostEstimate(flops=tiles * share * A * B * 16000, bytes_accessed=1024, transcendentals=0),
    )(place, *vectors, *parts, *parts, *factors, *after)
    return leaving, sums


def add_kernel(*refs, count):
    total = refs[0][...]
    for ref in refs[1:count]:
        total += ref[...]
    refs[-1][...] = total


def add(terms, after):
    vmem = pl.BlockSpec(memory_space=pltpu.VMEM)
    return pl.pallas_call(
        functools.partial(add_kernel, count=len(terms)),
        in_specs=[vmem] * len(terms) + [pl.BlockSpec(memory_space=pl.ANY)] * len(after),
        out_specs=vmem,
        out_shape=jax.ShapeDtypeStruct(terms[0].shape, terms[0].dtype),
        cost_estimate=pl.CostEstimate(flops=1, bytes_accessed=1024, transcendentals=0),
    )(*terms, *after)


def hold(arrays, after):
    anywhere = pl.BlockSpec(memory_space=pl.ANY)
    return pl.pallas_call(
        lambda *refs: None,
        in_specs=[anywhere] * (len(arrays) + len(after)),
        out_specs=[anywhere] * len(arrays),
        out_shape=[jax.ShapeDtypeStruct(a.shape, a.dtype) for a in arrays],
        input_output_aliases={i: i for i in range(len(arrays))},
        cost_estimate=pl.CostEstimate(flops=1, bytes_accessed=1024, transcendentals=0),
    )(*arrays, *after)


def block_diagonal(square, count):
    zero = jnp.zeros_like(square)
    return jnp.concatenate(
        [
            jnp.concatenate([square if i == j else zero for j in range(count)], axis=1)
            for i in range(count)
        ],
        axis=0,
    )


def sum_over_mesh(sums, beside):
    beside = [None, *beside]

    def exchange_with(array, axis, bit):
        after = beside.pop(0) if beside else None
        if after is not None:
            (array,) = hold([array], after)
        size = lax.axis_size(axis)
        return array, lax.ppermute(array, axis, [(i, i ^ bit) for i in range(size)])

    dp = lax.axis_index("dp")
    bits = [1 << k for k in range(lax.axis_size("dp").bit_length() - 1)]
    for bit in reversed(bits):
        halves = sums.reshape(2, -1, LANES)
        high = (dp & bit) != 0
        _, other = exchange_with(jnp.where(high, halves[0], halves[1]), "dp", bit)
        sums = jnp.where(high, halves[1], halves[0]) + other
    bit = 1
    while bit < lax.axis_size("ctx"):
        sums, other = exchange_with(sums, "ctx", bit)
        sums = sums + other
        bit *= 2
    for bit in bits:
        sums, other = exchange_with(sums, "dp", bit)
        high = (dp & bit) != 0
        sums = jnp.concatenate([jnp.where(high, other, sums), jnp.where(high, sums, other)])
    return sums


def body(tokens, cotangent, first_factor, second_factor, twiddle, gate_gain, gate_bias, skip_gain):
    seq_count, tok_rows, width = tokens.shape
    ctx_size = lax.axis_size("ctx")
    dp_size = lax.axis_size("dp")
    share = LANES // ctx_size
    local_rows = tok_rows // B
    tiles = width // LANES
    pair = 2
    half = tiles // 2
    groups = [(0, 1, True), (1, half - 1, False), (half, tiles - half, True)]

    place = (lax.axis_index("ctx") * share).astype(jnp.int32).reshape(1)
    second = block_diagonal(second_factor, pair)
    second_t = block_diagonal(second_factor.T, pair)
    vectors = [gate_gain, gate_bias, skip_gain]
    used_rows = CHANNEL_AT + 3 * tiles
    sum_rows = -(-used_rows // (8 * dp_size)) * 8 * dp_size

    def exchange(parts, sign, rotated):
        if not rotated:
            return [lax.all_to_all(parts[0], "ctx", split_axis=0, concat_axis=0, tiled=True)]
        moved = [parts[0]]
        for shift in range(1, ctx_size):
            pairs = [(i, (i + sign * shift) % ctx_size) for i in range(ctx_size)]
            moved.append(lax.ppermute(parts[shift], "ctx", pairs))
        return moved

    terms = []
    leaving = []
    for seq in range(seq_count):
        tok_blocks = tokens[seq].reshape(local_rows, B, width)
        cot_blocks = cotangent[seq].reshape(local_rows, B, width)
        split = []
        for at, count, rotated in groups:
            own = twiddle if at == 0 else None
            split.append(
                split_channels(place, tok_blocks, cot_blocks, at, count, ctx_size, rotated, own)
            )
        arrived = [exchange(p, 1, group[2]) for p, group in zip(split, groups)]
        planes = jnp.stack([part[2 * share :] for part in arrived[0]]).astype(jnp.float32)
        planes = planes[:, 0] + planes[:, 1] + planes[:, 2]
        twice = jnp.concatenate([planes[::-1]] * 2, axis=0)
        turn = ctx_size - 1 - lax.axis_index("ctx")
        twiddle_all = lax.dynamic_slice_in_dim(twice, turn, ctx_size, 0).reshape(A, B)
        factors = [first_factor, first_factor.T, second, second_t, twiddle_all]
        returned = []
        for which, (at, count, rotated) in enumerate(groups):
            parts, own_sums = mix(
                arrived[which], at, count, 2 * share, place, vectors, factors, sum_rows, ctx_size,
                rotated, [],
            )
            if which == 1:
                parts = hold(parts, arrived[2][1:])
            returned.append(exchange(parts, -1, rotated))
            terms.append(own_sums)
        leaving.append(returned)

    back = leaving[-1][2]
    sums = sum_over_mesh(add(terms, []), [None, back[-2:], back[1:2], back[2:3], back[3:5], back[5:-2]])
    grads = []
    for returned in leaving:
        held = None
        for which in (1, 2, 0):
            at, count, rotated = groups[which]
            after = []
            held = merge_channels(
                place, returned[which], held, at, count, ctx_size, rotated, width, after
            )
        grads.append(held.reshape(tok_rows, width))
    grad_tokens = jnp.stack(grads)

    total_seqs = seq_count * dp_size
    first_norm = math.sqrt(total_seqs * B * width)
    second_norm = math.sqrt(total_seqs * A * width)
    twiddle_norm = math.sqrt(total_seqs * width)
    channel_norm = math.sqrt(total_seqs * A * B)
    first_sum = jnp.concatenate([sums[half * A : (half + 1) * A] for half in range(A // B)], axis=1)
    mine = TWIDDLE_AT + lax.axis_index("ctx") * local_rows
    twiddle_sum = lax.dynamic_slice_in_dim(sums, mine, local_rows, 0)
    channel_sum = sums[CHANNEL_AT:used_rows].reshape(3, width)
    return (
        grad_tokens,
        first_sum / first_norm,
        sums[SECOND_AT:TWIDDLE_AT] / second_norm,
        twiddle_sum / twiddle_norm,
        channel_sum[0] / channel_norm,
        channel_sum[1] / channel_norm,
        channel_sum[2] / channel_norm,
    )


def solution(mesh):
    return jax.shard_map(
        body,
        mesh=mesh,
        in_specs=(
            P("dp", "ctx", None),
            P("dp", "ctx", None),
            P(),
            P(),
            P("ctx", None),
            P(),
            P(),
            P(),
        ),
        out_specs=(P("dp", "ctx", None), P(), P(), P("ctx", None), P(), P(), P()),
        check_vma=False,
    )
```

```python
import functools
import math

import jax
import jax.numpy as jnp
from jax import lax
from jax.experimental import pallas as pl
from jax.experimental.pallas import tpu as pltpu
from jax.sharding import PartitionSpec as P

A = 256
B = 128
LANES = 128
VMEM_BYTES = 48 * 1024 * 1024


def dot(left, right, left_dim, right_dim):
    return lax.dot_general(
        left, right, (((left_dim,), (right_dim,)), ((), ())), preferred_element_type=jnp.float32
    )


def views(refs, rotated):
    return list(refs) if rotated else [refs[0].at[i] for i in range(refs[0].shape[0])]


def split_tile(first_channel, ref, out_refs, swap_ref, lanes, at):
    rows = ref.shape[0]
    share = LANES // len(out_refs)
    for row in range(rows):
        swap_ref[row * LANES : (row + 1) * LANES, :] = ref[row, :, lanes].astype(jnp.float32).T
    for slot, out_ref in enumerate(out_refs):
        start = (first_channel + slot * share) % LANES
        for channel in range(share):
            out_ref[at + channel] = swap_ref[pl.ds(start + channel, rows, stride=LANES), :].astype(
                jnp.bfloat16
            )


def split_kernel(place_ref, tok_ref, cot_ref, *rest, rotated, tiles):
    first_channel = place_ref[0] if rotated else 0
    *rest, swap_ref = rest
    twiddle_ref = rest.pop(0) if tiles else None
    out_refs = views(rest, rotated)
    share = LANES // len(out_refs)
    for tile in range(max(tiles, 1)):
        lanes = slice(tile * LANES, (tile + 1) * LANES)
        for which, ref in enumerate((tok_ref, cot_ref)):
            at = (2 * tile + which) * share
            split_tile(first_channel, ref, out_refs, swap_ref, lanes, at)
    if tiles:
        left = twiddle_ref[...]
        for plane in range(3):
            part = left.astype(jnp.bfloat16)
            left = left - part.astype(jnp.float32)
            for out_ref in out_refs:
                out_ref[2 * tiles * share + plane] = part


def part_specs(devices, rotated, block, index):
    if rotated:
        return [pl.BlockSpec(block, index)] * devices
    return [pl.BlockSpec((devices, *block), lambda *at: (0, *index(*at)))]


def part_shapes(devices, rotated, shape):
    if rotated:
        return [jax.ShapeDtypeStruct(shape, jnp.bfloat16)] * devices
    return [jax.ShapeDtypeStruct((devices, *shape), jnp.bfloat16)]


def split_channels(place, tokens, cotangent, tile, tiles, devices, rotated, twiddle=None):
    rows, _, width = tokens.shape
    step = min(16, rows)
    share = LANES // devices
    specs = [pl.BlockSpec(memory_space=pltpu.SMEM)]
    if twiddle is None:
        given, inner, steps, planes = [place, tokens, cotangent], 0, tiles, 2 * share
        specs += [pl.BlockSpec((step, B, LANES), lambda t, i: (i, 0, tile + t))] * 2
    else:
        given, inner, steps = [place, tokens, cotangent, twiddle], tiles, 1
        planes = 2 * tiles * share + 3
        block = (step, B, tiles * LANES)
        specs += [pl.BlockSpec(block, lambda t, i: (i, 0, tile // tiles))] * 2
        specs.append(pl.BlockSpec((step, B), lambda t, i: (i, 0)))
    return pl.pallas_call(
        functools.partial(split_kernel, rotated=rotated, tiles=inner),
        grid=(steps, rows // step),
        in_specs=specs,
        out_specs=part_specs(devices, rotated, (planes, step, B), lambda t, i: (t, i, 0)),
        out_shape=part_shapes(devices, rotated, (steps * planes, rows, B)),
        scratch_shapes=[pltpu.VMEM((step * LANES, B), jnp.float32)],
        compiler_params=pltpu.CompilerParams(vmem_limit_bytes=VMEM_BYTES),
        cost_estimate=pl.CostEstimate(
            flops=1, bytes_accessed=16 * rows * B * LANES * tiles, transcendentals=0
        ),
    )(*given)


def merge_kernel(place_ref, *rest, parts, rotated):
    part_refs, out_ref, swap_ref = views(rest[:parts], rotated), rest[-2], rest[-1]
    share, rows, _ = part_refs[0].shape
    for slot, part_ref in enumerate(part_refs):
        start = (place_ref[0] + slot * share) % LANES if rotated else slot * share
        for channel in range(share):
            at = pl.multiple_of((start + channel) * rows, rows)
            swap_ref[pl.ds(at, rows), :] = part_ref[channel].astype(jnp.float32)
    for row in range(rows):
        out_ref[row] = swap_ref[pl.ds(row, LANES, stride=rows), :].T.astype(jnp.bfloat16)


def merge_channels(place, parts, held, tile, tiles, devices, rotated, width, after):
    rows = parts[0].shape[-2]
    step = min(16, rows)
    share = LANES // devices
    given = [place, *parts]
    specs = [pl.BlockSpec(memory_space=pltpu.SMEM)]
    specs += part_specs(devices, rotated, (share, step, B), lambda t, i: (t, i, 0))
    for array in after if held is None else [held, *after]:
        given.append(array)
        specs.append(pl.BlockSpec(memory_space=pl.ANY))
    return pl.pallas_call(
        functools.partial(merge_kernel, parts=len(parts), rotated=rotated),
        grid=(tiles, rows // step),
        in_specs=specs,
        out_specs=pl.BlockSpec((step, B, LANES), lambda t, i: (i, 0, tile + t)),
        out_shape=jax.ShapeDtypeStruct((rows, B, width), jnp.bfloat16),
        scratch_shapes=[pltpu.VMEM((step * LANES, B), jnp.float32)],
        input_output_aliases={} if held is None else {len(parts) + 1: 0},
        compiler_params=pltpu.CompilerParams(vmem_limit_bytes=VMEM_BYTES),
        cost_estimate=pl.CostEstimate(flops=1, bytes_accessed=8 * rows * B * LANES * tiles, transcendentals=0),
    )(*given)


SECOND_AT = 2 * A
TWIDDLE_AT = SECOND_AT + B
CHANNEL_AT = TWIDDLE_AT + A


def mix_kernel(
    place_ref, gain_ref, bias_ref, skip_ref, *rest, parts, tile, tile_count, rotated
):
    tok_refs = views(rest[:parts], rotated)
    cot_refs = views(rest[parts : 2 * parts], rotated)
    first_ref, first_t_ref, second_ref, second_t_ref, twiddle_ref = rest[2 * parts : 2 * parts + 5]
    out_refs = views(rest[-3 - parts : -3], rotated)
    sums_ref, tok_all, cot_all = rest[-3:]
    t, step = pl.program_id(0), pl.program_id(1)

    @pl.when((t == 0) & (step == 0))
    def _():
        sums_ref[...] = jnp.zeros(sums_ref.shape, jnp.float32)

    devices = len(tok_refs)
    pair, rows, _ = tok_refs[0].shape
    share = LANES // devices
    lane_at = place_ref[0] + step * pair
    at = (tile + t) * LANES + lane_at

    def rows_from(shift):
        if not rotated:
            return slice(shift * rows, (shift + 1) * rows)
        source = (place_ref[0] // share - shift + devices) % devices
        return pl.ds(pl.multiple_of(source * rows, rows), rows)

    for refs, whole in ((tok_refs, tok_all), (cot_refs, cot_all)):
        for shift, ref in enumerate(refs):
            for c in range(pair):
                whole[rows_from(shift), c * B : (c + 1) * B] = ref[c].astype(jnp.float32)

    def spread(ref):
        lane = lax.broadcasted_iota(jnp.int32, (1, pair * B), 1)
        row = jnp.full((1, pair * B), ref[at], jnp.float32)
        for c in range(1, pair):
            row = jnp.where(lane >= c * B, ref[at + c], row)
        return row

    gain, bias, skip = spread(gain_ref), spread(bias_ref), spread(skip_ref)
    inputs = tok_all[...]
    tok = inputs.astype(jnp.bfloat16)
    upstream = cot_all[...]
    twiddle = jnp.concatenate([twiddle_ref[...]] * pair, axis=1)
    inner = dot(tok, second_t_ref[...], 1, 0)
    scaled = (inner * twiddle).astype(jnp.bfloat16)
    gate = jax.nn.sigmoid(gain * inputs + bias)
    grad_hidden = upstream * gate
    grad_outer = grad_hidden.astype(jnp.bfloat16)
    outer = dot(first_ref[...], scaled, 1, 0).astype(jnp.bfloat16).astype(jnp.float32)
    grad_scaled = dot(first_t_ref[...], grad_outer, 1, 0).astype(jnp.bfloat16).astype(jnp.float32)
    first_term = dot(grad_outer, scaled, 1, 1)
    for half in range(A // B):
        sums_ref[half * A : (half + 1) * A] += first_term[:, half * B : (half + 1) * B]
    hidden = outer + skip * inputs
    grad_pre = upstream * hidden * gate * (1.0 - gate)
    product = grad_scaled * inner
    sums_ref[TWIDDLE_AT:CHANNEL_AT] += sum(product[:, c * B : (c + 1) * B] for c in range(pair))
    grad_inner = (grad_scaled * twiddle).astype(jnp.bfloat16)
    second_term = dot(grad_inner, tok, 0, 0)
    sums_ref[SECOND_AT:TWIDDLE_AT] += sum(
        second_term[c * B : (c + 1) * B, c * B : (c + 1) * B] for c in range(pair)
    )
    lane = lax.broadcasted_iota(jnp.int32, (1, LANES), 1)
    for which, value in enumerate((grad_pre * inputs, grad_pre, grad_hidden * inputs)):
        total = jnp.sum(value, axis=0, keepdims=True)
        row = jnp.zeros((1, LANES), jnp.float32)
        for c in range(pair):
            channel = jnp.sum(total[:, c * B : (c + 1) * B], axis=1, keepdims=True)
            row = jnp.where(lane == lane_at + c, channel, row)
        sums_ref[pl.ds(CHANNEL_AT + which * tile_count + tile + t, 1), :] += row
    grad_in = dot(grad_inner, second_ref[...], 1, 0)
    tok_all[...] = grad_in + grad_hidden * skip + grad_pre * gain
    for shift, out_ref in enumerate(out_refs):
        for c in range(pair):
            out_ref[c] = tok_all[rows_from(shift), c * B : (c + 1) * B].astype(jnp.bfloat16)


def mix(parts, tile, tiles, planes, place, vectors, factors, sum_rows, devices, rotated, after):
    rows = parts[0].shape[-2]
    share = LANES // devices
    pair = factors[2].shape[0] // B
    steps = share // pair
    whole = lambda array: pl.BlockSpec(array.shape, lambda t, i: (0,) * array.ndim)
    tok_at = lambda t, i: (t * (planes // pair) + i, 0, 0)
    cot_at = lambda t, i: (t * (planes // pair) + steps + i, 0, 0)
    block = (pair, rows, B)
    tile_count = vectors[0].shape[0] // LANES
    *leaving, sums = pl.pallas_call(
        functools.partial(
            mix_kernel, parts=len(parts), tile=tile, tile_count=tile_count, rotated=rotated
        ),
        grid=(tiles, steps),
        in_specs=[pl.BlockSpec(memory_space=pltpu.SMEM)] * 4
        + part_specs(devices, rotated, block, tok_at)
        + part_specs(devices, rotated, block, cot_at)
        + [whole(f) for f in factors]
        + [pl.BlockSpec(memory_space=pl.ANY)] * len(after),
        out_specs=part_specs(devices, rotated, block, lambda t, i: (t * steps + i, 0, 0))
        + [pl.BlockSpec((sum_rows, LANES), lambda t, i: (0, 0))],
        out_shape=part_shapes(devices, rotated, (tiles * share, rows, B))
        + [jax.ShapeDtypeStruct((sum_rows, LANES), jnp.float32)],
        scratch_shapes=[pltpu.VMEM((A, pair * B), jnp.float32)] * 2,
        compiler_params=pltpu.CompilerParams(vmem_limit_bytes=VMEM_BYTES),
        cost_estimate=pl.CostEstimate(flops=tiles * share * A * B * 16000, bytes_accessed=1024, transcendentals=0),
    )(place, *vectors, *parts, *parts, *factors, *after)
    return leaving, sums


def add_kernel(*refs, count):
    total = refs[0][...]
    for ref in refs[1:count]:
        total += ref[...]
    refs[-1][...] = total


def add(terms, after):
    vmem = pl.BlockSpec(memory_space=pltpu.VMEM)
    return pl.pallas_call(
        functools.partial(add_kernel, count=len(terms)),
        in_specs=[vmem] * len(terms) + [pl.BlockSpec(memory_space=pl.ANY)] * len(after),
        out_specs=vmem,
        out_shape=jax.ShapeDtypeStruct(terms[0].shape, terms[0].dtype),
        cost_estimate=pl.CostEstimate(flops=1, bytes_accessed=1024, transcendentals=0),
    )(*terms, *after)


def hold(arrays, after):
    anywhere = pl.BlockSpec(memory_space=pl.ANY)
    return pl.pallas_call(
        lambda *refs: None,
        in_specs=[anywhere] * (len(arrays) + len(after)),
        out_specs=[anywhere] * len(arrays),
        out_shape=[jax.ShapeDtypeStruct(a.shape, a.dtype) for a in arrays],
        input_output_aliases={i: i for i in range(len(arrays))},
        cost_estimate=pl.CostEstimate(flops=1, bytes_accessed=1024, transcendentals=0),
    )(*arrays, *after)


def block_diagonal(square, count):
    zero = jnp.zeros_like(square)
    return jnp.concatenate(
        [
            jnp.concatenate([square if i == j else zero for j in range(count)], axis=1)
            for i in range(count)
        ],
        axis=0,
    )


def sum_over_mesh(sums, beside):
    beside = [None, *beside]

    def exchange_with(array, axis, bit):
        after = beside.pop(0) if beside else None
        if after is not None:
            (array,) = hold([array], after)
        size = lax.axis_size(axis)
        return array, lax.ppermute(array, axis, [(i, i ^ bit) for i in range(size)])

    dp = lax.axis_index("dp")
    bits = [1 << k for k in range(lax.axis_size("dp").bit_length() - 1)]
    for bit in reversed(bits):
        halves = sums.reshape(2, -1, LANES)
        high = (dp & bit) != 0
        _, other = exchange_with(jnp.where(high, halves[0], halves[1]), "dp", bit)
        sums = jnp.where(high, halves[1], halves[0]) + other
    bit = 1
    while bit < lax.axis_size("ctx"):
        sums, other = exchange_with(sums, "ctx", bit)
        sums = sums + other
        bit *= 2
    for bit in bits:
        sums, other = exchange_with(sums, "dp", bit)
        high = (dp & bit) != 0
        sums = jnp.concatenate([jnp.where(high, other, sums), jnp.where(high, sums, other)])
    return sums


def body(tokens, cotangent, first_factor, second_factor, twiddle, gate_gain, gate_bias, skip_gain):
    seq_count, tok_rows, width = tokens.shape
    ctx_size = lax.axis_size("ctx")
    dp_size = lax.axis_size("dp")
    share = LANES // ctx_size
    local_rows = tok_rows // B
    tiles = width // LANES
    pair = 2
    half = tiles // 2
    groups = [(0, half, True), (half, tiles - half - 1, False), (tiles - 1, 1, True)]

    place = (lax.axis_index("ctx") * share).astype(jnp.int32).reshape(1)
    second = block_diagonal(second_factor, pair)
    second_t = block_diagonal(second_factor.T, pair)
    vectors = [gate_gain, gate_bias, skip_gain]
    used_rows = CHANNEL_AT + 3 * tiles
    sum_rows = -(-used_rows // (8 * dp_size)) * 8 * dp_size

    def exchange(parts, sign, rotated):
        if not rotated:
            return [lax.all_to_all(parts[0], "ctx", split_axis=0, concat_axis=0, tiled=True)]
        moved = [parts[0]]
        for shift in range(1, ctx_size):
            pairs = [(i, (i + sign * shift) % ctx_size) for i in range(ctx_size)]
            moved.append(lax.ppermute(parts[shift], "ctx", pairs))
        return moved

    terms = []
    leaving = []
    for seq in range(seq_count):
        tok_blocks = tokens[seq].reshape(local_rows, B, width)
        cot_blocks = cotangent[seq].reshape(local_rows, B, width)
        split = []
        for at, count, rotated in groups:
            own = twiddle if at == 0 else None
            split.append(
                split_channels(place, tok_blocks, cot_blocks, at, count, ctx_size, rotated, own)
            )
        arrived = [exchange(p, 1, group[2]) for p, group in zip(split, groups)]
        planes = jnp.stack([part[2 * half * share :] for part in arrived[0]]).astype(jnp.float32)
        planes = planes[:, 0] + planes[:, 1] + planes[:, 2]
        twice = jnp.concatenate([planes[::-1]] * 2, axis=0)
        turn = ctx_size - 1 - lax.axis_index("ctx")
        twiddle_all = lax.dynamic_slice_in_dim(twice, turn, ctx_size, 0).reshape(A, B)
        factors = [first_factor, first_factor.T, second, second_t, twiddle_all]
        returned = []
        for which, (at, count, rotated) in enumerate(groups):
            parts, own_sums = mix(
                arrived[which], at, count, 2 * share, place, vectors, factors, sum_rows, ctx_size,
                rotated, [],
            )
            if which == 1:
                parts = hold(parts, arrived[2][1:])
            returned.append(exchange(parts, -1, rotated))
            terms.append(own_sums)
        leaving.append(returned)

    back = leaving[-1][0]
    sums = sum_over_mesh(add(terms, []), [None, back[-2:], back[1:2], back[2:3], back[3:5], back[5:-2]])
    grads = []
    for returned in leaving:
        held = None
        for which in (1, 0, 2):
            at, count, rotated = groups[which]
            after = []
            held = merge_channels(
                place, returned[which], held, at, count, ctx_size, rotated, width, after
            )
        grads.append(held.reshape(tok_rows, width))
    grad_tokens = jnp.stack(grads)

    total_seqs = seq_count * dp_size
    first_norm = math.sqrt(total_seqs * B * width)
    second_norm = math.sqrt(total_seqs * A * width)
    twiddle_norm = math.sqrt(total_seqs * width)
    channel_norm = math.sqrt(total_seqs * A * B)
    first_sum = jnp.concatenate([sums[half * A : (half + 1) * A] for half in range(A // B)], axis=1)
    mine = TWIDDLE_AT + lax.axis_index("ctx") * local_rows
    twiddle_sum = lax.dynamic_slice_in_dim(sums, mine, local_rows, 0)
    channel_sum = sums[CHANNEL_AT:used_rows].reshape(3, width)
    return (
        grad_tokens,
        first_sum / first_norm,
        sums[SECOND_AT:TWIDDLE_AT] / second_norm,
        twiddle_sum / twiddle_norm,
        channel_sum[0] / channel_norm,
        channel_sum[1] / channel_norm,
        channel_sum[2] / channel_norm,
    )


def solution(mesh):
    return jax.shard_map(
        body,
        mesh=mesh,
        in_specs=(
            P("dp", "ctx", None),
            P("dp", "ctx", None),
            P(),
            P(),
            P("ctx", None),
            P(),
            P(),
            P(),
        ),
        out_specs=(P("dp", "ctx", None), P(), P(), P("ctx", None), P(), P(), P()),
        check_vma=False,
    )
```

```python
import functools
import math

import jax
import jax.numpy as jnp
from jax import lax
from jax.experimental import pallas as pl
from jax.experimental.pallas import tpu as pltpu
from jax.sharding import PartitionSpec as P

A = 256
B = 128
LANES = 128
VMEM_BYTES = 48 * 1024 * 1024


def dot(left, right, left_dim, right_dim):
    return lax.dot_general(
        left, right, (((left_dim,), (right_dim,)), ((), ())), preferred_element_type=jnp.float32
    )


def views(refs, rotated):
    return list(refs) if rotated else [refs[0].at[i] for i in range(refs[0].shape[0])]


def split_tile(first_channel, tok_ref, cot_ref, out_refs, swap_ref):
    rows = tok_ref.shape[0]
    share = LANES // len(out_refs)
    for which, ref in enumerate((tok_ref, cot_ref)):
        for row in range(rows):
            swap_ref[row * LANES : (row + 1) * LANES, :] = ref[row].astype(jnp.float32).T
        for slot, out_ref in enumerate(out_refs):
            start = (first_channel + slot * share) % LANES
            for channel in range(share):
                out_ref[which * share + channel] = swap_ref[
                    pl.ds(start + channel, rows, stride=LANES), :
                ].astype(jnp.bfloat16)


def split_kernel(place_ref, tok_ref, cot_ref, *rest, rotated):
    first_channel = place_ref[0] if rotated else 0
    split_tile(first_channel, tok_ref, cot_ref, views(rest[:-1], rotated), rest[-1])


def split_twiddle_kernel(place_ref, tok_ref, cot_ref, twiddle_ref, *rest, rotated):
    split_kernel(place_ref, tok_ref, cot_ref, *rest, rotated=rotated)
    out_refs = views(rest[:-1], rotated)
    share = LANES // len(out_refs)
    left = twiddle_ref[...]
    for plane in range(3):
        part = left.astype(jnp.bfloat16)
        left = left - part.astype(jnp.float32)
        for out_ref in out_refs:
            out_ref[2 * share + plane] = part


def part_specs(devices, rotated, block, index):
    if rotated:
        return [pl.BlockSpec(block, index)] * devices
    return [pl.BlockSpec((devices, *block), lambda *at: (0, *index(*at)))]


def part_shapes(devices, rotated, shape):
    if rotated:
        return [jax.ShapeDtypeStruct(shape, jnp.bfloat16)] * devices
    return [jax.ShapeDtypeStruct((devices, *shape), jnp.bfloat16)]


def split_channels(place, tokens, cotangent, tile, tiles, devices, rotated, twiddle=None):
    rows = tokens.shape[0]
    step = min(16, rows)
    share = LANES // devices
    block = pl.BlockSpec((step, B, LANES), lambda t, i: (i, 0, tile + t))
    specs = [pl.BlockSpec(memory_space=pltpu.SMEM), block, block]
    if twiddle is None:
        kernel, given = split_kernel, [place, tokens, cotangent]
        planes = 2 * share
    else:
        kernel, given = split_twiddle_kernel, [place, tokens, cotangent, twiddle]
        specs.append(pl.BlockSpec((step, B), lambda t, i: (i, 0)))
        planes = 2 * share + 3
    return pl.pallas_call(
        functools.partial(kernel, rotated=rotated),
        grid=(tiles, rows // step),
        in_specs=specs,
        out_specs=part_specs(devices, rotated, (planes, step, B), lambda t, i: (t, i, 0)),
        out_shape=part_shapes(devices, rotated, (tiles * planes, rows, B)),
        scratch_shapes=[pltpu.VMEM((step * LANES, B), jnp.float32)],
        compiler_params=pltpu.CompilerParams(vmem_limit_bytes=VMEM_BYTES),
        cost_estimate=pl.CostEstimate(flops=1, bytes_accessed=16 * rows * B * LANES * tiles, transcendentals=0),
    )(*given)


def merge_kernel(place_ref, *rest, parts, rotated):
    part_refs, out_ref, swap_ref = views(rest[:parts], rotated), rest[-2], rest[-1]
    share, rows, _ = part_refs[0].shape
    for slot, part_ref in enumerate(part_refs):
        start = (place_ref[0] + slot * share) % LANES if rotated else slot * share
        for channel in range(share):
            at = pl.multiple_of((start + channel) * rows, rows)
            swap_ref[pl.ds(at, rows), :] = part_ref[channel].astype(jnp.float32)
    for row in range(rows):
        out_ref[row] = swap_ref[pl.ds(row, LANES, stride=rows), :].T.astype(jnp.bfloat16)


def merge_channels(place, parts, held, tile, tiles, devices, rotated, width, after):
    rows = parts[0].shape[-2]
    step = min(16, rows)
    share = LANES // devices
    given = [place, *parts]
    specs = [pl.BlockSpec(memory_space=pltpu.SMEM)]
    specs += part_specs(devices, rotated, (share, step, B), lambda t, i: (t, i, 0))
    for array in after if held is None else [held, *after]:
        given.append(array)
        specs.append(pl.BlockSpec(memory_space=pl.ANY))
    return pl.pallas_call(
        functools.partial(merge_kernel, parts=len(parts), rotated=rotated),
        grid=(tiles, rows // step),
        in_specs=specs,
        out_specs=pl.BlockSpec((step, B, LANES), lambda t, i: (i, 0, tile + t)),
        out_shape=jax.ShapeDtypeStruct((rows, B, width), jnp.bfloat16),
        scratch_shapes=[pltpu.VMEM((step * LANES, B), jnp.float32)],
        input_output_aliases={} if held is None else {len(parts) + 1: 0},
        compiler_params=pltpu.CompilerParams(vmem_limit_bytes=VMEM_BYTES),
        cost_estimate=pl.CostEstimate(flops=1, bytes_accessed=8 * rows * B * LANES * tiles, transcendentals=0),
    )(*given)


SECOND_AT = 2 * A
TWIDDLE_AT = SECOND_AT + B
CHANNEL_AT = TWIDDLE_AT + A


def mix_kernel(
    place_ref, gain_ref, bias_ref, skip_ref, *rest, parts, tile, tile_count, rotated
):
    tok_refs = views(rest[:parts], rotated)
    cot_refs = views(rest[parts : 2 * parts], rotated)
    first_ref, first_t_ref, second_ref, second_t_ref, twiddle_ref = rest[2 * parts : 2 * parts + 5]
    out_refs = views(rest[-3 - parts : -3], rotated)
    sums_ref, tok_all, cot_all = rest[-3:]
    t, step = pl.program_id(0), pl.program_id(1)

    @pl.when((t == 0) & (step == 0))
    def _():
        sums_ref[...] = jnp.zeros(sums_ref.shape, jnp.float32)

    devices = len(tok_refs)
    pair, rows, _ = tok_refs[0].shape
    share = LANES // devices
    lane_at = place_ref[0] + step * pair
    at = (tile + t) * LANES + lane_at

    def rows_from(shift):
        if not rotated:
            return slice(shift * rows, (shift + 1) * rows)
        source = (place_ref[0] // share - shift + devices) % devices
        return pl.ds(pl.multiple_of(source * rows, rows), rows)

    for refs, whole in ((tok_refs, tok_all), (cot_refs, cot_all)):
        for shift, ref in enumerate(refs):
            for c in range(pair):
                whole[rows_from(shift), c * B : (c + 1) * B] = ref[c].astype(jnp.float32)

    def spread(ref):
        lane = lax.broadcasted_iota(jnp.int32, (1, pair * B), 1)
        row = jnp.full((1, pair * B), ref[at], jnp.float32)
        for c in range(1, pair):
            row = jnp.where(lane >= c * B, ref[at + c], row)
        return row

    gain, bias, skip = spread(gain_ref), spread(bias_ref), spread(skip_ref)
    inputs = tok_all[...]
    tok = inputs.astype(jnp.bfloat16)
    upstream = cot_all[...]
    twiddle = jnp.concatenate([twiddle_ref[...]] * pair, axis=1)
    inner = dot(tok, second_t_ref[...], 1, 0)
    scaled = (inner * twiddle).astype(jnp.bfloat16)
    gate = jax.nn.sigmoid(gain * inputs + bias)
    grad_hidden = upstream * gate
    grad_outer = grad_hidden.astype(jnp.bfloat16)
    outer = dot(first_ref[...], scaled, 1, 0).astype(jnp.bfloat16).astype(jnp.float32)
    grad_scaled = dot(first_t_ref[...], grad_outer, 1, 0).astype(jnp.bfloat16).astype(jnp.float32)
    first_term = dot(grad_outer, scaled, 1, 1)
    for half in range(A // B):
        sums_ref[half * A : (half + 1) * A] += first_term[:, half * B : (half + 1) * B]
    hidden = outer + skip * inputs
    grad_pre = upstream * hidden * gate * (1.0 - gate)
    product = grad_scaled * inner
    sums_ref[TWIDDLE_AT:CHANNEL_AT] += sum(product[:, c * B : (c + 1) * B] for c in range(pair))
    grad_inner = (grad_scaled * twiddle).astype(jnp.bfloat16)
    second_term = dot(grad_inner, tok, 0, 0)
    sums_ref[SECOND_AT:TWIDDLE_AT] += sum(
        second_term[c * B : (c + 1) * B, c * B : (c + 1) * B] for c in range(pair)
    )
    lane = lax.broadcasted_iota(jnp.int32, (1, LANES), 1)
    for which, value in enumerate((grad_pre * inputs, grad_pre, grad_hidden * inputs)):
        total = jnp.sum(value, axis=0, keepdims=True)
        row = jnp.zeros((1, LANES), jnp.float32)
        for c in range(pair):
            channel = jnp.sum(total[:, c * B : (c + 1) * B], axis=1, keepdims=True)
            row = jnp.where(lane == lane_at + c, channel, row)
        sums_ref[pl.ds(CHANNEL_AT + which * tile_count + tile + t, 1), :] += row
    grad_in = dot(grad_inner, second_ref[...], 1, 0)
    tok_all[...] = grad_in + grad_hidden * skip + grad_pre * gain
    for shift, out_ref in enumerate(out_refs):
        for c in range(pair):
            out_ref[c] = tok_all[rows_from(shift), c * B : (c + 1) * B].astype(jnp.bfloat16)


def mix(parts, tile, tiles, planes, place, vectors, factors, sum_rows, devices, rotated, after):
    rows = parts[0].shape[-2]
    share = LANES // devices
    pair = factors[2].shape[0] // B
    steps = share // pair
    whole = lambda array: pl.BlockSpec(array.shape, lambda t, i: (0,) * array.ndim)
    tok_at = lambda t, i: (t * (planes // pair) + i, 0, 0)
    cot_at = lambda t, i: (t * (planes // pair) + steps + i, 0, 0)
    block = (pair, rows, B)
    tile_count = vectors[0].shape[0] // LANES
    *leaving, sums = pl.pallas_call(
        functools.partial(
            mix_kernel, parts=len(parts), tile=tile, tile_count=tile_count, rotated=rotated
        ),
        grid=(tiles, steps),
        in_specs=[pl.BlockSpec(memory_space=pltpu.SMEM)] * 4
        + part_specs(devices, rotated, block, tok_at)
        + part_specs(devices, rotated, block, cot_at)
        + [whole(f) for f in factors]
        + [pl.BlockSpec(memory_space=pl.ANY)] * len(after),
        out_specs=part_specs(devices, rotated, block, lambda t, i: (t * steps + i, 0, 0))
        + [pl.BlockSpec((sum_rows, LANES), lambda t, i: (0, 0))],
        out_shape=part_shapes(devices, rotated, (tiles * share, rows, B))
        + [jax.ShapeDtypeStruct((sum_rows, LANES), jnp.float32)],
        scratch_shapes=[pltpu.VMEM((A, pair * B), jnp.float32)] * 2,
        compiler_params=pltpu.CompilerParams(vmem_limit_bytes=VMEM_BYTES),
        cost_estimate=pl.CostEstimate(flops=tiles * share * A * B * 16000, bytes_accessed=1024, transcendentals=0),
    )(place, *vectors, *parts, *parts, *factors, *after)
    return leaving, sums


def add_kernel(*refs, count):
    total = refs[0][...]
    for ref in refs[1:count]:
        total += ref[...]
    refs[-1][...] = total


def add(terms, after):
    vmem = pl.BlockSpec(memory_space=pltpu.VMEM)
    return pl.pallas_call(
        functools.partial(add_kernel, count=len(terms)),
        in_specs=[vmem] * len(terms) + [pl.BlockSpec(memory_space=pl.ANY)] * len(after),
        out_specs=vmem,
        out_shape=jax.ShapeDtypeStruct(terms[0].shape, terms[0].dtype),
        cost_estimate=pl.CostEstimate(flops=1, bytes_accessed=1024, transcendentals=0),
    )(*terms, *after)


def hold(arrays, after):
    anywhere = pl.BlockSpec(memory_space=pl.ANY)
    return pl.pallas_call(
        lambda *refs: None,
        in_specs=[anywhere] * (len(arrays) + len(after)),
        out_specs=[anywhere] * len(arrays),
        out_shape=[jax.ShapeDtypeStruct(a.shape, a.dtype) for a in arrays],
        input_output_aliases={i: i for i in range(len(arrays))},
        cost_estimate=pl.CostEstimate(flops=1, bytes_accessed=1024, transcendentals=0),
    )(*arrays, *after)


def block_diagonal(square, count):
    zero = jnp.zeros_like(square)
    return jnp.concatenate(
        [
            jnp.concatenate([square if i == j else zero for j in range(count)], axis=1)
            for i in range(count)
        ],
        axis=0,
    )


def sum_over_mesh(sums, beside):
    beside = [None, *beside]

    def exchange_with(array, axis, bit):
        after = beside.pop(0) if beside else None
        if after is not None:
            (array,) = hold([array], after)
        size = lax.axis_size(axis)
        return array, lax.ppermute(array, axis, [(i, i ^ bit) for i in range(size)])

    dp = lax.axis_index("dp")
    bits = [1 << k for k in range(lax.axis_size("dp").bit_length() - 1)]
    for bit in reversed(bits):
        halves = sums.reshape(2, -1, LANES)
        high = (dp & bit) != 0
        _, other = exchange_with(jnp.where(high, halves[0], halves[1]), "dp", bit)
        sums = jnp.where(high, halves[1], halves[0]) + other
    bit = 1
    while bit < lax.axis_size("ctx"):
        sums, other = exchange_with(sums, "ctx", bit)
        sums = sums + other
        bit *= 2
    for bit in bits:
        sums, other = exchange_with(sums, "dp", bit)
        high = (dp & bit) != 0
        sums = jnp.concatenate([jnp.where(high, other, sums), jnp.where(high, sums, other)])
    return sums


def body(tokens, cotangent, first_factor, second_factor, twiddle, gate_gain, gate_bias, skip_gain):
    seq_count, tok_rows, width = tokens.shape
    ctx_size = lax.axis_size("ctx")
    dp_size = lax.axis_size("dp")
    share = LANES // ctx_size
    local_rows = tok_rows // B
    tiles = width // LANES
    pair = 2
    half = tiles // 2
    groups = [(0, 1, True), (1, half - 1, False), (half, tiles - half, True)]

    place = (lax.axis_index("ctx") * share).astype(jnp.int32).reshape(1)
    second = block_diagonal(second_factor, pair)
    second_t = block_diagonal(second_factor.T, pair)
    vectors = [gate_gain, gate_bias, skip_gain]
    used_rows = CHANNEL_AT + 3 * tiles
    sum_rows = -(-used_rows // (8 * dp_size)) * 8 * dp_size

    def exchange(parts, sign, rotated):
        if not rotated:
            return [lax.all_to_all(parts[0], "ctx", split_axis=0, concat_axis=0, tiled=True)]
        moved = [parts[0]]
        for shift in range(1, ctx_size):
            pairs = [(i, (i + sign * shift) % ctx_size) for i in range(ctx_size)]
            moved.append(lax.ppermute(parts[shift], "ctx", pairs))
        return moved

    terms = []
    leaving = []
    for seq in range(seq_count):
        tok_blocks = tokens[seq].reshape(local_rows, B, width)
        cot_blocks = cotangent[seq].reshape(local_rows, B, width)
        split = []
        for at, count, rotated in groups:
            own = twiddle if at == 0 else None
            split.append(
                split_channels(place, tok_blocks, cot_blocks, at, count, ctx_size, rotated, own)
            )
        arrived = [exchange(p, 1, group[2]) for p, group in zip(split, groups)]
        planes = jnp.stack([part[2 * share :] for part in arrived[0]]).astype(jnp.float32)
        planes = planes[:, 0] + planes[:, 1] + planes[:, 2]
        twice = jnp.concatenate([planes[::-1]] * 2, axis=0)
        turn = ctx_size - 1 - lax.axis_index("ctx")
        twiddle_all = lax.dynamic_slice_in_dim(twice, turn, ctx_size, 0).reshape(A, B)
        factors = [first_factor, first_factor.T, second, second_t, twiddle_all]
        returned = []
        for which, (at, count, rotated) in enumerate(groups):
            parts, own_sums = mix(
                arrived[which], at, count, 2 * share, place, vectors, factors, sum_rows, ctx_size,
                rotated, [],
            )
            if which == 1:
                parts = hold(parts, arrived[2][1:])
            returned.append(exchange(parts, -1, rotated))
            terms.append(own_sums)
        leaving.append(returned)

    back, first = leaving[-1][2], leaving[-1][0]
    sums = sum_over_mesh(add(terms, []), [None, back[-2:], back[1:2], back[2:4], back[4:-2], first[1:4]])
    grads = []
    for returned in leaving:
        held = None
        for which in (1, 2, 0):
            at, count, rotated = groups[which]
            after = []
            held = merge_channels(
                place, returned[which], held, at, count, ctx_size, rotated, width, after
            )
        grads.append(held.reshape(tok_rows, width))
    grad_tokens = jnp.stack(grads)

    total_seqs = seq_count * dp_size
    first_norm = math.sqrt(total_seqs * B * width)
    second_norm = math.sqrt(total_seqs * A * width)
    twiddle_norm = math.sqrt(total_seqs * width)
    channel_norm = math.sqrt(total_seqs * A * B)
    first_sum = jnp.concatenate([sums[half * A : (half + 1) * A] for half in range(A // B)], axis=1)
    mine = TWIDDLE_AT + lax.axis_index("ctx") * local_rows
    twiddle_sum = lax.dynamic_slice_in_dim(sums, mine, local_rows, 0)
    channel_sum = sums[CHANNEL_AT:used_rows].reshape(3, width)
    return (
        grad_tokens,
        first_sum / first_norm,
        sums[SECOND_AT:TWIDDLE_AT] / second_norm,
        twiddle_sum / twiddle_norm,
        channel_sum[0] / channel_norm,
        channel_sum[1] / channel_norm,
        channel_sum[2] / channel_norm,
    )


def solution(mesh):
    return jax.shard_map(
        body,
        mesh=mesh,
        in_specs=(
            P("dp", "ctx", None),
            P("dp", "ctx", None),
            P(),
            P(),
            P("ctx", None),
            P(),
            P(),
            P(),
        ),
        out_specs=(P("dp", "ctx", None), P(), P(), P("ctx", None), P(), P(), P()),
        check_vma=False,
    )
```

```python
import functools
import math

import jax
import jax.numpy as jnp
from jax import lax
from jax.experimental import pallas as pl
from jax.experimental.pallas import tpu as pltpu
from jax.sharding import PartitionSpec as P

A = 256
B = 128
LANES = 128
VMEM_BYTES = 48 * 1024 * 1024


def dot(left, right, left_dim, right_dim):
    return lax.dot_general(
        left, right, (((left_dim,), (right_dim,)), ((), ())), preferred_element_type=jnp.float32
    )


def views(refs, rotated):
    return list(refs) if rotated else [refs[0].at[i] for i in range(refs[0].shape[0])]


def split_tile(first_channel, tok_ref, cot_ref, out_refs, swap_ref):
    rows = tok_ref.shape[0]
    share = LANES // len(out_refs)
    for which, ref in enumerate((tok_ref, cot_ref)):
        for row in range(rows):
            swap_ref[row * LANES : (row + 1) * LANES, :] = ref[row].astype(jnp.float32).T
        for slot, out_ref in enumerate(out_refs):
            start = (first_channel + slot * share) % LANES
            for channel in range(share):
                out_ref[which * share + channel] = swap_ref[
                    pl.ds(start + channel, rows, stride=LANES), :
                ].astype(jnp.bfloat16)


def split_kernel(place_ref, tok_ref, cot_ref, *rest, rotated):
    first_channel = place_ref[0] if rotated else 0
    split_tile(first_channel, tok_ref, cot_ref, views(rest[:-1], rotated), rest[-1])


def split_twiddle_kernel(place_ref, tok_ref, cot_ref, twiddle_ref, *rest, rotated):
    split_kernel(place_ref, tok_ref, cot_ref, *rest, rotated=rotated)
    out_refs = views(rest[:-1], rotated)
    share = LANES // len(out_refs)
    left = twiddle_ref[...]
    for plane in range(3):
        part = left.astype(jnp.bfloat16)
        left = left - part.astype(jnp.float32)
        for out_ref in out_refs:
            out_ref[2 * share + plane] = part


def part_specs(devices, rotated, block, index):
    if rotated:
        return [pl.BlockSpec(block, index)] * devices
    return [pl.BlockSpec((devices, *block), lambda *at: (0, *index(*at)))]


def part_shapes(devices, rotated, shape):
    if rotated:
        return [jax.ShapeDtypeStruct(shape, jnp.bfloat16)] * devices
    return [jax.ShapeDtypeStruct((devices, *shape), jnp.bfloat16)]


def split_channels(place, tokens, cotangent, tile, tiles, devices, rotated, twiddle=None):
    rows = tokens.shape[0]
    step = min(16, rows)
    share = LANES // devices
    block = pl.BlockSpec((step, B, LANES), lambda t, i: (i, 0, tile + t))
    specs = [pl.BlockSpec(memory_space=pltpu.SMEM), block, block]
    if twiddle is None:
        kernel, given = split_kernel, [place, tokens, cotangent]
        planes = 2 * share
    else:
        kernel, given = split_twiddle_kernel, [place, tokens, cotangent, twiddle]
        specs.append(pl.BlockSpec((step, B), lambda t, i: (i, 0)))
        planes = 2 * share + 3
    return pl.pallas_call(
        functools.partial(kernel, rotated=rotated),
        grid=(tiles, rows // step),
        in_specs=specs,
        out_specs=part_specs(devices, rotated, (planes, step, B), lambda t, i: (t, i, 0)),
        out_shape=part_shapes(devices, rotated, (tiles * planes, rows, B)),
        scratch_shapes=[pltpu.VMEM((step * LANES, B), jnp.float32)],
        compiler_params=pltpu.CompilerParams(vmem_limit_bytes=VMEM_BYTES),
        cost_estimate=pl.CostEstimate(flops=1, bytes_accessed=16 * rows * B * LANES * tiles, transcendentals=0),
    )(*given)


def merge_kernel(place_ref, *rest, parts, rotated):
    part_refs, out_ref, swap_ref = views(rest[:parts], rotated), rest[-2], rest[-1]
    share, rows, _ = part_refs[0].shape
    for slot, part_ref in enumerate(part_refs):
        start = (place_ref[0] + slot * share) % LANES if rotated else slot * share
        for channel in range(share):
            at = pl.multiple_of((start + channel) * rows, rows)
            swap_ref[pl.ds(at, rows), :] = part_ref[channel].astype(jnp.float32)
    for row in range(rows):
        out_ref[row] = swap_ref[pl.ds(row, LANES, stride=rows), :].T.astype(jnp.bfloat16)


def merge_channels(place, parts, held, tile, tiles, devices, rotated, width, after):
    rows = parts[0].shape[-2]
    step = min(16, rows)
    share = LANES // devices
    given = [place, *parts]
    specs = [pl.BlockSpec(memory_space=pltpu.SMEM)]
    specs += part_specs(devices, rotated, (share, step, B), lambda t, i: (t, i, 0))
    for array in after if held is None else [held, *after]:
        given.append(array)
        specs.append(pl.BlockSpec(memory_space=pl.ANY))
    return pl.pallas_call(
        functools.partial(merge_kernel, parts=len(parts), rotated=rotated),
        grid=(tiles, rows // step),
        in_specs=specs,
        out_specs=pl.BlockSpec((step, B, LANES), lambda t, i: (i, 0, tile + t)),
        out_shape=jax.ShapeDtypeStruct((rows, B, width), jnp.bfloat16),
        scratch_shapes=[pltpu.VMEM((step * LANES, B), jnp.float32)],
        input_output_aliases={} if held is None else {len(parts) + 1: 0},
        compiler_params=pltpu.CompilerParams(vmem_limit_bytes=VMEM_BYTES),
        cost_estimate=pl.CostEstimate(flops=1, bytes_accessed=8 * rows * B * LANES * tiles, transcendentals=0),
    )(*given)


SECOND_AT = 2 * A
TWIDDLE_AT = SECOND_AT + B
CHANNEL_AT = TWIDDLE_AT + A


def mix_kernel(
    place_ref, gain_ref, bias_ref, skip_ref, *rest, parts, tile, tile_count, rotated
):
    tok_refs = views(rest[:parts], rotated)
    cot_refs = views(rest[parts : 2 * parts], rotated)
    first_ref, first_t_ref, second_ref, second_t_ref, twiddle_ref = rest[2 * parts : 2 * parts + 5]
    out_refs = views(rest[-3 - parts : -3], rotated)
    sums_ref, tok_all, cot_all = rest[-3:]
    t, step = pl.program_id(0), pl.program_id(1)

    @pl.when((t == 0) & (step == 0))
    def _():
        sums_ref[...] = jnp.zeros(sums_ref.shape, jnp.float32)

    devices = len(tok_refs)
    pair, rows, _ = tok_refs[0].shape
    share = LANES // devices
    lane_at = place_ref[0] + step * pair
    at = (tile + t) * LANES + lane_at

    def rows_from(shift):
        if not rotated:
            return slice(shift * rows, (shift + 1) * rows)
        source = (place_ref[0] // share - shift + devices) % devices
        return pl.ds(pl.multiple_of(source * rows, rows), rows)

    for refs, whole in ((tok_refs, tok_all), (cot_refs, cot_all)):
        for shift, ref in enumerate(refs):
            for c in range(pair):
                whole[rows_from(shift), c * B : (c + 1) * B] = ref[c].astype(jnp.float32)

    def spread(ref):
        lane = lax.broadcasted_iota(jnp.int32, (1, pair * B), 1)
        row = jnp.full((1, pair * B), ref[at], jnp.float32)
        for c in range(1, pair):
            row = jnp.where(lane >= c * B, ref[at + c], row)
        return row

    gain, bias, skip = spread(gain_ref), spread(bias_ref), spread(skip_ref)
    inputs = tok_all[...]
    tok = inputs.astype(jnp.bfloat16)
    upstream = cot_all[...]
    twiddle = jnp.concatenate([twiddle_ref[...]] * pair, axis=1)
    inner = dot(tok, second_t_ref[...], 1, 0)
    scaled = (inner * twiddle).astype(jnp.bfloat16)
    gate = jax.nn.sigmoid(gain * inputs + bias)
    grad_hidden = upstream * gate
    grad_outer = grad_hidden.astype(jnp.bfloat16)
    outer = dot(first_ref[...], scaled, 1, 0).astype(jnp.bfloat16).astype(jnp.float32)
    grad_scaled = dot(first_t_ref[...], grad_outer, 1, 0).astype(jnp.bfloat16).astype(jnp.float32)
    first_term = dot(grad_outer, scaled, 1, 1)
    for half in range(A // B):
        sums_ref[half * A : (half + 1) * A] += first_term[:, half * B : (half + 1) * B]
    hidden = outer + skip * inputs
    grad_pre = upstream * hidden * gate * (1.0 - gate)
    product = grad_scaled * inner
    sums_ref[TWIDDLE_AT:CHANNEL_AT] += sum(product[:, c * B : (c + 1) * B] for c in range(pair))
    grad_inner = (grad_scaled * twiddle).astype(jnp.bfloat16)
    second_term = dot(grad_inner, tok, 0, 0)
    sums_ref[SECOND_AT:TWIDDLE_AT] += sum(
        second_term[c * B : (c + 1) * B, c * B : (c + 1) * B] for c in range(pair)
    )
    lane = lax.broadcasted_iota(jnp.int32, (1, LANES), 1)
    for which, value in enumerate((grad_pre * inputs, grad_pre, grad_hidden * inputs)):
        total = jnp.sum(value, axis=0, keepdims=True)
        row = jnp.zeros((1, LANES), jnp.float32)
        for c in range(pair):
            channel = jnp.sum(total[:, c * B : (c + 1) * B], axis=1, keepdims=True)
            row = jnp.where(lane == lane_at + c, channel, row)
        sums_ref[pl.ds(CHANNEL_AT + which * tile_count + tile + t, 1), :] += row
    grad_in = dot(grad_inner, second_ref[...], 1, 0)
    tok_all[...] = grad_in + grad_hidden * skip + grad_pre * gain
    for shift, out_ref in enumerate(out_refs):
        for c in range(pair):
            out_ref[c] = tok_all[rows_from(shift), c * B : (c + 1) * B].astype(jnp.bfloat16)


def mix(parts, tile, tiles, planes, place, vectors, factors, sum_rows, devices, rotated, after):
    rows = parts[0].shape[-2]
    share = LANES // devices
    pair = factors[2].shape[0] // B
    steps = share // pair
    whole = lambda array: pl.BlockSpec(array.shape, lambda t, i: (0,) * array.ndim)
    tok_at = lambda t, i: (t * (planes // pair) + i, 0, 0)
    cot_at = lambda t, i: (t * (planes // pair) + steps + i, 0, 0)
    block = (pair, rows, B)
    tile_count = vectors[0].shape[0] // LANES
    *leaving, sums = pl.pallas_call(
        functools.partial(
            mix_kernel, parts=len(parts), tile=tile, tile_count=tile_count, rotated=rotated
        ),
        grid=(tiles, steps),
        in_specs=[pl.BlockSpec(memory_space=pltpu.SMEM)] * 4
        + part_specs(devices, rotated, block, tok_at)
        + part_specs(devices, rotated, block, cot_at)
        + [whole(f) for f in factors]
        + [pl.BlockSpec(memory_space=pl.ANY)] * len(after),
        out_specs=part_specs(devices, rotated, block, lambda t, i: (t * steps + i, 0, 0))
        + [pl.BlockSpec((sum_rows, LANES), lambda t, i: (0, 0))],
        out_shape=part_shapes(devices, rotated, (tiles * share, rows, B))
        + [jax.ShapeDtypeStruct((sum_rows, LANES), jnp.float32)],
        scratch_shapes=[pltpu.VMEM((A, pair * B), jnp.float32)] * 2,
        compiler_params=pltpu.CompilerParams(vmem_limit_bytes=VMEM_BYTES),
        cost_estimate=pl.CostEstimate(flops=tiles * share * A * B * 16000, bytes_accessed=1024, transcendentals=0),
    )(place, *vectors, *parts, *parts, *factors, *after)
    return leaving, sums


def add_kernel(*refs, count):
    total = refs[0][...]
    for ref in refs[1:count]:
        total += ref[...]
    refs[-1][...] = total


def add(terms, after):
    vmem = pl.BlockSpec(memory_space=pltpu.VMEM)
    return pl.pallas_call(
        functools.partial(add_kernel, count=len(terms)),
        in_specs=[vmem] * len(terms) + [pl.BlockSpec(memory_space=pl.ANY)] * len(after),
        out_specs=vmem,
        out_shape=jax.ShapeDtypeStruct(terms[0].shape, terms[0].dtype),
        cost_estimate=pl.CostEstimate(flops=1, bytes_accessed=1024, transcendentals=0),
    )(*terms, *after)


def hold(arrays, after):
    anywhere = pl.BlockSpec(memory_space=pl.ANY)
    return pl.pallas_call(
        lambda *refs: None,
        in_specs=[anywhere] * (len(arrays) + len(after)),
        out_specs=[anywhere] * len(arrays),
        out_shape=[jax.ShapeDtypeStruct(a.shape, a.dtype) for a in arrays],
        input_output_aliases={i: i for i in range(len(arrays))},
        cost_estimate=pl.CostEstimate(flops=1, bytes_accessed=1024, transcendentals=0),
    )(*arrays, *after)


def block_diagonal(square, count):
    zero = jnp.zeros_like(square)
    return jnp.concatenate(
        [
            jnp.concatenate([square if i == j else zero for j in range(count)], axis=1)
            for i in range(count)
        ],
        axis=0,
    )


def sum_over_mesh(sums, beside):
    beside = [None, *beside]

    def exchange_with(array, axis, bit):
        after = beside.pop(0) if beside else None
        if after is not None:
            (array,) = hold([array], after)
        size = lax.axis_size(axis)
        return array, lax.ppermute(array, axis, [(i, i ^ bit) for i in range(size)])

    dp = lax.axis_index("dp")
    bits = [1 << k for k in range(lax.axis_size("dp").bit_length() - 1)]
    for bit in reversed(bits):
        halves = sums.reshape(2, -1, LANES)
        high = (dp & bit) != 0
        _, other = exchange_with(jnp.where(high, halves[0], halves[1]), "dp", bit)
        sums = jnp.where(high, halves[1], halves[0]) + other
    bit = 1
    while bit < lax.axis_size("ctx"):
        sums, other = exchange_with(sums, "ctx", bit)
        sums = sums + other
        bit *= 2
    for bit in bits:
        sums, other = exchange_with(sums, "dp", bit)
        high = (dp & bit) != 0
        sums = jnp.concatenate([jnp.where(high, other, sums), jnp.where(high, sums, other)])
    return sums


def body(tokens, cotangent, first_factor, second_factor, twiddle, gate_gain, gate_bias, skip_gain):
    seq_count, tok_rows, width = tokens.shape
    ctx_size = lax.axis_size("ctx")
    dp_size = lax.axis_size("dp")
    share = LANES // ctx_size
    local_rows = tok_rows // B
    tiles = width // LANES
    pair = 2
    half = tiles // 2
    groups = [(0, 1, True), (1, half - 1, False), (half, tiles - half, True)]

    place = (lax.axis_index("ctx") * share).astype(jnp.int32).reshape(1)
    second = block_diagonal(second_factor, pair)
    second_t = block_diagonal(second_factor.T, pair)
    vectors = [gate_gain, gate_bias, skip_gain]
    used_rows = CHANNEL_AT + 3 * tiles
    sum_rows = -(-used_rows // (8 * dp_size)) * 8 * dp_size

    def exchange(parts, sign, rotated):
        if not rotated:
            return [lax.all_to_all(parts[0], "ctx", split_axis=0, concat_axis=0, tiled=True)]
        moved = [parts[0]]
        for shift in range(1, ctx_size):
            pairs = [(i, (i + sign * shift) % ctx_size) for i in range(ctx_size)]
            moved.append(lax.ppermute(parts[shift], "ctx", pairs))
        return moved

    terms = []
    leaving = []
    for seq in range(seq_count):
        tok_blocks = tokens[seq].reshape(local_rows, B, width)
        cot_blocks = cotangent[seq].reshape(local_rows, B, width)
        split = []
        for at, count, rotated in groups:
            own = twiddle if at == 0 else None
            split.append(
                split_channels(place, tok_blocks, cot_blocks, at, count, ctx_size, rotated, own)
            )
        arrived = [exchange(p, 1, group[2]) for p, group in zip(split, groups)]
        planes = jnp.stack([part[2 * share :] for part in arrived[0]]).astype(jnp.float32)
        planes = planes[:, 0] + planes[:, 1] + planes[:, 2]
        twice = jnp.concatenate([planes[::-1]] * 2, axis=0)
        turn = ctx_size - 1 - lax.axis_index("ctx")
        twiddle_all = lax.dynamic_slice_in_dim(twice, turn, ctx_size, 0).reshape(A, B)
        factors = [first_factor, first_factor.T, second, second_t, twiddle_all]
        returned = []
        released = []
        for which, (at, count, rotated) in enumerate(groups):
            parts, own_sums = mix(
                arrived[which], at, count, 2 * share, place, vectors, factors, sum_rows, ctx_size,
                rotated, released if which == 2 else [],
            )
            if which == 1:
                parts = released = hold(parts, arrived[2][1:])
            returned.append(exchange(parts, -1, rotated))
            terms.append(own_sums)
        leaving.append(returned)

    back, first = leaving[-1][2], leaving[-1][0]
    sums = sum_over_mesh(add(terms, []), [None, back[-2:], back[1:2], back[2:3], back[3:-2], first[1:3]])
    grads = []
    for returned in leaving:
        held = None
        for which in (1, 2, 0):
            at, count, rotated = groups[which]
            after = []
            held = merge_channels(
                place, returned[which], held, at, count, ctx_size, rotated, width, after
            )
        grads.append(held.reshape(tok_rows, width))
    grad_tokens = jnp.stack(grads)

    total_seqs = seq_count * dp_size
    first_norm = math.sqrt(total_seqs * B * width)
    second_norm = math.sqrt(total_seqs * A * width)
    twiddle_norm = math.sqrt(total_seqs * width)
    channel_norm = math.sqrt(total_seqs * A * B)
    first_sum = jnp.concatenate([sums[half * A : (half + 1) * A] for half in range(A // B)], axis=1)
    mine = TWIDDLE_AT + lax.axis_index("ctx") * local_rows
    twiddle_sum = lax.dynamic_slice_in_dim(sums, mine, local_rows, 0)
    channel_sum = sums[CHANNEL_AT:used_rows].reshape(3, width)
    return (
        grad_tokens,
        first_sum / first_norm,
        sums[SECOND_AT:TWIDDLE_AT] / second_norm,
        twiddle_sum / twiddle_norm,
        channel_sum[0] / channel_norm,
        channel_sum[1] / channel_norm,
        channel_sum[2] / channel_norm,
    )


def solution(mesh):
    return jax.shard_map(
        body,
        mesh=mesh,
        in_specs=(
            P("dp", "ctx", None),
            P("dp", "ctx", None),
            P(),
            P(),
            P("ctx", None),
            P(),
            P(),
            P(),
        ),
        out_specs=(P("dp", "ctx", None), P(), P(), P("ctx", None), P(), P(), P()),
        check_vma=False,
    )
```

```python
import functools
import math

import jax
import jax.numpy as jnp
from jax import lax
from jax.experimental import pallas as pl
from jax.experimental.pallas import tpu as pltpu
from jax.sharding import PartitionSpec as P

A = 256
B = 128
LANES = 128
VMEM_BYTES = 48 * 1024 * 1024


def dot(left, right, left_dim, right_dim):
    return lax.dot_general(
        left, right, (((left_dim,), (right_dim,)), ((), ())), preferred_element_type=jnp.float32
    )


def views(refs, rotated):
    return list(refs) if rotated else [refs[0].at[i] for i in range(refs[0].shape[0])]


def split_tile(first_channel, tok_ref, cot_ref, out_refs, swap_ref):
    rows = tok_ref.shape[0]
    share = LANES // len(out_refs)
    for which, ref in enumerate((tok_ref, cot_ref)):
        for row in range(rows):
            swap_ref[row * LANES : (row + 1) * LANES, :] = ref[row].astype(jnp.float32).T
        for slot, out_ref in enumerate(out_refs):
            start = (first_channel + slot * share) % LANES
            for channel in range(share):
                out_ref[which * share + channel] = swap_ref[
                    pl.ds(start + channel, rows, stride=LANES), :
                ].astype(jnp.bfloat16)


def split_kernel(place_ref, tok_ref, cot_ref, *rest, rotated):
    first_channel = place_ref[0] if rotated else 0
    split_tile(first_channel, tok_ref, cot_ref, views(rest[:-1], rotated), rest[-1])


def split_twiddle_kernel(place_ref, tok_ref, cot_ref, twiddle_ref, *rest, rotated):
    split_kernel(place_ref, tok_ref, cot_ref, *rest, rotated=rotated)
    out_refs = views(rest[:-1], rotated)
    share = LANES // len(out_refs)
    left = twiddle_ref[...]
    for plane in range(3):
        part = left.astype(jnp.bfloat16)
        left = left - part.astype(jnp.float32)
        for out_ref in out_refs:
            out_ref[2 * share + plane] = part


def part_specs(devices, rotated, block, index):
    if rotated:
        return [pl.BlockSpec(block, index)] * devices
    return [pl.BlockSpec((devices, *block), lambda *at: (0, *index(*at)))]


def part_shapes(devices, rotated, shape):
    if rotated:
        return [jax.ShapeDtypeStruct(shape, jnp.bfloat16)] * devices
    return [jax.ShapeDtypeStruct((devices, *shape), jnp.bfloat16)]


def split_channels(place, tokens, cotangent, tile, tiles, devices, rotated, twiddle=None):
    rows = tokens.shape[0]
    step = min(16, rows)
    share = LANES // devices
    block = pl.BlockSpec((step, B, LANES), lambda t, i: (i, 0, tile + t))
    specs = [pl.BlockSpec(memory_space=pltpu.SMEM), block, block]
    if twiddle is None:
        kernel, given = split_kernel, [place, tokens, cotangent]
        planes = 2 * share
    else:
        kernel, given = split_twiddle_kernel, [place, tokens, cotangent, twiddle]
        specs.append(pl.BlockSpec((step, B), lambda t, i: (i, 0)))
        planes = 2 * share + 3
    return pl.pallas_call(
        functools.partial(kernel, rotated=rotated),
        grid=(tiles, rows // step),
        in_specs=specs,
        out_specs=part_specs(devices, rotated, (planes, step, B), lambda t, i: (t, i, 0)),
        out_shape=part_shapes(devices, rotated, (tiles * planes, rows, B)),
        scratch_shapes=[pltpu.VMEM((step * LANES, B), jnp.float32)],
        compiler_params=pltpu.CompilerParams(vmem_limit_bytes=VMEM_BYTES),
        cost_estimate=pl.CostEstimate(flops=1, bytes_accessed=16 * rows * B * LANES * tiles, transcendentals=0),
    )(*given)


def merge_kernel(place_ref, *rest, parts, rotated):
    part_refs, out_ref, swap_ref = views(rest[:parts], rotated), rest[-2], rest[-1]
    share, rows, _ = part_refs[0].shape
    for slot, part_ref in enumerate(part_refs):
        start = (place_ref[0] + slot * share) % LANES if rotated else slot * share
        for channel in range(share):
            at = pl.multiple_of((start + channel) * rows, rows)
            swap_ref[pl.ds(at, rows), :] = part_ref[channel].astype(jnp.float32)
    for row in range(rows):
        out_ref[row] = swap_ref[pl.ds(row, LANES, stride=rows), :].T.astype(jnp.bfloat16)


def merge_channels(place, parts, held, tile, tiles, devices, rotated, width, after):
    rows = parts[0].shape[-2]
    step = min(16, rows)
    share = LANES // devices
    given = [place, *parts]
    specs = [pl.BlockSpec(memory_space=pltpu.SMEM)]
    specs += part_specs(devices, rotated, (share, step, B), lambda t, i: (t, i, 0))
    for array in after if held is None else [held, *after]:
        given.append(array)
        specs.append(pl.BlockSpec(memory_space=pl.ANY))
    return pl.pallas_call(
        functools.partial(merge_kernel, parts=len(parts), rotated=rotated),
        grid=(tiles, rows // step),
        in_specs=specs,
        out_specs=pl.BlockSpec((step, B, LANES), lambda t, i: (i, 0, tile + t)),
        out_shape=jax.ShapeDtypeStruct((rows, B, width), jnp.bfloat16),
        scratch_shapes=[pltpu.VMEM((step * LANES, B), jnp.float32)],
        input_output_aliases={} if held is None else {len(parts) + 1: 0},
        compiler_params=pltpu.CompilerParams(vmem_limit_bytes=VMEM_BYTES),
        cost_estimate=pl.CostEstimate(flops=1, bytes_accessed=8 * rows * B * LANES * tiles, transcendentals=0),
    )(*given)


SECOND_AT = 2 * A
TWIDDLE_AT = SECOND_AT + B
CHANNEL_AT = TWIDDLE_AT + A


def mix_kernel(
    place_ref, gain_ref, bias_ref, skip_ref, *rest, parts, tile, tile_count, rotated
):
    tok_refs = views(rest[:parts], rotated)
    cot_refs = views(rest[parts : 2 * parts], rotated)
    first_ref, first_t_ref, second_ref, second_t_ref, twiddle_ref = rest[2 * parts : 2 * parts + 5]
    out_refs = views(rest[-3 - parts : -3], rotated)
    sums_ref, tok_all, cot_all = rest[-3:]
    t, step = pl.program_id(0), pl.program_id(1)

    @pl.when((t == 0) & (step == 0))
    def _():
        sums_ref[...] = jnp.zeros(sums_ref.shape, jnp.float32)

    devices = len(tok_refs)
    pair, rows, _ = tok_refs[0].shape
    share = LANES // devices
    lane_at = place_ref[0] + step * pair
    at = (tile + t) * LANES + lane_at

    def rows_from(shift):
        if not rotated:
            return slice(shift * rows, (shift + 1) * rows)
        source = (place_ref[0] // share - shift + devices) % devices
        return pl.ds(pl.multiple_of(source * rows, rows), rows)

    for refs, whole in ((tok_refs, tok_all), (cot_refs, cot_all)):
        for shift, ref in enumerate(refs):
            for c in range(pair):
                whole[rows_from(shift), c * B : (c + 1) * B] = ref[c].astype(jnp.float32)

    def spread(ref):
        lane = lax.broadcasted_iota(jnp.int32, (1, pair * B), 1)
        row = jnp.full((1, pair * B), ref[at], jnp.float32)
        for c in range(1, pair):
            row = jnp.where(lane >= c * B, ref[at + c], row)
        return row

    gain, bias, skip = spread(gain_ref), spread(bias_ref), spread(skip_ref)
    inputs = tok_all[...]
    tok = inputs.astype(jnp.bfloat16)
    upstream = cot_all[...]
    twiddle = jnp.concatenate([twiddle_ref[...]] * pair, axis=1)
    inner = dot(tok, second_t_ref[...], 1, 0)
    scaled = (inner * twiddle).astype(jnp.bfloat16)
    gate = jax.nn.sigmoid(gain * inputs + bias)
    grad_hidden = upstream * gate
    grad_outer = grad_hidden.astype(jnp.bfloat16)
    outer = dot(first_ref[...], scaled, 1, 0).astype(jnp.bfloat16).astype(jnp.float32)
    grad_scaled = dot(first_t_ref[...], grad_outer, 1, 0).astype(jnp.bfloat16).astype(jnp.float32)
    first_term = dot(grad_outer, scaled, 1, 1)
    for half in range(A // B):
        sums_ref[half * A : (half + 1) * A] += first_term[:, half * B : (half + 1) * B]
    hidden = outer + skip * inputs
    grad_pre = upstream * hidden * gate * (1.0 - gate)
    product = grad_scaled * inner
    sums_ref[TWIDDLE_AT:CHANNEL_AT] += sum(product[:, c * B : (c + 1) * B] for c in range(pair))
    grad_inner = (grad_scaled * twiddle).astype(jnp.bfloat16)
    second_term = dot(grad_inner, tok, 0, 0)
    sums_ref[SECOND_AT:TWIDDLE_AT] += sum(
        second_term[c * B : (c + 1) * B, c * B : (c + 1) * B] for c in range(pair)
    )
    lane = lax.broadcasted_iota(jnp.int32, (1, LANES), 1)
    for which, value in enumerate((grad_pre * inputs, grad_pre, grad_hidden * inputs)):
        total = jnp.sum(value, axis=0, keepdims=True)
        row = jnp.zeros((1, LANES), jnp.float32)
        for c in range(pair):
            channel = jnp.sum(total[:, c * B : (c + 1) * B], axis=1, keepdims=True)
            row = jnp.where(lane == lane_at + c, channel, row)
        sums_ref[pl.ds(CHANNEL_AT + which * tile_count + tile + t, 1), :] += row
    grad_in = dot(grad_inner, second_ref[...], 1, 0)
    tok_all[...] = grad_in + grad_hidden * skip + grad_pre * gain
    for shift, out_ref in enumerate(out_refs):
        for c in range(pair):
            out_ref[c] = tok_all[rows_from(shift), c * B : (c + 1) * B].astype(jnp.bfloat16)


def mix(parts, tile, tiles, planes, place, vectors, factors, sum_rows, devices, rotated, after):
    rows = parts[0].shape[-2]
    share = LANES // devices
    pair = factors[2].shape[0] // B
    steps = share // pair
    whole = lambda array: pl.BlockSpec(array.shape, lambda t, i: (0,) * array.ndim)
    tok_at = lambda t, i: (t * (planes // pair) + i, 0, 0)
    cot_at = lambda t, i: (t * (planes // pair) + steps + i, 0, 0)
    block = (pair, rows, B)
    tile_count = vectors[0].shape[0] // LANES
    *leaving, sums = pl.pallas_call(
        functools.partial(
            mix_kernel, parts=len(parts), tile=tile, tile_count=tile_count, rotated=rotated
        ),
        grid=(tiles, steps),
        in_specs=[pl.BlockSpec(memory_space=pltpu.SMEM)] * 4
        + part_specs(devices, rotated, block, tok_at)
        + part_specs(devices, rotated, block, cot_at)
        + [whole(f) for f in factors]
        + [pl.BlockSpec(memory_space=pl.ANY)] * len(after),
        out_specs=part_specs(devices, rotated, block, lambda t, i: (t * steps + i, 0, 0))
        + [pl.BlockSpec((sum_rows, LANES), lambda t, i: (0, 0))],
        out_shape=part_shapes(devices, rotated, (tiles * share, rows, B))
        + [jax.ShapeDtypeStruct((sum_rows, LANES), jnp.float32)],
        scratch_shapes=[pltpu.VMEM((A, pair * B), jnp.float32)] * 2,
        compiler_params=pltpu.CompilerParams(vmem_limit_bytes=VMEM_BYTES),
        cost_estimate=pl.CostEstimate(flops=tiles * share * A * B * 16000, bytes_accessed=1024, transcendentals=0),
    )(place, *vectors, *parts, *parts, *factors, *after)
    return leaving, sums


def add_kernel(*refs, count):
    total = refs[0][...]
    for ref in refs[1:count]:
        total += ref[...]
    refs[-1][...] = total


def add(terms, after):
    vmem = pl.BlockSpec(memory_space=pltpu.VMEM)
    return pl.pallas_call(
        functools.partial(add_kernel, count=len(terms)),
        in_specs=[vmem] * len(terms) + [pl.BlockSpec(memory_space=pl.ANY)] * len(after),
        out_specs=vmem,
        out_shape=jax.ShapeDtypeStruct(terms[0].shape, terms[0].dtype),
        cost_estimate=pl.CostEstimate(flops=1, bytes_accessed=1024, transcendentals=0),
    )(*terms, *after)


def hold(arrays, after):
    anywhere = pl.BlockSpec(memory_space=pl.ANY)
    return pl.pallas_call(
        lambda *refs: None,
        in_specs=[anywhere] * (len(arrays) + len(after)),
        out_specs=[anywhere] * len(arrays),
        out_shape=[jax.ShapeDtypeStruct(a.shape, a.dtype) for a in arrays],
        input_output_aliases={i: i for i in range(len(arrays))},
        cost_estimate=pl.CostEstimate(flops=1, bytes_accessed=1024, transcendentals=0),
    )(*arrays, *after)


def block_diagonal(square, count):
    zero = jnp.zeros_like(square)
    return jnp.concatenate(
        [
            jnp.concatenate([square if i == j else zero for j in range(count)], axis=1)
            for i in range(count)
        ],
        axis=0,
    )


def sum_over_mesh(sums, beside):
    beside = [None, *beside]

    def exchange_with(array, axis, bit):
        after = beside.pop(0) if beside else None
        if after is not None:
            (array,) = hold([array], after)
        size = lax.axis_size(axis)
        return array, lax.ppermute(array, axis, [(i, i ^ bit) for i in range(size)])

    dp = lax.axis_index("dp")
    bits = [1 << k for k in range(lax.axis_size("dp").bit_length() - 1)]
    for bit in reversed(bits):
        halves = sums.reshape(2, -1, LANES)
        high = (dp & bit) != 0
        _, other = exchange_with(jnp.where(high, halves[0], halves[1]), "dp", bit)
        sums = jnp.where(high, halves[1], halves[0]) + other
    bit = 1
    while bit < lax.axis_size("ctx"):
        sums, other = exchange_with(sums, "ctx", bit)
        sums = sums + other
        bit *= 2
    for bit in bits:
        sums, other = exchange_with(sums, "dp", bit)
        high = (dp & bit) != 0
        sums = jnp.concatenate([jnp.where(high, other, sums), jnp.where(high, sums, other)])
    return sums


def body(tokens, cotangent, first_factor, second_factor, twiddle, gate_gain, gate_bias, skip_gain):
    seq_count, tok_rows, width = tokens.shape
    ctx_size = lax.axis_size("ctx")
    dp_size = lax.axis_size("dp")
    share = LANES // ctx_size
    local_rows = tok_rows // B
    tiles = width // LANES
    pair = 2
    half = tiles // 2
    groups = [(0, 1, True), (1, half - 1, False), (half, tiles - half, True)]

    place = (lax.axis_index("ctx") * share).astype(jnp.int32).reshape(1)
    second = block_diagonal(second_factor, pair)
    second_t = block_diagonal(second_factor.T, pair)
    vectors = [gate_gain, gate_bias, skip_gain]
    used_rows = CHANNEL_AT + 3 * tiles
    sum_rows = -(-used_rows // (8 * dp_size)) * 8 * dp_size

    def exchange(parts, sign, rotated):
        if not rotated:
            return [lax.all_to_all(parts[0], "ctx", split_axis=0, concat_axis=0, tiled=True)]
        moved = [parts[0]]
        for shift in range(1, ctx_size):
            pairs = [(i, (i + sign * shift) % ctx_size) for i in range(ctx_size)]
            moved.append(lax.ppermute(parts[shift], "ctx", pairs))
        return moved

    terms = []
    leaving = []
    for seq in range(seq_count):
        tok_blocks = tokens[seq].reshape(local_rows, B, width)
        cot_blocks = cotangent[seq].reshape(local_rows, B, width)
        split = []
        for at, count, rotated in groups:
            own = twiddle if at == 0 else None
            split.append(
                split_channels(place, tok_blocks, cot_blocks, at, count, ctx_size, rotated, own)
            )
        arrived = [exchange(p, 1, group[2]) for p, group in zip(split, groups)]
        planes = jnp.stack([part[2 * share :] for part in arrived[0]]).astype(jnp.float32)
        planes = planes[:, 0] + planes[:, 1] + planes[:, 2]
        twice = jnp.concatenate([planes[::-1]] * 2, axis=0)
        turn = ctx_size - 1 - lax.axis_index("ctx")
        twiddle_all = lax.dynamic_slice_in_dim(twice, turn, ctx_size, 0).reshape(A, B)
        factors = [first_factor, first_factor.T, second, second_t, twiddle_all]
        returned = []
        released = []
        for which, (at, count, rotated) in enumerate(groups):
            parts, own_sums = mix(
                arrived[which], at, count, 2 * share, place, vectors, factors, sum_rows, ctx_size,
                rotated, released if which == 2 else [],
            )
            if which == 1:
                parts = released = hold(parts, arrived[2][1:])
            returned.append(exchange(parts, -1, rotated))
            terms.append(own_sums)
        leaving.append(returned)

    back, first = leaving[-1][2], leaving[-1][0]
    sums = sum_over_mesh(add(terms, []), [None, back[-2:], back[1:2], back[2:3], back[3:-2] + first[3:6]])
    grads = []
    for returned in leaving:
        held = None
        for which in (1, 2, 0):
            at, count, rotated = groups[which]
            after = []
            held = merge_channels(
                place, returned[which], held, at, count, ctx_size, rotated, width, after
            )
        grads.append(held.reshape(tok_rows, width))
    grad_tokens = jnp.stack(grads)

    total_seqs = seq_count * dp_size
    first_norm = math.sqrt(total_seqs * B * width)
    second_norm = math.sqrt(total_seqs * A * width)
    twiddle_norm = math.sqrt(total_seqs * width)
    channel_norm = math.sqrt(total_seqs * A * B)
    first_sum = jnp.concatenate([sums[half * A : (half + 1) * A] for half in range(A // B)], axis=1)
    mine = TWIDDLE_AT + lax.axis_index("ctx") * local_rows
    twiddle_sum = lax.dynamic_slice_in_dim(sums, mine, local_rows, 0)
    channel_sum = sums[CHANNEL_AT:used_rows].reshape(3, width)
    return (
        grad_tokens,
        first_sum / first_norm,
        sums[SECOND_AT:TWIDDLE_AT] / second_norm,
        twiddle_sum / twiddle_norm,
        channel_sum[0] / channel_norm,
        channel_sum[1] / channel_norm,
        channel_sum[2] / channel_norm,
    )


def solution(mesh):
    return jax.shard_map(
        body,
        mesh=mesh,
        in_specs=(
            P("dp", "ctx", None),
            P("dp", "ctx", None),
            P(),
            P(),
            P("ctx", None),
            P(),
            P(),
            P(),
        ),
        out_specs=(P("dp", "ctx", None), P(), P(), P("ctx", None), P(), P(), P()),
        check_vma=False,
    )
```

```python
import functools
import math

import jax
import jax.numpy as jnp
from jax import lax
from jax.experimental import pallas as pl
from jax.experimental.pallas import tpu as pltpu
from jax.sharding import PartitionSpec as P

A = 256
B = 128
LANES = 128
VMEM_BYTES = 48 * 1024 * 1024


def dot(left, right, left_dim, right_dim):
    return lax.dot_general(
        left, right, (((left_dim,), (right_dim,)), ((), ())), preferred_element_type=jnp.float32
    )


def views(refs, rotated):
    return list(refs) if rotated else [refs[0].at[i] for i in range(refs[0].shape[0])]


def split_tile(first_channel, tok_ref, cot_ref, out_refs, swap_ref):
    rows = tok_ref.shape[0]
    share = LANES // len(out_refs)
    for which, ref in enumerate((tok_ref, cot_ref)):
        for row in range(rows):
            swap_ref[row * LANES : (row + 1) * LANES, :] = ref[row].astype(jnp.float32).T
        for slot, out_ref in enumerate(out_refs):
            start = (first_channel + slot * share) % LANES
            for channel in range(share):
                out_ref[which * share + channel] = swap_ref[
                    pl.ds(start + channel, rows, stride=LANES), :
                ].astype(jnp.bfloat16)


def split_kernel(place_ref, tok_ref, cot_ref, *rest, rotated):
    first_channel = place_ref[0] if rotated else 0
    split_tile(first_channel, tok_ref, cot_ref, views(rest[:-1], rotated), rest[-1])


def split_twiddle_kernel(place_ref, tok_ref, cot_ref, twiddle_ref, *rest, rotated):
    split_kernel(place_ref, tok_ref, cot_ref, *rest, rotated=rotated)
    out_refs = views(rest[:-1], rotated)
    share = LANES // len(out_refs)
    left = twiddle_ref[...]
    for plane in range(3):
        part = left.astype(jnp.bfloat16)
        left = left - part.astype(jnp.float32)
        for out_ref in out_refs:
            out_ref[2 * share + plane] = part


def part_specs(devices, rotated, block, index):
    if rotated:
        return [pl.BlockSpec(block, index)] * devices
    return [pl.BlockSpec((devices, *block), lambda *at: (0, *index(*at)))]


def part_shapes(devices, rotated, shape):
    if rotated:
        return [jax.ShapeDtypeStruct(shape, jnp.bfloat16)] * devices
    return [jax.ShapeDtypeStruct((devices, *shape), jnp.bfloat16)]


def split_channels(place, tokens, cotangent, tile, tiles, devices, rotated, twiddle=None):
    rows = tokens.shape[0]
    step = min(16, rows)
    share = LANES // devices
    block = pl.BlockSpec((step, B, LANES), lambda t, i: (i, 0, tile + t))
    specs = [pl.BlockSpec(memory_space=pltpu.SMEM), block, block]
    if twiddle is None:
        kernel, given = split_kernel, [place, tokens, cotangent]
        planes = 2 * share
    else:
        kernel, given = split_twiddle_kernel, [place, tokens, cotangent, twiddle]
        specs.append(pl.BlockSpec((step, B), lambda t, i: (i, 0)))
        planes = 2 * share + 3
    return pl.pallas_call(
        functools.partial(kernel, rotated=rotated),
        grid=(tiles, rows // step),
        in_specs=specs,
        out_specs=part_specs(devices, rotated, (planes, step, B), lambda t, i: (t, i, 0)),
        out_shape=part_shapes(devices, rotated, (tiles * planes, rows, B)),
        scratch_shapes=[pltpu.VMEM(((step + 1) * LANES, B), jnp.float32)],
        compiler_params=pltpu.CompilerParams(vmem_limit_bytes=VMEM_BYTES),
        cost_estimate=pl.CostEstimate(flops=1, bytes_accessed=16 * rows * B * LANES * tiles, transcendentals=0),
    )(*given)


def merge_kernel(place_ref, *rest, parts, rotated):
    part_refs, out_ref, swap_ref = views(rest[:parts], rotated), rest[-2], rest[-1]
    share, rows, _ = part_refs[0].shape
    for slot, part_ref in enumerate(part_refs):
        start = (place_ref[0] + slot * share) % LANES if rotated else slot * share
        for channel in range(share):
            at = pl.multiple_of((start + channel) * rows, rows)
            swap_ref[pl.ds(at, rows), :] = part_ref[channel].astype(jnp.float32)
    for row in range(rows):
        out_ref[row] = swap_ref[pl.ds(row, LANES, stride=rows), :].T.astype(jnp.bfloat16)


def merge_channels(place, parts, held, tile, tiles, devices, rotated, width, after):
    rows = parts[0].shape[-2]
    step = min(16, rows)
    share = LANES // devices
    given = [place, *parts]
    specs = [pl.BlockSpec(memory_space=pltpu.SMEM)]
    specs += part_specs(devices, rotated, (share, step, B), lambda t, i: (t, i, 0))
    for array in after if held is None else [held, *after]:
        given.append(array)
        specs.append(pl.BlockSpec(memory_space=pl.ANY))
    return pl.pallas_call(
        functools.partial(merge_kernel, parts=len(parts), rotated=rotated),
        grid=(tiles, rows // step),
        in_specs=specs,
        out_specs=pl.BlockSpec((step, B, LANES), lambda t, i: (i, 0, tile + t)),
        out_shape=jax.ShapeDtypeStruct((rows, B, width), jnp.bfloat16),
        scratch_shapes=[pltpu.VMEM(((step + 1) * LANES, B), jnp.float32)],
        input_output_aliases={} if held is None else {len(parts) + 1: 0},
        compiler_params=pltpu.CompilerParams(vmem_limit_bytes=VMEM_BYTES),
        cost_estimate=pl.CostEstimate(flops=1, bytes_accessed=8 * rows * B * LANES * tiles, transcendentals=0),
    )(*given)


SECOND_AT = 2 * A
TWIDDLE_AT = SECOND_AT + B
CHANNEL_AT = TWIDDLE_AT + A


def mix_kernel(
    place_ref, gain_ref, bias_ref, skip_ref, *rest, parts, tile, tile_count, rotated
):
    tok_refs = views(rest[:parts], rotated)
    cot_refs = views(rest[parts : 2 * parts], rotated)
    first_ref, first_t_ref, second_ref, second_t_ref, twiddle_ref = rest[2 * parts : 2 * parts + 5]
    out_refs = views(rest[-3 - parts : -3], rotated)
    sums_ref, tok_all, cot_all = rest[-3:]
    t, step = pl.program_id(0), pl.program_id(1)

    @pl.when((t == 0) & (step == 0))
    def _():
        sums_ref[...] = jnp.zeros(sums_ref.shape, jnp.float32)

    devices = len(tok_refs)
    pair, rows, _ = tok_refs[0].shape
    share = LANES // devices
    lane_at = place_ref[0] + step * pair
    at = (tile + t) * LANES + lane_at

    def rows_from(shift):
        if not rotated:
            return slice(shift * rows, (shift + 1) * rows)
        source = (place_ref[0] // share - shift + devices) % devices
        return pl.ds(pl.multiple_of(source * rows, rows), rows)

    for refs, whole in ((tok_refs, tok_all), (cot_refs, cot_all)):
        for shift, ref in enumerate(refs):
            for c in range(pair):
                whole[rows_from(shift), c * B : (c + 1) * B] = ref[c].astype(jnp.float32)

    def spread(ref):
        lane = lax.broadcasted_iota(jnp.int32, (1, pair * B), 1)
        row = jnp.full((1, pair * B), ref[at], jnp.float32)
        for c in range(1, pair):
            row = jnp.where(lane >= c * B, ref[at + c], row)
        return row

    gain, bias, skip = spread(gain_ref), spread(bias_ref), spread(skip_ref)
    inputs = tok_all[...]
    tok = inputs.astype(jnp.bfloat16)
    upstream = cot_all[...]
    twiddle = jnp.concatenate([twiddle_ref[...]] * pair, axis=1)
    inner = dot(tok, second_t_ref[...], 1, 0)
    scaled = (inner * twiddle).astype(jnp.bfloat16)
    gate = jax.nn.sigmoid(gain * inputs + bias)
    grad_hidden = upstream * gate
    grad_outer = grad_hidden.astype(jnp.bfloat16)
    outer = dot(first_ref[...], scaled, 1, 0).astype(jnp.bfloat16).astype(jnp.float32)
    grad_scaled = dot(first_t_ref[...], grad_outer, 1, 0).astype(jnp.bfloat16).astype(jnp.float32)
    first_term = dot(grad_outer, scaled, 1, 1)
    for half in range(A // B):
        sums_ref[half * A : (half + 1) * A] += first_term[:, half * B : (half + 1) * B]
    hidden = outer + skip * inputs
    grad_pre = upstream * hidden * gate * (1.0 - gate)
    product = grad_scaled * inner
    sums_ref[TWIDDLE_AT:CHANNEL_AT] += sum(product[:, c * B : (c + 1) * B] for c in range(pair))
    grad_inner = (grad_scaled * twiddle).astype(jnp.bfloat16)
    second_term = dot(grad_inner, tok, 0, 0)
    sums_ref[SECOND_AT:TWIDDLE_AT] += sum(
        second_term[c * B : (c + 1) * B, c * B : (c + 1) * B] for c in range(pair)
    )
    lane = lax.broadcasted_iota(jnp.int32, (1, LANES), 1)
    for which, value in enumerate((grad_pre * inputs, grad_pre, grad_hidden * inputs)):
        total = jnp.sum(value, axis=0, keepdims=True)
        row = jnp.zeros((1, LANES), jnp.float32)
        for c in range(pair):
            channel = jnp.sum(total[:, c * B : (c + 1) * B], axis=1, keepdims=True)
            row = jnp.where(lane == lane_at + c, channel, row)
        sums_ref[pl.ds(CHANNEL_AT + which * tile_count + tile + t, 1), :] += row
    grad_in = dot(grad_inner, second_ref[...], 1, 0)
    tok_all[...] = grad_in + grad_hidden * skip + grad_pre * gain
    for shift, out_ref in enumerate(out_refs):
        for c in range(pair):
            out_ref[c] = tok_all[rows_from(shift), c * B : (c + 1) * B].astype(jnp.bfloat16)


def mix(parts, tile, tiles, planes, place, vectors, factors, sum_rows, devices, rotated, after):
    rows = parts[0].shape[-2]
    share = LANES // devices
    pair = factors[2].shape[0] // B
    steps = share // pair
    whole = lambda array: pl.BlockSpec(array.shape, lambda t, i: (0,) * array.ndim)
    tok_at = lambda t, i: (t * (planes // pair) + i, 0, 0)
    cot_at = lambda t, i: (t * (planes // pair) + steps + i, 0, 0)
    block = (pair, rows, B)
    tile_count = vectors[0].shape[0] // LANES
    *leaving, sums = pl.pallas_call(
        functools.partial(
            mix_kernel, parts=len(parts), tile=tile, tile_count=tile_count, rotated=rotated
        ),
        grid=(tiles, steps),
        in_specs=[pl.BlockSpec(memory_space=pltpu.SMEM)] * 4
        + part_specs(devices, rotated, block, tok_at)
        + part_specs(devices, rotated, block, cot_at)
        + [whole(f) for f in factors]
        + [pl.BlockSpec(memory_space=pl.ANY)] * len(after),
        out_specs=part_specs(devices, rotated, block, lambda t, i: (t * steps + i, 0, 0))
        + [pl.BlockSpec((sum_rows, LANES), lambda t, i: (0, 0))],
        out_shape=part_shapes(devices, rotated, (tiles * share, rows, B))
        + [jax.ShapeDtypeStruct((sum_rows, LANES), jnp.float32)],
        scratch_shapes=[pltpu.VMEM((A, pair * B), jnp.float32)] * 2,
        compiler_params=pltpu.CompilerParams(vmem_limit_bytes=VMEM_BYTES),
        cost_estimate=pl.CostEstimate(flops=tiles * share * A * B * 16000, bytes_accessed=1024, transcendentals=0),
    )(place, *vectors, *parts, *parts, *factors, *after)
    return leaving, sums


def add_kernel(*refs, count):
    total = refs[0][...]
    for ref in refs[1:count]:
        total += ref[...]
    refs[-1][...] = total


def add(terms, after):
    vmem = pl.BlockSpec(memory_space=pltpu.VMEM)
    return pl.pallas_call(
        functools.partial(add_kernel, count=len(terms)),
        in_specs=[vmem] * len(terms) + [pl.BlockSpec(memory_space=pl.ANY)] * len(after),
        out_specs=vmem,
        out_shape=jax.ShapeDtypeStruct(terms[0].shape, terms[0].dtype),
        cost_estimate=pl.CostEstimate(flops=1, bytes_accessed=1024, transcendentals=0),
    )(*terms, *after)


def hold(arrays, after):
    anywhere = pl.BlockSpec(memory_space=pl.ANY)
    return pl.pallas_call(
        lambda *refs: None,
        in_specs=[anywhere] * (len(arrays) + len(after)),
        out_specs=[anywhere] * len(arrays),
        out_shape=[jax.ShapeDtypeStruct(a.shape, a.dtype) for a in arrays],
        input_output_aliases={i: i for i in range(len(arrays))},
        cost_estimate=pl.CostEstimate(flops=1, bytes_accessed=1024, transcendentals=0),
    )(*arrays, *after)


def block_diagonal(square, count):
    zero = jnp.zeros_like(square)
    return jnp.concatenate(
        [
            jnp.concatenate([square if i == j else zero for j in range(count)], axis=1)
            for i in range(count)
        ],
        axis=0,
    )


def sum_over_mesh(sums, beside):
    beside = [None, *beside]

    def exchange_with(array, axis, bit):
        after = beside.pop(0) if beside else None
        if after is not None:
            (array,) = hold([array], after)
        size = lax.axis_size(axis)
        return array, lax.ppermute(array, axis, [(i, i ^ bit) for i in range(size)])

    dp = lax.axis_index("dp")
    bits = [1 << k for k in range(lax.axis_size("dp").bit_length() - 1)]
    for bit in reversed(bits):
        halves = sums.reshape(2, -1, LANES)
        high = (dp & bit) != 0
        _, other = exchange_with(jnp.where(high, halves[0], halves[1]), "dp", bit)
        sums = jnp.where(high, halves[1], halves[0]) + other
    bit = 1
    while bit < lax.axis_size("ctx"):
        sums, other = exchange_with(sums, "ctx", bit)
        sums = sums + other
        bit *= 2
    for bit in bits:
        sums, other = exchange_with(sums, "dp", bit)
        high = (dp & bit) != 0
        sums = jnp.concatenate([jnp.where(high, other, sums), jnp.where(high, sums, other)])
    return sums


def body(tokens, cotangent, first_factor, second_factor, twiddle, gate_gain, gate_bias, skip_gain):
    seq_count, tok_rows, width = tokens.shape
    ctx_size = lax.axis_size("ctx")
    dp_size = lax.axis_size("dp")
    share = LANES // ctx_size
    local_rows = tok_rows // B
    tiles = width // LANES
    pair = 2
    half = tiles // 2
    groups = [(0, 1, True), (1, half - 1, False), (half, tiles - half, True)]

    place = (lax.axis_index("ctx") * share).astype(jnp.int32).reshape(1)
    second = block_diagonal(second_factor, pair)
    second_t = block_diagonal(second_factor.T, pair)
    vectors = [gate_gain, gate_bias, skip_gain]
    used_rows = CHANNEL_AT + 3 * tiles
    sum_rows = -(-used_rows // (8 * dp_size)) * 8 * dp_size

    def exchange(parts, sign, rotated):
        if not rotated:
            return [lax.all_to_all(parts[0], "ctx", split_axis=0, concat_axis=0, tiled=True)]
        moved = [parts[0]]
        for shift in range(1, ctx_size):
            pairs = [(i, (i + sign * shift) % ctx_size) for i in range(ctx_size)]
            moved.append(lax.ppermute(parts[shift], "ctx", pairs))
        return moved

    terms = []
    leaving = []
    for seq in range(seq_count):
        tok_blocks = tokens[seq].reshape(local_rows, B, width)
        cot_blocks = cotangent[seq].reshape(local_rows, B, width)
        split = []
        for at, count, rotated in groups:
            own = twiddle if at == 0 else None
            split.append(
                split_channels(place, tok_blocks, cot_blocks, at, count, ctx_size, rotated, own)
            )
        arrived = [exchange(p, 1, group[2]) for p, group in zip(split, groups)]
        planes = jnp.stack([part[2 * share :] for part in arrived[0]]).astype(jnp.float32)
        planes = planes[:, 0] + planes[:, 1] + planes[:, 2]
        twice = jnp.concatenate([planes[::-1]] * 2, axis=0)
        turn = ctx_size - 1 - lax.axis_index("ctx")
        twiddle_all = lax.dynamic_slice_in_dim(twice, turn, ctx_size, 0).reshape(A, B)
        factors = [first_factor, first_factor.T, second, second_t, twiddle_all]
        returned = []
        released = []
        for which, (at, count, rotated) in enumerate(groups):
            parts, own_sums = mix(
                arrived[which], at, count, 2 * share, place, vectors, factors, sum_rows, ctx_size,
                rotated, released if which == 2 else [],
            )
            if which == 1:
                parts = released = hold(parts, arrived[2][1:])
            returned.append(exchange(parts, -1, rotated))
            terms.append(own_sums)
        leaving.append(returned)

    back, first = leaving[-1][2], leaving[-1][0]
    sums = sum_over_mesh(add(terms, []), [None, back[-2:], back[1:2], back[2:3], back[3:-2], first[3:5]])
    grads = []
    for returned in leaving:
        held = None
        for which in (1, 2, 0):
            at, count, rotated = groups[which]
            after = []
            held = merge_channels(
                place, returned[which], held, at, count, ctx_size, rotated, width, after
            )
        grads.append(held.reshape(tok_rows, width))
    grad_tokens = jnp.stack(grads)

    total_seqs = seq_count * dp_size
    first_norm = math.sqrt(total_seqs * B * width)
    second_norm = math.sqrt(total_seqs * A * width)
    twiddle_norm = math.sqrt(total_seqs * width)
    channel_norm = math.sqrt(total_seqs * A * B)
    first_sum = jnp.concatenate([sums[half * A : (half + 1) * A] for half in range(A // B)], axis=1)
    mine = TWIDDLE_AT + lax.axis_index("ctx") * local_rows
    twiddle_sum = lax.dynamic_slice_in_dim(sums, mine, local_rows, 0)
    channel_sum = sums[CHANNEL_AT:used_rows].reshape(3, width)
    return (
        grad_tokens,
        first_sum / first_norm,
        sums[SECOND_AT:TWIDDLE_AT] / second_norm,
        twiddle_sum / twiddle_norm,
        channel_sum[0] / channel_norm,
        channel_sum[1] / channel_norm,
        channel_sum[2] / channel_norm,
    )


def solution(mesh):
    return jax.shard_map(
        body,
        mesh=mesh,
        in_specs=(
            P("dp", "ctx", None),
            P("dp", "ctx", None),
            P(),
            P(),
            P("ctx", None),
            P(),
            P(),
            P(),
        ),
        out_specs=(P("dp", "ctx", None), P(), P(), P("ctx", None), P(), P(), P()),
        check_vma=False,
    )
```
